512 devices in a mesh: row: 128 (over y, x, z_lo, core), col: 4 (over z_hi).
Axes of the slice: x: 4, y: 4, z: 16 (z_hi: 4, z_lo: 4; z = z_hi * 4 + z_lo), core: 2. Of those that a mesh axis runs over, the one named last changes fastest.
Arguments:
- homolog_matrix: bfloat16 [256, 128, 4, 1, 256], P('row', None, 'col'), may hold values from -6 to 6
- pairs: bfloat16 [512, 128, 4, 1, 128], P('row', None, 'col'), may hold values from -6 to 6
- row_attention_weights: bfloat16 [256, 1024], replicated, may hold values from -2 to 2
- horizontal_projector: bfloat16 [256, 256], replicated, may hold values from -0.375 to 0.375
- pair_bias: bfloat16 [128, 8], replicated, may hold values from -0.5 to 0.5
- column_project: bfloat16 [256, 1024], replicated, may hold values from -2 to 2
- vertical_projector: bfloat16 [256, 256], replicated, may hold values from -0.375 to 0.375
- tensor_pair_maps: bfloat16 [256, 64], replicated, may hold values from -0.375 to 0.375
- outer_output: bfloat16 [1024, 128], replicated, may hold values from -1 to 1
- outgoing_project: bfloat16 [128, 640], replicated, may hold values from -0.5 to 0.5
- outgoing_output: bfloat16 [128, 128], replicated, may hold values from -0.5 to 0.5
- incoming_project: bfloat16 [128, 640], replicated, may hold values from -0.5 to 0.5
- incoming_output: bfloat16 [128, 128], replicated, may hold values from -0.5 to 0.5
Outputs:
- revised_homolog_matrix: bfloat16 [256, 128, 4, 1, 256], P('row', None, 'col')
- new_pairs: float32 [512, 128, 4, 1, 128], P('row', None, 'col')
The draws below stay inside these ranges and needn't reach their ends.
All inputs are finite; a program needn't handle non-finite values.
Results may differ from the reference program's by a relative error of at most 0.018.
Values may be sent and summed in bfloat16 or wider, within the bound.
A program may use at most 64 MiB of HBM per device.

```python
import math
import jax
import jax.numpy as jnp
from jax import lax

ALIGNED_CHANNELS = 256
C_Z = 128
HEAD_NUMBER = 8
HEAD_BREADTH = 32
OUTER_CHANNELS = 32
C_TRI = 128
TILE_SPAN = 1
HOMOLOG_TOTAL = 256
AMINO_TOTAL = 512
N_ROW = 128
N_COL = 4


def shaped(key, shared):
    universal_lookup, personal_lookup = jax.random.split(key)
    universal = jax.random.normal(universal_lookup, (ALIGNED_CHANNELS, HEAD_NUMBER, 1, HEAD_BREADTH), jnp.float32)
    distinct = jax.random.normal(personal_lookup, (ALIGNED_CHANNELS, HEAD_NUMBER, 4, HEAD_BREADTH), jnp.float32)
    combined = jnp.concatenate([shared * universal, shared * universal, 0.0 * universal, 0.0 * universal], axis=2)
    coefficient = (combined + distinct) * ALIGNED_CHANNELS ** (-0.5)
    return jnp.clip(coefficient, -2.0, 2.0).reshape(ALIGNED_CHANNELS, 4 * HEAD_NUMBER * HEAD_BREADTH).astype(jnp.bfloat16)


def draw_row_attention_weights(key, part):
    key = jax.random.fold_in(key, 11)
    return shaped(key, 0.0)


def draw_column_project(key, part):
    key = jax.random.fold_in(key, 12)
    return shaped(key, 0.0)


def block_scale(own_key, shape, cuts, least, top_value):
    def one(dim, parts):
        heights = jax.random.uniform(jax.random.fold_in(jax.random.fold_in(own_key, 6), dim), (parts,), jnp.float32, least / len(cuts), top_value / len(cuts))
        return jnp.repeat(jnp.exp(heights), shape[dim] // parts).reshape((-1,) + (1,) * (len(shape) - dim - 1))

    factor_of = one(*cuts[0])
    for cut in cuts[1:]:
        factor_of = factor_of * one(*cut)
    return factor_of


def normal_values(own_key, dims, deviation, limit, shards=(), dtype=jnp.bfloat16):
    values = jax.random.normal(own_key, dims, jnp.float32) * deviation
    if len(shards) > 0:
        values = block_scale(own_key, dims, shards, -0.22, 0.18) * values
    return jnp.clip(values, min=-limit, max=limit).astype(dtype)


def setup_inputs(seed: int = 0) -> dict:
    seeds = jax.random.split(jax.random.key(seed), 14)
    return {
        "homolog_matrix": normal_values(seeds[0], (HOMOLOG_TOTAL, N_ROW, N_COL, TILE_SPAN, ALIGNED_CHANNELS), 1.0, 6.0, ((0, 128), (2, 4))),
        "pairs": normal_values(seeds[1], (AMINO_TOTAL, N_ROW, N_COL, TILE_SPAN, C_Z), 1.0, 6.0, ((0, 128), (2, 4))),
        "row_attention_weights": draw_row_attention_weights(jax.random.fold_in(seeds[13], 71), 0),
        "horizontal_projector": normal_values(seeds[3], (HEAD_NUMBER * HEAD_BREADTH, ALIGNED_CHANNELS), (HEAD_NUMBER * HEAD_BREADTH) ** -0.5, 0.375),
        "pair_bias": normal_values(seeds[4], (C_Z, HEAD_NUMBER), C_Z ** -0.5, 0.5),
        "column_project": draw_column_project(jax.random.fold_in(seeds[13], 71), 0),
        "vertical_projector": normal_values(seeds[6], (HEAD_NUMBER * HEAD_BREADTH, ALIGNED_CHANNELS), (HEAD_NUMBER * HEAD_BREADTH) ** -0.5, 0.375),
        "tensor_pair_maps": normal_values(seeds[7], (ALIGNED_CHANNELS, 2 * OUTER_CHANNELS), ALIGNED_CHANNELS ** -0.5, 0.375),
        "outer_output": normal_values(seeds[8], (OUTER_CHANNELS * OUTER_CHANNELS, C_Z), OUTER_CHANNELS ** -0.5, 1.0),
        "outgoing_project": normal_values(seeds[9], (C_Z, 4 * C_TRI + C_Z), C_Z ** -0.5, 0.5),
        "outgoing_output": normal_values(seeds[10], (C_TRI, C_Z), C_TRI ** -0.5, 0.5),
        "incoming_project": normal_values(seeds[11], (C_Z, 4 * C_TRI + C_Z), C_Z ** -0.5, 0.5),
        "incoming_output": normal_values(seeds[12], (C_TRI, C_Z), C_TRI ** -0.5, 0.5),
    }


EPS = 1e-05

def normalized_state(values):
    values = values.astype(jnp.float32)
    center = values - lax.optimization_barrier(jnp.mean(values, axis=-1, keepdims=True))
    spread = lax.optimization_barrier(jnp.mean(center * center, axis=-1, keepdims=True))
    return center * lax.rsqrt(spread + EPS)

def gated_heads(rows, coefficient, output, bias_terms):
    length = rows.shape[0]
    projected = jnp.dot(normalized_state(rows).astype(jnp.bfloat16), coefficient, preferred_element_type=jnp.float32).astype(jnp.bfloat16)
    projected = projected.reshape(length, HEAD_NUMBER, 4, HEAD_BREADTH).astype(jnp.float32)
    scores = jnp.einsum('ihd,jhd->hij', projected[:, :, 0], projected[:, :, 1]) / math.sqrt(HEAD_BREADTH)
    scores = scores + bias_terms
    weights = jax.nn.softmax(scores, axis=-1).astype(jnp.bfloat16).astype(jnp.float32)
    mixture = jnp.einsum('hij,jhd->ihd', weights, projected[:, :, 2])
    gated = (jax.nn.sigmoid(projected[:, :, 3]) * mixture).astype(jnp.bfloat16).reshape(length, HEAD_NUMBER * HEAD_BREADTH)
    return rows.astype(jnp.float32) + jnp.dot(gated, output, preferred_element_type=jnp.float32)

def triangle(current, project, output, outgoing):
    block_rows = N_COL * TILE_SPAN
    normed_state = normalized_state(current).astype(jnp.bfloat16)

    def segment_list(rows):
        combined = jnp.dot(rows.reshape(-1, C_Z), project, preferred_element_type=jnp.float32)
        left_part = (jax.nn.sigmoid(combined[:, :C_TRI]) * combined[:, C_TRI:2 * C_TRI]).astype(jnp.bfloat16)
        right_part = (jax.nn.sigmoid(combined[:, 2 * C_TRI:3 * C_TRI]) * combined[:, 3 * C_TRI:4 * C_TRI]).astype(jnp.bfloat16)
        gating = jax.nn.sigmoid(combined[:, 4 * C_TRI:])
        return (left_part, right_part, gating)
    left_part, right_part, gating = lax.map(segment_list, normed_state.reshape(AMINO_TOTAL // block_rows, block_rows, AMINO_TOTAL, C_Z))
    left_part = left_part.reshape(AMINO_TOTAL, AMINO_TOTAL, C_TRI).transpose(2, 0, 1)
    right_part = right_part.reshape(AMINO_TOTAL, AMINO_TOTAL, C_TRI).transpose(2, 0, 1)
    gating = gating.reshape(AMINO_TOTAL, AMINO_TOTAL, C_Z)

    def per_channel(operands):
        left_plane, right_plane = operands
        if outgoing:
            product = jnp.dot(left_plane, right_plane.T, preferred_element_type=jnp.float32)
        else:
            product = jnp.dot(left_plane.T, right_plane, preferred_element_type=jnp.float32)
        return product.astype(jnp.bfloat16)
    mixture = lax.map(per_channel, (left_part, right_part)).transpose(1, 2, 0)
    normed_mix = normalized_state(mixture).astype(jnp.bfloat16)
    state_increment = jnp.dot(normed_mix.reshape(AMINO_TOTAL * AMINO_TOTAL, C_TRI), output, preferred_element_type=jnp.float32).reshape(AMINO_TOTAL, AMINO_TOTAL, C_Z)
    return current + gating * state_increment

def reference(homolog_matrix, pairs, row_attention_weights, horizontal_projector, pair_bias, column_project, vertical_projector, tensor_pair_maps, outer_output, outgoing_project, outgoing_output, incoming_project, incoming_output):
    homolog_lines = homolog_matrix.reshape(HOMOLOG_TOTAL, AMINO_TOTAL, ALIGNED_CHANNELS)
    pair_grid = pairs.reshape(AMINO_TOTAL, AMINO_TOTAL, C_Z)
    bias = jnp.dot(normalized_state(pair_grid).astype(jnp.bfloat16).reshape(AMINO_TOTAL * AMINO_TOTAL, C_Z), pair_bias, preferred_element_type=jnp.float32)
    bias = bias.astype(jnp.bfloat16).astype(jnp.float32).reshape(AMINO_TOTAL, AMINO_TOTAL, HEAD_NUMBER).transpose(2, 0, 1)

    def single_row(sequence):
        return gated_heads(sequence, row_attention_weights, horizontal_projector, bias).astype(jnp.bfloat16)
    state_after_rows = lax.map(single_row, homolog_lines)

    def one_column(column):
        renewed = gated_heads(column, column_project, vertical_projector, jnp.zeros((), jnp.float32))
        outer_ab = jnp.dot(normalized_state(renewed).astype(jnp.bfloat16), tensor_pair_maps, preferred_element_type=jnp.float32)
        return (renewed.astype(jnp.bfloat16), outer_ab.astype(jnp.bfloat16))
    refreshed_verticals, outer_ab = lax.map(one_column, state_after_rows.transpose(1, 0, 2))
    revised_homolog_matrix = refreshed_verticals.transpose(1, 0, 2).reshape(HOMOLOG_TOTAL, N_ROW, N_COL, TILE_SPAN, ALIGNED_CHANNELS)
    left_feat = outer_ab[:, :, :OUTER_CHANNELS].astype(jnp.float32)
    right_feat = outer_ab[:, :, OUTER_CHANNELS:].astype(jnp.float32)
    block_rows = N_COL * TILE_SPAN

    def outer_block(left_block):
        outer_prod = jnp.einsum('isp,jsq->ijpq', left_block, right_feat) / HOMOLOG_TOTAL
        outer_prod = outer_prod.astype(jnp.bfloat16).reshape(block_rows * AMINO_TOTAL, OUTER_CHANNELS * OUTER_CHANNELS)
        return jnp.dot(outer_prod, outer_output, preferred_element_type=jnp.float32).reshape(block_rows, AMINO_TOTAL, C_Z)
    outer_terms = lax.map(outer_block, left_feat.reshape(AMINO_TOTAL // block_rows, block_rows, HOMOLOG_TOTAL, OUTER_CHANNELS)).reshape(AMINO_TOTAL, AMINO_TOTAL, C_Z)
    after_outer = pair_grid.astype(jnp.float32) + outer_terms
    after_out = triangle(after_outer, outgoing_project, outgoing_output, True)
    final_grid = triangle(after_out, incoming_project, incoming_output, False)
    return (revised_homolog_matrix, final_grid.reshape(AMINO_TOTAL, N_ROW, N_COL, TILE_SPAN, C_Z))
```

```python
import functools
import math

import jax
import jax.numpy as jnp
from jax import lax
from jax.experimental import pallas as pl
from jax.experimental.pallas import tpu as pltpu
from jax.sharding import PartitionSpec as P

MESH = pl.DeviceIdType.MESH
BF = jnp.bfloat16
F32 = jnp.float32
EPS = 1e-05
HEADS = 8
NXY = 16
NZC = 8
NCOL = 4


def nn(a, b):
    return lax.dot_general(a, b, (((1,), (0,)), ((), ())), preferred_element_type=F32)


def nt(a, b):
    return lax.dot_general(a, b, (((1,), (1,)), ((), ())), preferred_element_type=F32)


def tn(a, b):
    return lax.dot_general(a, b, (((0,), (0,)), ((), ())), preferred_element_type=F32)


def norm(x, axis=-1):
    c = x - jnp.mean(x, axis=axis, keepdims=True)
    v = jnp.mean(c * c, axis=axis, keepdims=True)
    return c * lax.rsqrt(v + EPS)


def sig(x):
    return 1.0 / (1.0 + jnp.exp(-x))


def perm(sizes, order):
    n = math.prod(sizes)
    strides = [math.prod(sizes[k + 1 :]) for k in range(len(sizes))]
    out = lax.broadcasted_iota(jnp.int32, (n, n), 0)
    src = jnp.zeros((n, n), jnp.int32)
    rest = out
    for axis in reversed(order):
        src = src + (rest & (sizes[axis] - 1)) * strides[axis]
        rest = lax.shift_right_logical(rest, int(math.log2(sizes[axis])))
    inp = lax.broadcasted_iota(jnp.int32, (n, n), 1)
    return jnp.where(src == inp, 1.0, 0.0).astype(BF)


def where_am_i():
    row, col = lax.axis_index("row"), lax.axis_index("col")
    return row, col, row // NZC, row % NZC


class Swap:
    def __init__(self, r, name):
        self.send, self.recv = r[name + "_s"], r[name + "_r"]
        self.row, self.col, self.xy, self.zc = where_am_i()

    def put(self, src, dst, row, col):
        pltpu.make_async_remote_copy(
            src_ref=src,
            dst_ref=dst,
            send_sem=self.send,
            recv_sem=self.recv,
            device_id=(row, col),
            device_id_type=MESH,
        ).start()

    def keep(self, src, dst):
        pltpu.make_async_copy(src, dst, self.recv).start()

    def peers(self, kind):
        if kind == "xy":
            for d in range(1, NXY):
                g = lax.rem(self.xy + d, NXY)
                yield g, g * NZC + self.zc, self.col
        elif kind == "zc":
            for d in range(1, NZC):
                g = lax.rem(self.zc + d, NZC)
                yield g, self.xy * NZC + g, self.col
        else:
            for d in range(1, NCOL):
                g = lax.rem(self.col + d, NCOL)
                yield g, self.row, g

    def mine(self, kind):
        return {"xy": self.xy, "zc": self.zc, "col": self.col}[kind]

    def exchange(self, kind, src, dst):
        me = self.mine(kind)
        for g, row, col in self.peers(kind):
            self.put(src.at[g], dst.at[me], row, col)
        self.keep(src.at[me], dst.at[me])

    def gather(self, kind, buf):
        me = self.mine(kind)
        for g, row, col in self.peers(kind):
            self.put(buf.at[me], buf.at[me], row, col)

    def got(self, ref):
        pltpu.make_async_copy(ref, ref, self.recv).wait()

    def sent(self, ref):
        pltpu.make_async_copy(ref, ref, self.send).wait()


def barrier_signal():
    row, col, xy, zc = where_am_i()
    sem = pltpu.get_barrier_semaphore()

    def hail(r, c):
        pl.semaphore_signal(sem, inc=1, device_id=(r, c), device_id_type=MESH)

    for d in range(1, NXY):
        hail(lax.rem(xy + d, NXY) * NZC + zc, col)
    for d in range(1, NZC):
        hail(xy * NZC + lax.rem(zc + d, NZC), col)
    for d in range(1, NCOL):
        hail(row, lax.rem(col + d, NCOL))


def barrier_wait():
    pl.semaphore_wait(pltpu.get_barrier_semaphore(), NXY + NZC + NCOL - 3)


def attend(keys, own, weights, bias):
    length = keys.shape[0]
    q = nn(own, weights[:, 0:256]).astype(BF)
    k = nn(keys, weights[:, 256:512]).astype(BF)
    v = nn(keys, weights[:, 512:768]).astype(BF)
    gate = nn(own, weights[:, 768:1024]).astype(BF).astype(F32)
    v = jnp.concatenate([v, jnp.ones((length, 128), BF)], axis=1)
    head = lax.broadcasted_iota(jnp.int32, q.shape, 1) // 32
    total = jnp.zeros(q.shape, F32)
    for h in range(HEADS):
        scores = nt(jnp.where(head == h, q, jnp.zeros_like(q)), k) * (1.0 / math.sqrt(32.0))
        if bias is not None:
            scores = scores + bias(h)
        top = jnp.max(scores, axis=-1, keepdims=True)
        p = jnp.exp(scores - top).astype(BF)
        mixed = nn(p, v)
        inv = 1.0 / mixed[:, 256:384]
        mixed = mixed[:, 0:256] * jnp.concatenate([inv, inv], axis=1)
        total = total + jnp.where(head == h, mixed, 0.0)
    return (sig(gate) * total).astype(BF)


def by_kind(ref):
    w = ref[...]
    return jnp.concatenate(
        [w[:, 128 * h + 32 * k : 128 * h + 32 * k + 32] for k in range(4) for h in range(HEADS)], axis=1
    )


ROW_SCRATCH = dict(
    xg=((2, 4, 128, 256), BF),
    bsend=((4, 8, 128), F32),
    brecv=((4, 8, 128), F32),
    bz=((8, 16, 256), BF),
    bx=((16, 128, 256), BF),
    wrow=((256, 1024), BF),
)
ROW_SEMS = ["m0", "m1", "b0", "b1", "b2"]


def row_part(r):
    row, col, xy, zc = where_am_i()
    m = r["msa"]
    x = norm(m[...].astype(F32)).astype(BF)
    xg = r["xg"]
    for s in range(2):
        xg[s, col] = x[s]
    barrier_wait()
    swaps = [Swap(r, "m0"), Swap(r, "m1")]
    zn = norm(r["pairs"][...].astype(F32)).astype(BF).reshape(512, 128)
    bias_t = nt(r["pair_bias"][...].T, zn)
    for k in range(4):
        r["bsend"][k] = bias_t[:, 128 * k : 128 * k + 128]
    s0 = Swap(r, "b0")
    s0.exchange("col", r["bsend"], r["brecv"])
    for s in range(2):
        swaps[s].gather("col", xg.at[s])
    r["wrow"][...] = by_kind(r["row_w"])
    s0.got(r["brecv"])
    b = r["brecv"]
    lo = jnp.concatenate([b[0], b[1]], axis=1)
    hi = jnp.concatenate([b[2], b[3]], axis=1)
    r["bz"][zc] = jnp.concatenate([lo, hi], axis=0).astype(BF)
    s1 = Swap(r, "b1")
    s1.gather("zc", r["bz"])
    pz = perm((8, 16), (1, 0))
    s1.got(r["bz"].at[pl.ds(0, 7)])
    r["bx"][xy] = nn(pz, r["bz"][...].reshape(128, 256)).astype(BF)
    s2 = Swap(r, "b2")
    s2.gather("xy", r["bx"])
    if "prep" in r:
        r["prep"]()
    s2.got(r["bx"].at[pl.ds(0, 15)])
    cache = {}

    def bias(h):
        if h not in cache:
            pair = h // 2 * 2
            parts = []
            for jh in range(2):
                at = (jh * 8 + pair) * 8
                parts.append(r["bx"][:, at : at + 16, :].astype(F32))
            for k in range(2):
                cache[pair + k] = jnp.concatenate(
                    [p[:, 8 * k : 8 * k + 8].reshape(128, 256) for p in parts], axis=1
                )
        return cache[h]

    for s in range(2):
        swaps[s].got(xg.at[s, pl.ds(0, 3)])
        cache.clear()
        gated = attend(xg[s].reshape(512, 256), xg[s, col], r["wrow"], bias)
        r["m1"][s] = (m[s].astype(F32) + nn(gated, r["row_out"][...])).astype(BF)
    for s in range(2):
        swaps[s].sent(xg.at[s, pl.ds(0, 3)])
    s0.sent(r["bsend"].at[pl.ds(0, 3)])
    s1.sent(r["bz"].at[pl.ds(0, 7)])
    s2.sent(r["bx"].at[pl.ds(0, 15)])


COL_SCRATCH = dict(
    cs1=((16, 16, 256), BF),
    cr1=((16, 16, 256), BF),
    cs2=((8, 32, 256), BF),
    cr2=((8, 32, 256), BF),
    ds1=((8, 32, 256), BF),
    dr1=((8, 32, 256), BF),
    ds2=((16, 16, 256), BF),
    dr2=((16, 16, 256), BF),
    lg=((4, 32, 256), BF),
    rz=((8, 32, 256), BF),
    rx=((16, 256, 256), BF),
    wcol=((256, 1024), BF),
    bd=((32, 128, 512), BF),
)
COL_SEMS = ["c1", "c2", "d1", "d2", "lg", "rz", "rx", "rc"]


def col_prep(r):
    r["wcol"][...] = by_kind(r["col_w"])
    by_u = nn(perm((32, 32), (1, 0)), r["outer_out"][...]).astype(BF).reshape(32, 32, 128)
    r["bd"][...] = jnp.zeros((32, 128, 512), BF)
    for i in range(4):
        r["bd"][:, 32 * i : 32 * i + 32, 128 * i : 128 * i + 128] = by_u


def col_part(r):
    row, col, xy, zc = where_am_i()
    core = lax.rem(zc, 2)
    m1 = r["m1"][...].astype(F32).reshape(2, 16, 8, 256)
    r["cs1"][...] = jnp.concatenate([m1[0], m1[1]], axis=1).astype(BF)
    c1 = Swap(r, "c1")
    c1.exchange("xy", r["cs1"], r["cr1"])
    to_zc = perm((16, 2, 8), (2, 0, 1))
    c1.got(r["cr1"])
    r["cs2"][...] = nn(to_zc, r["cr1"][...].reshape(256, 256)).astype(BF).reshape(8, 32, 256)
    c2 = Swap(r, "c2")
    c2.exchange("zc", r["cs2"], r["cr2"])
    c2.got(r["cr2"])
    lines = r["cr2"][...].reshape(256, 256).astype(F32)
    x = norm(lines).astype(BF)
    gated = attend(x, x, r["wcol"], None)
    m2 = lines + nn(gated, r["col_out"][...])
    x = norm(m2).astype(BF)
    ab = nt(r["maps"][...].T, x).astype(BF)
    r["lg"][col] = ab[0:32]
    r["rz"][zc] = ab[32:64]
    rz = Swap(r, "rz")
    rz.gather("zc", r["rz"])
    lg = Swap(r, "lg")
    lg.gather("col", r["lg"])
    r["ds1"][...] = m2.astype(BF).reshape(8, 32, 256)
    d1 = Swap(r, "d1")
    d1.exchange("zc", r["ds1"], r["dr1"])
    rz.got(r["rz"].at[pl.ds(0, 7)])
    right = nn(perm((8, 32), (1, 0)), r["rz"][...].reshape(256, 256)).astype(BF)
    rx = r["rx"]
    for k in range(2):

        @pl.when(core == k)
        def _():
            rx[xy, 128 * k : 128 * k + 128] = right[128 * k : 128 * k + 128]

    half = pl.ds(pl.multiple_of(core * 128, 128), 128)
    other = pl.ds(pl.multiple_of(128 - core * 128, 128), 128)
    rxs = Swap(r, "rx")
    for g, prow, pcol in rxs.peers("xy"):
        rxs.put(rx.at[xy, half], rx.at[xy, half], prow, pcol)
    d1.got(r["dr1"])
    r["ds2"][...] = nn(perm((8, 16, 2), (1, 2, 0)), r["dr1"][...].reshape(256, 256)).astype(BF).reshape(16, 16, 256)
    d2 = Swap(r, "d2")
    d2.exchange("xy", r["ds2"], r["dr2"])
    lg.got(r["lg"].at[pl.ds(0, 3)])
    left = r["lg"][...].reshape(128, 256).T
    rxs.got(rx.at[pl.ds(0, 15), pl.ds(0, 128)])
    rc = Swap(r, "rc")
    rc.put(rx.at[:, half], rx.at[:, half], row + 1 - 2 * core, col)
    d2.got(r["dr2"])
    dr2 = r["dr2"][...].astype(F32)
    for s in range(2):
        r["msa_out"][s] = dr2[:, 8 * s : 8 * s + 8].reshape(128, 256).astype(BF)

    def add(base, acc):
        for up in range(8):
            at = pl.multiple_of(base * 8 + up * 16, 16)
            block = rx[:, pl.ds(at, 16), :].astype(F32)
            for k in range(2):
                a = nn(left, r["bd"][base + 2 * up + k]).astype(BF)
                acc = acc + nn(block[:, 8 * k : 8 * k + 8].reshape(128, 256).astype(BF), a)
        return acc

    acc = add(core * 16, jnp.zeros((128, 512), F32))
    rc.got(rx.at[:, other])
    acc = add(16 - core * 16, acc)
    for i in range(4):
        r["z1"][i] = r["pairs"][i].astype(F32) + acc[:, 128 * i : 128 * i + 128] * (1.0 / 256.0)
    c1.sent(r["cs1"].at[pl.ds(0, 15)])
    c2.sent(r["cs2"].at[pl.ds(0, 7)])
    d1.sent(r["ds1"].at[pl.ds(0, 7)])
    d2.sent(r["ds2"].at[pl.ds(0, 15)])
    lg.sent(r["lg"].at[pl.ds(0, 3)])
    rz.sent(r["rz"].at[pl.ds(0, 7)])
    rxs.sent(rx.at[pl.ds(0, 15), pl.ds(0, 128)])
    rc.sent(rx.at[:, half])


def tri_scratch(t):
    return {
        t + "s1": ((16, 16, 512), BF),
        t + "r1": ((16, 16, 512), BF),
        t + "s2": ((8, 32, 512), BF),
        t + "r2": ((8, 32, 512), BF),
        t + "ps": ((4, 512, 128), BF),
        t + "pr": ((4, 512, 128), BF),
        t + "s3": ((16, 32, 128), BF),
        t + "r3": ((16, 32, 128), BF),
        t + "s4": ((8, 64, 128), BF),
        t + "r4": ((8, 64, 128), BF),
        t + "gate": ((512, 128), F32),
        t + "wg": ((256, 128), BF),
        t + "wv": ((256, 128), BF),
        t + "wo": ((128, 128), BF),
    }


def tri_sems(t):
    return [t + k for k in ("1", "2", "p", "3", "4")]


def tri_prep(r, t):
    w = r[t + "_proj"][:, 0:512].astype(F32).T.reshape(4, 16, 8, 128)
    r[t + "wg"][...] = jnp.concatenate([w[0], w[2]], axis=1).astype(BF).reshape(256, 128)
    r[t + "wv"][...] = jnp.concatenate([w[1], w[3]], axis=1).astype(BF).reshape(256, 128)
    r[t + "wo"][...] = nn(perm((16, 8), (1, 0)), r[t + "_out"][...]).astype(BF)


def tri_part(r, t, src, dst, outgoing):
    row, col, xy, zc = where_am_i()
    x = norm(r[src][...]).astype(BF).reshape(512, 128)
    both = sig(nt(r[t + "wg"][...], x)) * nt(r[t + "wv"][...], x)
    r[t + "s1"][...] = both.astype(BF).reshape(16, 16, 512)
    e1 = Swap(r, t + "1")
    e1.exchange("xy", r[t + "s1"], r[t + "r1"])
    r[t + "gate"][...] = sig(nn(x, r[t + "_proj"][:, 512:640]))
    to_zc = perm((16, 2, 8), (2, 1, 0))
    e1.got(r[t + "r1"])
    r[t + "s2"][...] = nn(to_zc, r[t + "r1"][...].reshape(256, 512)).astype(BF).reshape(8, 32, 512)
    e2 = Swap(r, t + "2")
    e2.exchange("zc", r[t + "s2"], r[t + "r2"])
    natural = perm((8, 16), (1, 0))
    e2.got(r[t + "r2"])
    left = r[t + "r2"][:, 0:16, :].reshape(128, 512)
    right = r[t + "r2"][:, 16:32, :].reshape(128, 512)
    ep = Swap(r, t + "p")
    if outgoing:
        left = nn(natural, left).astype(BF)
        right = nn(natural, right).astype(BF)
        left = jnp.concatenate([left[:, 128 * q : 128 * q + 128] for q in range(4)], axis=0)
        for q in range(4):
            r[t + "ps"][q] = nt(left, right[:, 128 * q : 128 * q + 128]).astype(BF)
        ep.exchange("col", r[t + "ps"], r[t + "pr"])
        ep.got(r[t + "pr"])
        pr = r[t + "pr"]
        mix = (pr[0].astype(F32) + pr[1].astype(F32)) + (pr[2].astype(F32) + pr[3].astype(F32))
    else:
        gathered = r[t + "pg"]
        gathered[col] = jnp.concatenate([left[:, 128 * q : 128 * q + 128].T for q in range(4)], axis=1)
        ep.gather("col", gathered)
        right = jnp.concatenate([right[:, 128 * q : 128 * q + 128] for q in range(4)], axis=0)
        ep.got(gathered.at[pl.ds(0, 3)])
        mix = nn(gathered[...].reshape(512, 512), right)
    mix = mix.reshape(4, 16, 8, 128)
    r[t + "s3"][...] = jnp.concatenate([mix[q] for q in range(4)], axis=1).astype(BF)
    e3 = Swap(r, t + "3")
    e3.exchange("xy", r[t + "s3"], r[t + "r3"])
    back = perm((16, 4, 8), (2, 1, 0))
    e3.got(r[t + "r3"])
    r[t + "s4"][...] = nn(back, r[t + "r3"][...].reshape(512, 128)).astype(BF).reshape(8, 64, 128)
    e4 = Swap(r, t + "4")
    e4.exchange("zc", r[t + "s4"], r[t + "r4"])
    e4.got(r[t + "r4"])
    for q in range(4):
        mq = r[t + "r4"][:, 16 * q : 16 * q + 16, :].reshape(128, 128).astype(F32)
        step = tn(norm(mq, 0).astype(BF), r[t + "wo"][...])
        r[dst][q] = r[src][q] + r[t + "gate"][128 * q : 128 * q + 128] * step
    e1.sent(r[t + "s1"].at[pl.ds(0, 15)])
    e2.sent(r[t + "s2"].at[pl.ds(0, 7)])
    if outgoing:
        ep.sent(r[t + "ps"].at[pl.ds(0, 3)])
    else:
        ep.sent(r[t + "pg"].at[pl.ds(0, 3)])
    e3.sent(r[t + "s3"].at[pl.ds(0, 15)])
    e4.sent(r[t + "s4"].at[pl.ds(0, 7)])


SHAPES = dict(
    m1=((2, 128, 256), BF),
    z1=((4, 128, 128), F32),
    z2=((4, 128, 128), F32),
    z3=((4, 128, 128), F32),
    msa_out=((2, 128, 256), BF),
)


def out_scratch():
    return tri_scratch("o")


def in_scratch():
    s = tri_scratch("i")
    del s["ips"], s["ipr"]
    s["ipg"] = ((4, 128, 512), BF)
    return s


PARTS = dict(
    row=dict(ins=["msa", "pairs", "row_w", "row_out", "pair_bias"], outs=["m1"], scratch=ROW_SCRATCH, sems=ROW_SEMS),
    col=dict(
        ins=["m1", "pairs", "col_w", "col_out", "maps", "outer_out"],
        outs=["msa_out", "z1"],
        scratch=COL_SCRATCH,
        sems=COL_SEMS,
    ),
    out=dict(ins=["z1", "o_proj", "o_out"], outs=["z2"], scratch=out_scratch(), sems=tri_sems("o")),
    inc=dict(ins=["z2", "i_proj", "i_out"], outs=["z3"], scratch=in_scratch(), sems=tri_sems("i")),
)


def run_parts(parts, arrays, results, number):
    ins, made, scratch, sems = [], [], {}, []
    for p in parts:
        spec = PARTS[p]
        ins += [n for n in spec["ins"] if n not in ins and n not in made]
        made += spec["outs"]
        scratch.update(spec["scratch"])
        sems += spec["sems"]
    outs = [n for n in made if n in results]
    inner = {n: SHAPES[n] for n in made if n not in results}
    scratch = {**scratch, **inner}
    sem_names = [s + e for s in sems for e in ("_s", "_r")]

    def body(*refs):
        r = dict(zip(ins + outs + list(scratch) + sem_names, refs))
        barrier_signal()

        def prep():
            if "col" in parts:
                col_prep(r)
            if "out" in parts:
                tri_prep(r, "o")
            if "inc" in parts:
                tri_prep(r, "i")

        if parts[0] == "row":
            r["prep"] = prep
        else:
            prep()
            barrier_wait()
        for p in parts:
            if p == "row":
                row_part(r)
            elif p == "col":
                col_part(r)
            elif p == "out":
                tri_part(r, "o", "z1", "z2", True)
            else:
                tri_part(r, "i", "z2", "z3", False)

    vm = pl.BlockSpec(memory_space=pltpu.VMEM)
    got = pl.pallas_call(
        body,
        out_shape=[jax.ShapeDtypeStruct(*SHAPES[n]) for n in outs],
        in_specs=[vm] * len(ins),
        out_specs=[vm] * len(outs),
        scratch_shapes=[pltpu.VMEM(*scratch[n]) for n in scratch] + [pltpu.SemaphoreType.DMA] * len(sem_names),
        compiler_params=pltpu.CompilerParams(
            collective_id=number, has_side_effects=True, vmem_limit_bytes=56 * 1024 * 1024
        ),
        name="_".join(parts),
    )(*[arrays[n] for n in ins])
    arrays.update(zip(outs, got))


GROUPS = [["row", "col", "out", "inc"]]


def shards(*args, groups=None, results=("msa_out", "z3")):
    groups = groups or GROUPS
    names = ["msa", "pairs", "row_w", "row_out", "pair_bias", "col_w", "col_out", "maps", "outer_out"]
    names += ["o_proj", "o_out", "i_proj", "i_out"]
    arrays = dict(zip(names, args))
    msa_shape, pair_shape = arrays["msa"].shape, arrays["pairs"].shape
    arrays["msa"] = arrays["msa"].reshape(2, 128, 256)
    arrays["pairs"] = arrays["pairs"].reshape(4, 128, 128)
    for number, group in enumerate(groups):
        later = [n for g in groups[number + 1 :] for p in g for n in PARTS[p]["ins"]]
        run_parts(group, arrays, set(results) | set(later), number)
    outs = dict(
        msa_out=lambda a: a.reshape(msa_shape),
        z3=lambda a: a.reshape(pair_shape),
    )
    return tuple(outs.get(n, lambda a: a)(arrays[n]) for n in results)


def solution(mesh):
    return jax.shard_map(
        shards,
        mesh=mesh,
        in_specs=(P("row", None, "col", None, None),) * 2 + (P(),) * 11,
        out_specs=(P("row", None, "col", None, None),) * 2,
        check_vma=False,
    )
```

```python
import functools
import math

import jax
import jax.numpy as jnp
from jax import lax
from jax.experimental import pallas as pl
from jax.experimental.pallas import tpu as pltpu
from jax.sharding import PartitionSpec as P

MESH = pl.DeviceIdType.MESH
BF = jnp.bfloat16
F32 = jnp.float32
EPS = 1e-05
HEADS = 8
NXY = 16
NZC = 8
NCOL = 4


def nn(a, b):
    return lax.dot_general(a, b, (((1,), (0,)), ((), ())), preferred_element_type=F32)


def nt(a, b):
    return lax.dot_general(a, b, (((1,), (1,)), ((), ())), preferred_element_type=F32)


def tn(a, b):
    return lax.dot_general(a, b, (((0,), (0,)), ((), ())), preferred_element_type=F32)


def norm(x, axis=-1):
    c = x - jnp.mean(x, axis=axis, keepdims=True)
    v = jnp.mean(c * c, axis=axis, keepdims=True)
    return c * lax.rsqrt(v + EPS)


def sig(x):
    return 1.0 / (1.0 + jnp.exp(-x))


def perm(sizes, order):
    n = math.prod(sizes)
    strides = [math.prod(sizes[k + 1 :]) for k in range(len(sizes))]
    out = lax.broadcasted_iota(jnp.int32, (n, n), 0)
    src = jnp.zeros((n, n), jnp.int32)
    rest = out
    for axis in reversed(order):
        src = src + (rest & (sizes[axis] - 1)) * strides[axis]
        rest = lax.shift_right_logical(rest, int(math.log2(sizes[axis])))
    inp = lax.broadcasted_iota(jnp.int32, (n, n), 1)
    return jnp.where(src == inp, 1.0, 0.0).astype(BF)


def where_am_i():
    row, col = lax.axis_index("row"), lax.axis_index("col")
    return row, col, row // NZC, row % NZC


def in_quad():
    row, col, xy, zc = where_am_i()
    return 2 * col + zc // 4, zc % 4


def place(xy, m, e):
    return xy * NZC + m % 2 * 4 + e, m // 2


class Swap:
    def __init__(self, r, name):
        self.send, self.recv = r[name + "_s"], r[name + "_r"]
        self.row, self.col, self.xy, self.zc = where_am_i()
        self.m, self.e = in_quad()

    def put(self, src, dst, row, col):
        pltpu.make_async_remote_copy(
            src_ref=src,
            dst_ref=dst,
            send_sem=self.send,
            recv_sem=self.recv,
            device_id=(row, col),
            device_id_type=MESH,
        ).start()

    def keep(self, src, dst):
        pltpu.make_async_copy(src, dst, self.recv).start()

    def peers(self, kind):
        if kind == "xy":
            for d in range(1, NXY):
                g = lax.rem(self.xy + d, NXY)
                yield g, g * NZC + self.zc, self.col
        elif kind == "zc":
            for d in range(1, NZC):
                g = lax.rem(self.zc + d, NZC)
                yield g, self.xy * NZC + g, self.col
        elif kind == "quad":
            for d in range(1, 4):
                g = lax.rem(self.e + d, 4)
                yield g, *place(self.xy, self.m, g)
        else:
            for d in range(1, NCOL):
                g = lax.rem(self.col + d, NCOL)
                yield g, self.row, g

    def mine(self, kind):
        return {"xy": self.xy, "zc": self.zc, "col": self.col, "quad": self.e}[kind]

    def exchange(self, kind, src, dst):
        me = self.mine(kind)
        for g, row, col in self.peers(kind):
            self.put(src.at[g], dst.at[me], row, col)
        self.keep(src.at[me], dst.at[me])

    def gather(self, kind, buf):
        me = self.mine(kind)
        for g, row, col in self.peers(kind):
            self.put(buf.at[me], buf.at[me], row, col)

    def ring(self, src_of, dst):
        here = self.m * 4 + self.e
        for d in range(1, 32):
            t = lax.rem(here + d, 32)
            m, e = t // 4, t % 4
            self.put(src_of(m, e), dst.at[self.zc, self.col], *place(self.xy, m, e))
        self.keep(src_of(self.m, self.e), dst.at[self.zc, self.col])

    def either(self, src, dst, away, row, col):
        @pl.when(away)
        def _():
            self.put(src, dst, row, col)

        @pl.when(jnp.logical_not(away))
        def _():
            self.keep(src, dst)

    def out(self, src, dst):
        for d in range(1, 8):
            m = lax.rem(self.m + d, 8)
            self.put(src.at[m], dst.at[self.zc], *place(self.xy, m, self.col))
        row, col = place(self.xy, self.m, self.col)
        self.either(src.at[self.m], dst.at[self.zc], self.e != self.col, row, col)

    def back(self, src, dst):
        for d in range(1, 8):
            g = lax.rem(self.zc + d, 8)
            self.put(src.at[g], dst.at[self.m], self.xy * NZC + g, self.e)
        self.either(src.at[self.zc], dst.at[self.m], self.e != self.col, self.row, self.e)

    def sent8(self, src):
        self.sent(src.at[pl.ds(0, 7)])

        @pl.when(self.e != self.col)
        def _():
            self.sent(src.at[0])

    def got(self, ref):
        pltpu.make_async_copy(ref, ref, self.recv).wait()

    def sent(self, ref):
        pltpu.make_async_copy(ref, ref, self.send).wait()


def barrier_signal():
    row, col, xy, zc = where_am_i()
    m, e = in_quad()
    sem = pltpu.get_barrier_semaphore()

    def hail(r, c):
        pl.semaphore_signal(sem, inc=1, device_id=(r, c), device_id_type=MESH)

    for d in range(1, NXY):
        hail(lax.rem(xy + d, NXY) * NZC + zc, col)
    for d in range(1, 32):
        t = lax.rem(m * 4 + e + d, 32)
        hail(*place(xy, t // 4, t % 4))


def barrier_wait():
    pl.semaphore_wait(pltpu.get_barrier_semaphore(), NXY + 32 - 2)


def attend(keys, own, weights, bias):
    length = keys.shape[0]
    q = nn(own, weights[:, 0:256]).astype(BF)
    k = nn(keys, weights[:, 256:512]).astype(BF)
    v = nn(keys, weights[:, 512:768]).astype(BF)
    gate = nn(own, weights[:, 768:1024]).astype(BF).astype(F32)
    v = jnp.concatenate([v, jnp.ones((length, 128), BF)], axis=1)
    head = lax.broadcasted_iota(jnp.int32, q.shape, 1) // 32
    total = jnp.zeros(q.shape, F32)
    for h in range(HEADS):
        scores = nt(jnp.where(head == h, q, jnp.zeros_like(q)), k) * (1.0 / math.sqrt(32.0))
        if bias is not None:
            scores = scores + bias(h)
        top = jnp.max(scores, axis=-1, keepdims=True)
        p = jnp.exp(scores - top).astype(BF)
        mixed = nn(p, v)
        inv = 1.0 / mixed[:, 256:384]
        mixed = mixed[:, 0:256] * jnp.concatenate([inv, inv], axis=1)
        total = total + jnp.where(head == h, mixed, 0.0)
    return (sig(gate) * total).astype(BF)


def by_kind(ref):
    w = ref[...]
    return jnp.concatenate(
        [w[:, 128 * h + 32 * k : 128 * h + 32 * k + 32] for k in range(4) for h in range(HEADS)], axis=1
    )


ROW_SCRATCH = dict(
    xr=((2, 128, 256), BF),
    xg=((2, 4, 128, 256), BF),
    bsend=((4, 8, 128), F32),
    brecv=((8, 4, 8, 128), F32),
    bx=((16, 128, 256), BF),
    wrow=((256, 1024), BF),
)
ROW_SEMS = ["m0", "m1", "g0", "g1", "b0", "b2"]


def row_part(r):
    row, col, xy, zc = where_am_i()
    m, e = in_quad()
    msa, xr, xg = r["msa"], r["xr"], r["xg"]
    zn = norm(r["pairs"][...].astype(F32)).astype(BF).reshape(512, 128)
    bias_t = nt(r["pair_bias"][...].T, zn)
    for k in range(4):
        r["bsend"][k] = bias_t[:, 128 * k : 128 * k + 128]
    barrier_wait()
    s0 = Swap(r, "b0")
    s0.ring(lambda m, e: r["bsend"].at[e], r["brecv"])
    direct = [Swap(r, "m0"), Swap(r, "m1")]
    away = jnp.logical_or(zc != m, col != e)
    for s in range(2):
        direct[s].either(msa.at[s], xr.at[s], away, *place(xy, zc, col))
    r["wrow"][...] = by_kind(r["row_w"])
    pz = perm((8, 16), (1, 0))
    shared = [Swap(r, "g0"), Swap(r, "g1")]

    def share(s):
        direct[s].got(xr.at[s])
        xg[s, e] = norm(xr[s].astype(F32)).astype(BF)
        shared[s].gather("quad", xg.at[s])

    s0.got(r["brecv"])
    b = r["brecv"]
    lo = jnp.concatenate([b[:, 0], b[:, 1]], axis=2)
    hi = jnp.concatenate([b[:, 2], b[:, 3]], axis=2)
    rows = jnp.concatenate([lo, hi], axis=1).astype(BF).reshape(128, 256)
    r["bx"][xy] = nn(pz, rows).astype(BF)
    s2 = Swap(r, "b2")
    s2.gather("xy", r["bx"])
    share(0)
    share(1)
    if "prep" in r:
        r["prep"]()
    s2.got(r["bx"].at[pl.ds(0, 15)])
    cache = {}

    def bias(h):
        if h not in cache:
            pair = h // 2 * 2
            parts = []
            for jh in range(2):
                at = (jh * 8 + pair) * 8
                parts.append(r["bx"][:, at : at + 16, :].astype(F32))
            for k in range(2):
                cache[pair + k] = jnp.concatenate(
                    [p[:, 8 * k : 8 * k + 8].reshape(128, 256) for p in parts], axis=1
                )
        return cache[h]

    for s in range(2):
        shared[s].got(xg.at[s, pl.ds(0, 3)])
        cache.clear()
        gated = attend(xg[s].reshape(512, 256), xg[s, e], r["wrow"], bias)
        r["m1"][s] = (xr[s].astype(F32) + nn(gated, r["row_out"][...])).astype(BF)
    for s in range(2):
        shared[s].sent(xg.at[s, pl.ds(0, 3)])

        @pl.when(away)
        def _():
            direct[s].sent(msa.at[s])

    s0.sent(r["brecv"].at[pl.ds(0, 7)])
    s0.sent(r["brecv"].at[0, pl.ds(0, 3)])
    s2.sent(r["bx"].at[pl.ds(0, 15)])


COL_SCRATCH = dict(
    cs1=((8, 32, 256), BF),
    cr1=((8, 32, 256), BF),
    cs2=((16, 16, 256), BF),
    cr2=((16, 16, 256), BF),
    ds1=((16, 16, 256), BF),
    dr1=((16, 16, 256), BF),
    ds2=((8, 32, 256), BF),
    dr2=((8, 32, 256), BF),
    lg=((4, 32, 256), BF),
    rz=((8, 32, 256), BF),
    rx=((16, 256, 256), BF),
    wcol=((256, 1024), BF),
    bd=((32, 128, 512), BF),
)
COL_SEMS = ["c1", "c2", "d1", "d2", "lg", "rz", "rx", "rc"]


def col_prep(r):
    r["wcol"][...] = by_kind(r["col_w"])
    by_u = nn(perm((32, 32), (1, 0)), r["outer_out"][...]).astype(BF).reshape(32, 32, 128)
    r["bd"][...] = jnp.zeros((32, 128, 512), BF)
    for i in range(4):
        r["bd"][:, 32 * i : 32 * i + 32, 128 * i : 128 * i + 128] = by_u


def col_part(r):
    row, col, xy, zc = where_am_i()
    core = lax.rem(zc, 2)
    r["cs1"][...] = nn(perm((2, 16, 8), (2, 0, 1)), r["m1"][...].reshape(256, 256)).astype(BF).reshape(8, 32, 256)
    c1 = Swap(r, "c1")
    c1.back(r["cs1"], r["cr1"])
    to_xy = perm((8, 2, 16), (2, 0, 1))
    c1.got(r["cr1"])
    r["cs2"][...] = nn(to_xy, r["cr1"][...].reshape(256, 256)).astype(BF).reshape(16, 16, 256)
    c2 = Swap(r, "c2")
    c2.exchange("xy", r["cs2"], r["cr2"])
    c2.got(r["cr2"])
    lines = r["cr2"][...].reshape(256, 256).astype(F32)
    x = norm(lines).astype(BF)
    gated = attend(x, x, r["wcol"], None)
    m2 = lines + nn(gated, r["col_out"][...])
    x = norm(m2).astype(BF)
    ab = nt(r["maps"][...].T, x).astype(BF)
    r["lg"][col] = ab[0:32]
    r["rz"][zc] = ab[32:64]
    rz = Swap(r, "rz")
    rz.gather("zc", r["rz"])
    lg = Swap(r, "lg")
    lg.gather("col", r["lg"])
    r["ds1"][...] = m2.astype(BF).reshape(16, 16, 256)
    d1 = Swap(r, "d1")
    d1.exchange("xy", r["ds1"], r["dr1"])
    rz.got(r["rz"].at[pl.ds(0, 7)])
    right = nn(perm((8, 32), (1, 0)), r["rz"][...].reshape(256, 256)).astype(BF)
    rx = r["rx"]
    for k in range(2):

        @pl.when(core == k)
        def _():
            rx[xy, 128 * k : 128 * k + 128] = right[128 * k : 128 * k + 128]

    half = pl.ds(pl.multiple_of(core * 128, 128), 128)
    other = pl.ds(pl.multiple_of(128 - core * 128, 128), 128)
    rxs = Swap(r, "rx")
    for g, prow, pcol in rxs.peers("xy"):
        rxs.put(rx.at[xy, half], rx.at[xy, half], prow, pcol)
    d1.got(r["dr1"])
    r["ds2"][...] = nn(perm((16, 8, 2), (1, 2, 0)), r["dr1"][...].reshape(256, 256)).astype(BF).reshape(8, 32, 256)
    d2 = Swap(r, "d2")
    d2.exchange("zc", r["ds2"], r["dr2"])
    lg.got(r["lg"].at[pl.ds(0, 3)])
    left = r["lg"][...].reshape(128, 256).T
    rxs.got(rx.at[pl.ds(0, 15), pl.ds(0, 128)])
    rc = Swap(r, "rc")
    rc.put(rx.at[:, half], rx.at[:, half], row + 1 - 2 * core, col)
    d2.got(r["dr2"])
    r["msa_out"][...] = (
        nn(perm((8, 2, 16), (1, 2, 0)), r["dr2"][...].reshape(256, 256)).astype(BF).reshape(2, 128, 256)
    )

    def add(base, acc):
        for up in range(8):
            at = pl.multiple_of(base * 8 + up * 16, 16)
            block = rx[:, pl.ds(at, 16), :].astype(F32)
            for k in range(2):
                a = nn(left, r["bd"][base + 2 * up + k]).astype(BF)
                acc = acc + nn(block[:, 8 * k : 8 * k + 8].reshape(128, 256).astype(BF), a)
        return acc

    acc = add(core * 16, jnp.zeros((128, 512), F32))
    rc.got(rx.at[:, other])
    acc = add(16 - core * 16, acc)
    for i in range(4):
        r["z1"][i] = r["pairs"][i].astype(F32) + acc[:, 128 * i : 128 * i + 128] * (1.0 / 256.0)
    c1.sent8(r["cs1"])
    c2.sent(r["cs2"].at[pl.ds(0, 15)])
    d1.sent(r["ds1"].at[pl.ds(0, 15)])
    d2.sent(r["ds2"].at[pl.ds(0, 7)])
    lg.sent(r["lg"].at[pl.ds(0, 3)])
    rz.sent(r["rz"].at[pl.ds(0, 7)])
    rxs.sent(rx.at[pl.ds(0, 15), pl.ds(0, 128)])
    rc.sent(rx.at[:, half])


def tri_scratch(t, outgoing):
    return {
        t + "s1": ((16, 16, 512), BF),
        t + "r1": ((16, 16, 512), BF),
        t + "s2": ((8, 32, 512), BF),
        t + "r2": ((8, 32, 512) if outgoing else (8, 4, 32, 128), BF),
        t + "ps": ((4, 512, 128), BF),
        t + "pr": ((4, 512, 128), BF),
        t + "s3": ((8, 64, 128), BF),
        t + "r3": ((8, 64, 128), BF),
        t + "s4": ((16, 32, 128), BF),
        t + "r4": ((16, 32, 128), BF),
        t + "gate": ((512, 128), F32),
        t + "wg": ((256, 128), BF),
        t + "wv": ((256, 128), BF),
    }


def tri_sems(t):
    return [t + k for k in ("1", "2", "p", "3", "4")]


def tri_prep(r, t):
    w = r[t + "_proj"][:, 0:512].astype(F32).T.reshape(4, 16, 8, 128)
    r[t + "wg"][...] = jnp.concatenate([w[0], w[2]], axis=1).astype(BF).reshape(256, 128)
    r[t + "wv"][...] = jnp.concatenate([w[1], w[3]], axis=1).astype(BF).reshape(256, 128)


def tri_part(r, t, src, dst, outgoing):
    row, col, xy, zc = where_am_i()
    m, e = in_quad()
    x = norm(r[src][...]).astype(BF).reshape(512, 128)
    both = sig(nt(r[t + "wg"][...], x)) * nt(r[t + "wv"][...], x)
    s1, r1, s2, r2 = (r[t + k] for k in ("s1", "r1", "s2", "r2"))
    s1[...] = both.astype(BF).reshape(16, 16, 512)
    e1 = Swap(r, t + "1")
    e1.exchange("xy", s1, r1)
    r[t + "gate"][...] = sig(nn(x, r[t + "_proj"][:, 512:640]))
    by_quad = perm((16, 2, 8), (2, 1, 0))
    e1.got(r1)
    s2[...] = nn(by_quad, r1[...].reshape(256, 512)).astype(BF).reshape(8, 32, 512)
    e2 = Swap(r, t + "2")
    if outgoing:
        e2.out(s2, r2)
        natural = perm((8, 16), (1, 0))
    else:
        e2.ring(lambda m, e: s2.at[m, :, pl.ds(pl.multiple_of(e * 128, 128), 128)], r2)
        natural = perm((16, 8), (1, 0))
    e2.got(r2)
    ps, pr = r[t + "ps"], r[t + "pr"]
    ep = Swap(r, t + "p")
    if outgoing:
        left = r2[:, 0:16, :].reshape(128, 512)
        right = nn(natural, r2[:, 16:32, :].reshape(128, 512)).astype(BF)
        left = jnp.concatenate([left[:, 128 * q : 128 * q + 128] for q in range(4)], axis=0)
        for q in range(4):
            ps[q] = nt(left, right[:, 128 * q : 128 * q + 128]).astype(BF)
    else:
        left = jnp.concatenate(
            [nt(natural, r2[:, c, 0:16, :].reshape(128, 128)).astype(BF) for c in range(4)], axis=0
        )
        for c in range(4):
            ps[c] = nn(left, r2[:, c, 16:32, :].reshape(128, 128)).astype(BF)
    ep.exchange("quad", ps, pr)
    ep.got(pr)
    mix = (pr[0].astype(F32) + pr[1].astype(F32)) + (pr[2].astype(F32) + pr[3].astype(F32))
    mix = mix.astype(BF).reshape(4, 8, 16, 128)
    s3, r3, s4, r4 = (r[t + k] for k in ("s3", "r3", "s4", "r4"))
    for q in range(4):
        s3[:, 16 * q : 16 * q + 16] = mix[q]
    e3 = Swap(r, t + "3")
    e3.back(s3, r3)
    by_plane = perm((8, 4, 16), (2, 1, 0))
    e3.got(r3)
    s4[...] = nn(by_plane, r3[...].reshape(512, 128)).astype(BF).reshape(16, 32, 128)
    e4 = Swap(r, t + "4")
    e4.exchange("xy", s4, r4)
    e4.got(r4)
    got = r4[...].astype(F32)
    for q in range(4):
        step = tn(norm(got[:, 8 * q : 8 * q + 8].reshape(128, 128), 0).astype(BF), r[t + "_out"][...])
        r[dst][q] = r[src][q] + r[t + "gate"][128 * q : 128 * q + 128] * step
    e1.sent(s1.at[pl.ds(0, 15)])
    if outgoing:
        e2.sent8(s2)
    else:
        e2.sent(r2.at[pl.ds(0, 7)])
        e2.sent(r2.at[0, pl.ds(0, 3)])
    ep.sent(ps.at[pl.ds(0, 3)])
    e3.sent8(s3)
    e4.sent(s4.at[pl.ds(0, 15)])


SHAPES = dict(
    m1=((2, 128, 256), BF),
    z1=((4, 128, 128), F32),
    z2=((4, 128, 128), F32),
    z3=((4, 128, 128), F32),
    msa_out=((2, 128, 256), BF),
)


PARTS = dict(
    row=dict(ins=["msa", "pairs", "row_w", "row_out", "pair_bias"], outs=["m1"], scratch=ROW_SCRATCH, sems=ROW_SEMS),
    col=dict(
        ins=["m1", "pairs", "col_w", "col_out", "maps", "outer_out"],
        outs=["msa_out", "z1"],
        scratch=COL_SCRATCH,
        sems=COL_SEMS,
    ),
    out=dict(ins=["z1", "o_proj", "o_out"], outs=["z2"], scratch=tri_scratch("o", True), sems=tri_sems("o")),
    inc=dict(ins=["z2", "i_proj", "i_out"], outs=["z3"], scratch=tri_scratch("i", False), sems=tri_sems("i")),
)


def run_parts(parts, arrays, results, number):
    ins, made, scratch, sems = [], [], {}, []
    for p in parts:
        spec = PARTS[p]
        ins += [n for n in spec["ins"] if n not in ins and n not in made]
        made += spec["outs"]
        scratch.update(spec["scratch"])
        sems += spec["sems"]
    outs = [n for n in made if n in results]
    inner = {n: SHAPES[n] for n in made if n not in results}
    scratch = {**scratch, **inner}
    sem_names = [s + e for s in sems for e in ("_s", "_r")]

    def body(*refs):
        r = dict(zip(ins + outs + list(scratch) + sem_names, refs))
        barrier_signal()

        def prep():
            if "col" in parts:
                col_prep(r)
            if "out" in parts:
                tri_prep(r, "o")
            if "inc" in parts:
                tri_prep(r, "i")

        if parts[0] == "row":
            r["prep"] = prep
        else:
            prep()
            barrier_wait()
        for p in parts:
            if p == "row":
                row_part(r)
            elif p == "col":
                col_part(r)
            elif p == "out":
                tri_part(r, "o", "z1", "z2", True)
            else:
                tri_part(r, "i", "z2", "z3", False)

    vm = pl.BlockSpec(memory_space=pltpu.VMEM)
    got = pl.pallas_call(
        body,
        out_shape=[jax.ShapeDtypeStruct(*SHAPES[n]) for n in outs],
        in_specs=[vm] * len(ins),
        out_specs=[vm] * len(outs),
        scratch_shapes=[pltpu.VMEM(*scratch[n]) for n in scratch] + [pltpu.SemaphoreType.DMA] * len(sem_names),
        compiler_params=pltpu.CompilerParams(
            collective_id=number, has_side_effects=True, vmem_limit_bytes=56 * 1024 * 1024
        ),
        name="_".join(parts),
    )(*[arrays[n] for n in ins])
    arrays.update(zip(outs, got))


GROUPS = [["row", "col", "out", "inc"]]


def shards(*args, groups=None, results=("msa_out", "z3")):
    groups = groups or GROUPS
    names = ["msa", "pairs", "row_w", "row_out", "pair_bias", "col_w", "col_out", "maps", "outer_out"]
    names += ["o_proj", "o_out", "i_proj", "i_out"]
    arrays = dict(zip(names, args))
    msa_shape, pair_shape = arrays["msa"].shape, arrays["pairs"].shape
    arrays["msa"] = arrays["msa"].reshape(2, 128, 256)
    arrays["pairs"] = arrays["pairs"].reshape(4, 128, 128)
    for number, group in enumerate(groups):
        later = [n for g in groups[number + 1 :] for p in g for n in PARTS[p]["ins"]]
        run_parts(group, arrays, set(results) | set(later), number)
    outs = dict(
        msa_out=lambda a: a.reshape(msa_shape),
        z3=lambda a: a.reshape(pair_shape),
    )
    return tuple(outs.get(n, lambda a: a)(arrays[n]) for n in results)


def solution(mesh):
    return jax.shard_map(
        shards,
        mesh=mesh,
        in_specs=(P("row", None, "col", None, None),) * 2 + (P(),) * 11,
        out_specs=(P("row", None, "col", None, None),) * 2,
        check_vma=False,
    )
```

```python
import functools
import math

import jax
import jax.numpy as jnp
from jax import lax
from jax.experimental import pallas as pl
from jax.experimental.pallas import tpu as pltpu
from jax.sharding import PartitionSpec as P

MESH = pl.DeviceIdType.MESH
BF = jnp.bfloat16
F32 = jnp.float32
EPS = 1e-05
HEADS = 8
NXY = 16
NZC = 8
NCOL = 4


def nn(a, b):
    return lax.dot_general(a, b, (((1,), (0,)), ((), ())), preferred_element_type=F32)


def nt(a, b):
    return lax.dot_general(a, b, (((1,), (1,)), ((), ())), preferred_element_type=F32)


def tn(a, b):
    return lax.dot_general(a, b, (((0,), (0,)), ((), ())), preferred_element_type=F32)


def norm(x, axis=-1):
    c = x - jnp.mean(x, axis=axis, keepdims=True)
    v = jnp.mean(c * c, axis=axis, keepdims=True)
    return c * lax.rsqrt(v + EPS)


def sig(x):
    return 1.0 / (1.0 + jnp.exp(-x))


def perm(sizes, order):
    n = math.prod(sizes)
    strides = [math.prod(sizes[k + 1 :]) for k in range(len(sizes))]
    out = lax.broadcasted_iota(jnp.int32, (n, n), 0)
    src = jnp.zeros((n, n), jnp.int32)
    rest = out
    for axis in reversed(order):
        src = src + (rest & (sizes[axis] - 1)) * strides[axis]
        rest = lax.shift_right_logical(rest, int(math.log2(sizes[axis])))
    inp = lax.broadcasted_iota(jnp.int32, (n, n), 1)
    return jnp.where(src == inp, 1.0, 0.0).astype(BF)


def where_am_i():
    row, col = lax.axis_index("row"), lax.axis_index("col")
    return row, col, row // NZC, row % NZC


def in_quad():
    row, col, xy, zc = where_am_i()
    return 2 * col + zc // 4, zc % 4


def place(xy, m, e):
    return xy * NZC + m % 2 * 4 + e, m // 2


class Swap:
    def __init__(self, r, name):
        self.send, self.recv = r[name + "_s"], r[name + "_r"]
        self.row, self.col, self.xy, self.zc = where_am_i()
        self.m, self.e = in_quad()

    def put(self, src, dst, row, col):
        pltpu.make_async_remote_copy(
            src_ref=src,
            dst_ref=dst,
            send_sem=self.send,
            recv_sem=self.recv,
            device_id=(row, col),
            device_id_type=MESH,
        ).start()

    def keep(self, src, dst):
        pltpu.make_async_copy(src, dst, self.recv).start()

    def peers(self, kind):
        if kind == "xy":
            for d in range(1, NXY):
                g = lax.rem(self.xy + d, NXY)
                yield g, g * NZC + self.zc, self.col
        elif kind == "zc":
            for d in range(1, NZC):
                g = lax.rem(self.zc + d, NZC)
                yield g, self.xy * NZC + g, self.col
        elif kind == "quad":
            for d in range(1, 4):
                g = lax.rem(self.e + d, 4)
                yield g, *place(self.xy, self.m, g)
        else:
            for d in range(1, NCOL):
                g = lax.rem(self.col + d, NCOL)
                yield g, self.row, g

    def mine(self, kind):
        return {"xy": self.xy, "zc": self.zc, "col": self.col, "quad": self.e}[kind]

    def exchange(self, kind, src, dst):
        me = self.mine(kind)
        for g, row, col in self.peers(kind):
            self.put(src.at[g], dst.at[me], row, col)
        self.keep(src.at[me], dst.at[me])

    def gather(self, kind, buf):
        me = self.mine(kind)
        for g, row, col in self.peers(kind):
            self.put(buf.at[me], buf.at[me], row, col)

    def either(self, src, dst, away, row, col):
        @pl.when(away)
        def _():
            self.put(src, dst, row, col)

        @pl.when(jnp.logical_not(away))
        def _():
            self.keep(src, dst)

    def out(self, src, dst):
        for d in range(1, 8):
            m = lax.rem(self.m + d, 8)
            self.put(src.at[m], dst.at[self.zc], *place(self.xy, m, self.col))
        row, col = place(self.xy, self.m, self.col)
        self.either(src.at[self.m], dst.at[self.zc], self.e != self.col, row, col)

    def back(self, src, dst):
        for d in range(1, 8):
            g = lax.rem(self.zc + d, 8)
            self.put(src.at[g], dst.at[self.m], self.xy * NZC + g, self.e)
        self.either(src.at[self.zc], dst.at[self.m], self.e != self.col, self.row, self.e)

    def out_by_row(self, src, dst):
        slot = dst.at[self.zc // 4, self.col]
        for d in range(1, 8):
            m = lax.rem(self.m + d, 8)
            self.put(src.at[m], slot, *place(self.xy, m, self.e))
        self.keep(src.at[self.m], slot)

    def sent8(self, src):
        self.sent(src.at[pl.ds(0, 7)])

        @pl.when(self.e != self.col)
        def _():
            self.sent(src.at[0])

    def got(self, ref):
        pltpu.make_async_copy(ref, ref, self.recv).wait()

    def sent(self, ref):
        pltpu.make_async_copy(ref, ref, self.send).wait()


def barrier_signal():
    row, col, xy, zc = where_am_i()
    m, e = in_quad()
    sem = pltpu.get_barrier_semaphore()

    def hail(r, c):
        pl.semaphore_signal(sem, inc=1, device_id=(r, c), device_id_type=MESH)

    for d in range(1, NXY):
        hail(lax.rem(xy + d, NXY) * NZC + zc, col)
    for d in range(1, 32):
        t = lax.rem(m * 4 + e + d, 32)
        hail(*place(xy, t // 4, t % 4))


def barrier_wait():
    pl.semaphore_wait(pltpu.get_barrier_semaphore(), NXY + 32 - 2)


def project(keys, own, weights):
    q = nn(own, weights[:, 0:256]).astype(BF)
    k = nn(keys, weights[:, 256:512]).astype(BF)
    v = nn(keys, weights[:, 512:768]).astype(BF)
    gate = nn(own, weights[:, 768:1024]).astype(BF).astype(F32)
    return q, k, jnp.concatenate([v, jnp.ones((keys.shape[0], 128), BF)], axis=1), gate


def attend(q, k, v, heads, bias):
    head = lax.broadcasted_iota(jnp.int32, q.shape, 1) // 32
    total = jnp.zeros(q.shape, F32)
    for h in heads:
        scores = nt(jnp.where(head == h, q, jnp.zeros_like(q)), k) * (1.0 / math.sqrt(32.0))
        if bias is not None:
            scores = scores + bias(h)
        top = jnp.max(scores, axis=-1, keepdims=True)
        p = jnp.exp(scores - top).astype(BF)
        mixed = nn(p, v)
        inv = 1.0 / mixed[:, 256:384]
        mixed = mixed[:, 0:256] * jnp.concatenate([inv, inv], axis=1)
        total = total + jnp.where(head == h, mixed, 0.0)
    return total


def by_kind(ref):
    w = ref[...]
    return jnp.concatenate(
        [w[:, 128 * h + 32 * k : 128 * h + 32 * k + 32] for k in range(4) for h in range(HEADS)], axis=1
    )


ROW_SCRATCH = dict(
    xr=((2, 128, 256), BF),
    xg=((2, 4, 128, 256), BF),
    bs=((2, 2, 8, 128), F32),
    bo=((2, 8, 128), F32),
    bq=((2, 16, 128), BF),
    brecv=((4, 4, 16, 128), BF),
    bx=((16, 128, 256), BF),
    wrow=((256, 1024), BF),
)
ROW_SEMS = ["m0", "m1", "g0", "g1", "bc", "b0", "b2", "b3"]


def row_part(r):
    row, col, xy, zc = where_am_i()
    m, e = in_quad()
    msa, xr, xg = r["msa"], r["xr"], r["xg"]
    zn = norm(r["pairs"][...].astype(F32)).astype(BF).reshape(512, 128)
    bias_t = nt(r["pair_bias"][...], zn)
    for k in range(4):
        r["bs"][k // 2, k % 2] = bias_t[:, 128 * k : 128 * k + 128]
    core = lax.rem(zc, 2)
    barrier_wait()
    sc = Swap(r, "bc")
    sc.put(r["bs"].at[1 - core], r["bo"], row + 1 - 2 * core, col)
    sc.got(r["bo"])
    ours, theirs = r["bs"][core], r["bo"][...]
    r["bq"][...] = jnp.concatenate(
        [jnp.where(core == 0, ours, theirs), jnp.where(core == 0, theirs, ours)], axis=1
    ).astype(BF)
    s0 = Swap(r, "b0")
    slot = r["brecv"].at[zc // 2, col]
    for d in range(1, 8):
        for k in range(2):
            s0.put(r["bq"].at[k], slot, *place(xy, lax.rem(m + d, 8), 2 * core + k))
    for k in range(2):
        s0.either(r["bq"].at[k], slot, e != 2 * core + k, *place(xy, m, 2 * core + k))
    direct = [Swap(r, "m0"), Swap(r, "m1")]
    away = jnp.logical_or(zc != m, col != e)
    for s in range(2):
        direct[s].either(msa.at[s], xr.at[s], away, *place(xy, zc, col))
    r["wrow"][...] = by_kind(r["row_w"])
    pz = perm((2, 4, 2, 2, 4), (3, 0, 4, 1, 2))
    shared = [Swap(r, "g0"), Swap(r, "g1")]

    def share(s):
        direct[s].got(xr.at[s])
        xg[s, e] = norm(xr[s].astype(F32)).astype(BF)
        shared[s].gather("quad", xg.at[s])

    s0.got(r["brecv"])
    b = r["brecv"]
    lo = jnp.concatenate([b[:, 0], b[:, 1]], axis=2).reshape(64, 256)
    hi = jnp.concatenate([b[:, 2], b[:, 3]], axis=2).reshape(64, 256)
    rows = jnp.concatenate([lo, hi], axis=0)
    r["bx"][xy] = nn(pz, rows).astype(BF)
    s2 = [Swap(r, "b2"), Swap(r, "b3")]
    for k in range(2):
        s2[k].gather("xy", r["bx"].at[:, pl.ds(64 * k, 64)])
    share(0)
    share(1)
    if "prep" in r:
        r["prep"]()
    ready = []
    for s in range(2):
        shared[s].got(xg.at[s, pl.ds(0, 3)])
        ready.append(project(xg[s].reshape(512, 256), xg[s, e], r["wrow"]))
    cache = {}
    to_zc = perm((16, 8), (1, 0))

    def bias(h):
        if h not in cache:
            pair = h // 2 * 2
            parts = []
            for jh in range(2):
                at = (h // 4 * 8 + jh * 4 + pair % 4) * 8
                parts.append(r["bx"][:, at : at + 16, :].astype(F32))
            for k in range(2):
                cache[pair + k] = jnp.concatenate(
                    [p[:, 8 * k : 8 * k + 8].reshape(128, 256) for p in parts], axis=1
                )
        return cache[h]

    totals = []
    for part in range(2):
        s2[part].got(r["bx"].at[pl.ds(0, 15), pl.ds(64 * part, 64)])
        for s in range(2):
            q, k, v, gate = ready[s]
            cache.clear()
            mixed = attend(q, k, v, range(4 * part, 4 * part + 4), bias)
            if part == 0:
                totals.append(mixed)
                continue
            gated = (sig(gate) * (totals[s] + mixed)).astype(BF)
            m1 = (xr[s].astype(F32) + nn(gated, r["row_out"][...])).astype(BF)
            r["cs1"][:, 16 * s : 16 * s + 16] = nn(to_zc, m1).astype(BF).reshape(8, 16, 256)
            rows = pl.ds(16 * s, 16)
            Swap(r, "c1" + "ab"[s]).back(r["cs1"].at[:, rows], r["cr1"].at[:, rows])
    def row_sent():
        for s in range(2):
            shared[s].sent(xg.at[s, pl.ds(0, 3)])

            @pl.when(away)
            def _():
                direct[s].sent(msa.at[s])

        s0.sent(r["brecv"].at[pl.ds(0, 3)])
        s0.sent(r["brecv"].at[0, pl.ds(0, 2)])
        for k in range(2):

            @pl.when(e != 2 * core + k)
            def _():
                s0.sent(r["bq"].at[k])

        sc.sent(r["bo"])
        for k in range(2):
            s2[k].sent(r["bx"].at[pl.ds(0, 15), pl.ds(64 * k, 64)])

    return row_sent


COL_SCRATCH = dict(
    cs1=((8, 32, 256), BF),
    cr1=((8, 32, 256), BF),
    cs2=((16, 16, 256), BF),
    cr2=((16, 16, 256), BF),
    ds1=((16, 16, 256), BF),
    dr1=((16, 16, 256), BF),
    ds2=((8, 32, 256), BF),
    dr2=((8, 32, 256), BF),
    lg=((4, 32, 256), BF),
    rz=((8, 32, 256), BF),
    rx=((16, 256, 256), BF),
    wcol=((256, 1024), BF),
    bd=((32, 128, 512), BF),
    at=((32, 256, 512), BF),
)
COL_SEMS = ["c1a", "c1b", "c2", "d1", "d2", "lg", "rz", "rx", "rc"]


def col_prep(r):
    r["wcol"][...] = by_kind(r["col_w"])
    by_u = nn(perm((32, 32), (1, 0)), r["outer_out"][...]).astype(BF).reshape(32, 32, 128)
    r["bd"][...] = jnp.zeros((32, 128, 512), BF)
    for i in range(4):
        r["bd"][:, 32 * i : 32 * i + 32, 128 * i : 128 * i + 128] = by_u


def col_part(r):
    row, col, xy, zc = where_am_i()
    core = lax.rem(zc, 2)
    to_xy = perm((8, 2, 16), (2, 0, 1))
    c1 = [Swap(r, "c1a"), Swap(r, "c1b")]
    for k in range(2):
        c1[k].got(r["cr1"].at[:, pl.ds(16 * k, 16)])
    r["cs2"][...] = nn(to_xy, r["cr1"][...].reshape(256, 256)).astype(BF).reshape(16, 16, 256)
    c2 = Swap(r, "c2")
    c2.exchange("xy", r["cs2"], r["cr2"])
    c2.got(r["cr2"])
    lines = r["cr2"][...].reshape(256, 256).astype(F32)
    x = norm(lines).astype(BF)
    q, k, v, gate = project(x, x, r["wcol"])
    gated = (sig(gate) * attend(q, k, v, range(HEADS), None)).astype(BF)
    m2 = lines + nn(gated, r["col_out"][...])
    x = norm(m2).astype(BF)
    ab = nt(r["maps"][...], x).astype(BF)
    r["lg"][col] = ab[0:32]
    r["rz"][zc] = ab[32:64]
    rz = Swap(r, "rz")
    rz.gather("zc", r["rz"])
    lg = Swap(r, "lg")
    lg.gather("col", r["lg"])
    r["ds1"][...] = m2.astype(BF).reshape(16, 16, 256)
    d1 = Swap(r, "d1")
    d1.exchange("xy", r["ds1"], r["dr1"])
    rz.got(r["rz"].at[pl.ds(0, 7)])
    right = nn(perm((8, 32), (1, 0)), r["rz"][...].reshape(256, 256)).astype(BF)
    rx = r["rx"]
    for k in range(2):

        @pl.when(core == k)
        def _():
            rx[xy, 128 * k : 128 * k + 128] = right[128 * k : 128 * k + 128]

    half = pl.ds(pl.multiple_of(core * 128, 128), 128)
    other = pl.ds(pl.multiple_of(128 - core * 128, 128), 128)
    rxs = Swap(r, "rx")
    for g, prow, pcol in rxs.peers("xy"):
        rxs.put(rx.at[xy, half], rx.at[xy, half], prow, pcol)
    d1.got(r["dr1"])
    r["ds2"][...] = nn(perm((16, 8, 2), (1, 2, 0)), r["dr1"][...].reshape(256, 256)).astype(BF).reshape(8, 32, 256)
    d2 = Swap(r, "d2")
    d2.exchange("zc", r["ds2"], r["dr2"])
    lg.got(r["lg"].at[pl.ds(0, 3)])
    left = r["lg"][...].reshape(128, 256).T
    for u in range(32):
        r["at"][u] = nn(left, r["bd"][u]).astype(BF)
    rxs.got(rx.at[pl.ds(0, 15), pl.ds(0, 128)])
    rc = Swap(r, "rc")
    rc.put(rx.at[:, half], rx.at[:, half], row + 1 - 2 * core, col)
    d2.got(r["dr2"])
    r["msa_out"][...] = (
        nn(perm((8, 2, 16), (1, 2, 0)), r["dr2"][...].reshape(256, 256)).astype(BF).reshape(2, 128, 256)
    )

    def add(base, acc):
        for up in range(8):
            at = pl.multiple_of(base * 8 + up * 16, 16)
            block = rx[:, pl.ds(at, 16), :].astype(F32)
            for k in range(2):
                acc = acc + nn(block[:, 8 * k : 8 * k + 8].reshape(128, 256).astype(BF), r["at"][base + 2 * up + k])
        return acc

    acc = add(core * 16, jnp.zeros((128, 512), F32))
    rc.got(rx.at[:, other])
    acc = add(16 - core * 16, acc)
    for i in range(4):
        r["z1"][i] = r["pairs"][i].astype(F32) + acc[:, 128 * i : 128 * i + 128] * (1.0 / 256.0)
    def col_sent():
        for k in range(2):
            c1[k].sent8(r["cs1"].at[:, pl.ds(16 * k, 16)])
        c2.sent(r["cs2"].at[pl.ds(0, 15)])
        d1.sent(r["ds1"].at[pl.ds(0, 15)])
        d2.sent(r["ds2"].at[pl.ds(0, 7)])
        lg.sent(r["lg"].at[pl.ds(0, 3)])
        rz.sent(r["rz"].at[pl.ds(0, 7)])
        rxs.sent(rx.at[pl.ds(0, 15), pl.ds(0, 128)])
        rc.sent(rx.at[:, half])

    return col_sent


def tri_scratch(t, outgoing):
    return {
        t + "s1": ((16, 16, 512), BF),
        t + "r1": ((16, 16, 512), BF),
        t + "s2": ((8, 32, 512), BF),
        t + "r2": ((8, 32, 512) if outgoing else (2, 4, 32, 512), BF),
        t + "ps": ((4, 512, 128), BF),
        t + "pr": ((4, 512, 128), BF),
        t + "s3": ((8, 64, 128), BF),
        t + "r3": ((8, 64, 128), BF),
        t + "s4": ((16, 32, 128), BF),
        t + "r4": ((16, 32, 128), BF),
        t + "gate": ((512, 128), F32),
        t + "wg": ((256, 128), BF),
        t + "wv": ((256, 128), BF),
    }


def tri_sems(t):
    return [t + k for k in ("1", "2", "p0", "p1", "30", "31", "40", "41")]


def tri_prep(r, t):
    w = r[t + "_proj"][:, 0:512].astype(F32).T.reshape(4, 16, 8, 128)
    r[t + "wg"][...] = jnp.concatenate([w[0], w[2]], axis=1).astype(BF).reshape(256, 128)
    r[t + "wv"][...] = jnp.concatenate([w[1], w[3]], axis=1).astype(BF).reshape(256, 128)


def tri_part(r, t, src, dst, outgoing):
    row, col, xy, zc = where_am_i()
    m, e = in_quad()
    x = norm(r[src][...]).astype(BF).reshape(512, 128)
    both = sig(nt(r[t + "wg"][...], x)) * nt(r[t + "wv"][...], x)
    s1, r1, s2, r2 = (r[t + k] for k in ("s1", "r1", "s2", "r2"))
    s1[...] = both.astype(BF).reshape(16, 16, 512)
    e1 = Swap(r, t + "1")
    e1.exchange("xy", s1, r1)
    r[t + "gate"][...] = sig(nn(x, r[t + "_proj"][:, 512:640]))
    by_quad = perm((16, 2, 8), (2, 1, 0))
    e1.got(r1)
    s2[...] = nn(by_quad, r1[...].reshape(256, 512)).astype(BF).reshape(8, 32, 512)
    e2 = Swap(r, t + "2")
    if outgoing:
        e2.out(s2, r2)
        natural = perm((8, 16), (1, 0))
    else:
        e2.out_by_row(s2, r2)
        natural = perm((16, 8), (1, 0))
    e2.got(r2)
    ps, pr = r[t + "ps"], r[t + "pr"]
    s3, r3, s4, r4 = (r[t + k] for k in ("s3", "r3", "s4", "r4"))
    if outgoing:
        left = r2[:, 0:16, :].reshape(128, 512)
        right = nn(natural, r2[:, 16:32, :].reshape(128, 512)).astype(BF)
        left = jnp.concatenate([left[:, 128 * q : 128 * q + 128] for q in range(4)], axis=0)
        right = [right[:, 128 * q : 128 * q + 128] for q in range(4)]
    else:

        def side(c, at):
            block = r2[:, c, at : at + 16, :].reshape(32, 512)
            return jnp.concatenate([block[:, 128 * q : 128 * q + 128] for q in range(4)], axis=0)

        left = jnp.concatenate([nt(natural, side(c, 0)).astype(BF) for c in range(4)], axis=0)
        right = [side(c, 16) for c in range(4)]
    ep = [Swap(r, t + "p0"), Swap(r, t + "p1")]
    e3 = [Swap(r, t + "30"), Swap(r, t + "31")]
    e4 = [Swap(r, t + "40"), Swap(r, t + "41")]
    for half in range(2):
        rows = pl.ds(256 * half, 256)
        part = left[256 * half : 256 * half + 256]
        for c in range(4):
            ps[c, rows] = (nt if outgoing else nn)(part, right[c]).astype(BF)
        ep[half].exchange("quad", ps.at[:, rows], pr.at[:, rows])
    by_plane = perm((8, 2, 16), (2, 1, 0))
    for half in range(2):
        rows = pl.ds(256 * half, 256)
        ep[half].got(pr.at[:, rows])
        mix = (pr[0, rows].astype(F32) + pr[1, rows].astype(F32)) + (pr[2, rows].astype(F32) + pr[3, rows].astype(F32))
        mix = mix.astype(BF).reshape(2, 8, 16, 128)
        for q in range(2):
            s3[:, 32 * half + 16 * q : 32 * half + 16 * q + 16] = mix[q]
        rows = pl.ds(32 * half, 32)
        e3[half].back(s3.at[:, rows], r3.at[:, rows])
    for half in range(2):
        rows = pl.ds(32 * half, 32)
        e3[half].got(r3.at[:, rows])
        rows4 = pl.ds(16 * half, 16)
        s4[:, rows4] = nn(by_plane, r3[:, rows].reshape(256, 128)).astype(BF).reshape(16, 16, 128)
        e4[half].exchange("xy", s4.at[:, rows4], r4.at[:, rows4])
    for half in range(2):
        rows4 = pl.ds(16 * half, 16)
        e4[half].got(r4.at[:, rows4])
        got = r4[:, rows4].astype(F32)
        for k in range(2):
            q = 2 * half + k
            step = tn(norm(got[:, 8 * k : 8 * k + 8].reshape(128, 128), 0).astype(BF), r[t + "_out"][...])
            r[dst][q] = r[src][q] + r[t + "gate"][128 * q : 128 * q + 128] * step
    def tri_sent():
        e1.sent(s1.at[pl.ds(0, 15)])
        if outgoing:
            e2.sent8(s2)
        else:
            e2.sent(s2.at[pl.ds(0, 7)])
        for half in range(2):
            ep[half].sent(ps.at[pl.ds(0, 3), pl.ds(0, 256)])
            e3[half].sent8(s3.at[:, pl.ds(32 * half, 32)])
            e4[half].sent(s4.at[pl.ds(0, 15), pl.ds(0, 16)])

    return tri_sent


SHAPES = dict(
    z1=((4, 128, 128), F32),
    z2=((4, 128, 128), F32),
    z3=((4, 128, 128), F32),
    msa_out=((2, 128, 256), BF),
)


PARTS = dict(
    row=dict(ins=["msa", "pairs", "row_w", "row_out", "pair_bias"], outs=[], scratch=ROW_SCRATCH, sems=ROW_SEMS),
    col=dict(
        ins=["pairs", "col_w", "col_out", "maps", "outer_out"],
        outs=["msa_out", "z1"],
        scratch=COL_SCRATCH,
        sems=COL_SEMS,
    ),
    out=dict(ins=["z1", "o_proj", "o_out"], outs=["z2"], scratch=tri_scratch("o", True), sems=tri_sems("o")),
    inc=dict(ins=["z2", "i_proj", "i_out"], outs=["z3"], scratch=tri_scratch("i", False), sems=tri_sems("i")),
)


def run_parts(parts, arrays, results, number):
    ins, made, scratch, sems = [], [], {}, []
    for p in parts:
        spec = PARTS[p]
        ins += [n for n in spec["ins"] if n not in ins and n not in made]
        made += spec["outs"]
        scratch.update(spec["scratch"])
        sems += spec["sems"]
    outs = [n for n in made if n in results]
    inner = {n: SHAPES[n] for n in made if n not in results}
    scratch = {**scratch, **inner}
    sem_names = [s + e for s in sems for e in ("_s", "_r")]

    def body(*refs):
        r = dict(zip(ins + outs + list(scratch) + sem_names, refs))
        barrier_signal()

        def prep():
            if "col" in parts:
                col_prep(r)
            if "out" in parts:
                tri_prep(r, "o")
            if "inc" in parts:
                tri_prep(r, "i")

        if parts[0] == "row":
            r["prep"] = prep
        else:
            prep()
            barrier_wait()
        waits = []
        for p in parts:
            if p == "row":
                waits.append(row_part(r))
            elif p == "col":
                waits.append(col_part(r))
            elif p == "out":
                waits.append(tri_part(r, "o", "z1", "z2", True))
            else:
                waits.append(tri_part(r, "i", "z2", "z3", False))
        for wait in waits:
            wait()

    vm = pl.BlockSpec(memory_space=pltpu.VMEM)
    got = pl.pallas_call(
        body,
        out_shape=[jax.ShapeDtypeStruct(*SHAPES[n]) for n in outs],
        in_specs=[vm] * len(ins),
        out_specs=[vm] * len(outs),
        scratch_shapes=[pltpu.VMEM(*scratch[n]) for n in scratch] + [pltpu.SemaphoreType.DMA] * len(sem_names),
        compiler_params=pltpu.CompilerParams(
            collective_id=number, has_side_effects=True, vmem_limit_bytes=56 * 1024 * 1024
        ),
        name="_".join(parts),
    )(*[arrays[n] for n in ins])
    arrays.update(zip(outs, got))


GROUPS = [["row", "col", "out", "inc"]]


def shards(*args, groups=None, results=("msa_out", "z3")):
    groups = groups or GROUPS
    names = ["msa", "pairs", "row_w", "row_out", "pair_bias", "col_w", "col_out", "maps", "outer_out"]
    names += ["o_proj", "o_out", "i_proj", "i_out"]
    arrays = dict(zip(names, args))
    msa_shape, pair_shape = arrays["msa"].shape, arrays["pairs"].shape
    arrays["pair_bias"], arrays["maps"] = arrays["pair_bias"].T, arrays["maps"].T
    arrays["msa"] = arrays["msa"].reshape(2, 128, 256)
    arrays["pairs"] = arrays["pairs"].reshape(4, 128, 128)
    for number, group in enumerate(groups):
        later = [n for g in groups[number + 1 :] for p in g for n in PARTS[p]["ins"]]
        run_parts(group, arrays, set(results) | set(later), number)
    outs = dict(
        msa_out=lambda a: a.reshape(msa_shape),
        z3=lambda a: a.reshape(pair_shape),
    )
    return tuple(outs.get(n, lambda a: a)(arrays[n]) for n in results)


def solution(mesh):
    return jax.shard_map(
        shards,
        mesh=mesh,
        in_specs=(P("row", None, "col", None, None),) * 2 + (P(),) * 11,
        out_specs=(P("row", None, "col", None, None),) * 2,
        check_vma=False,
    )
```

```python
import functools
import math

import jax
import jax.numpy as jnp
from jax import lax
from jax.experimental import pallas as pl
from jax.experimental.pallas import tpu as pltpu
from jax.sharding import PartitionSpec as P

MESH = pl.DeviceIdType.MESH
BF = jnp.bfloat16
F32 = jnp.float32
EPS = 1e-05
HEADS = 8
NXY = 16
NZC = 8
NCOL = 4


def nn(a, b):
    return lax.dot_general(a, b, (((1,), (0,)), ((), ())), preferred_element_type=F32)


def nt(a, b):
    return lax.dot_general(a, b, (((1,), (1,)), ((), ())), preferred_element_type=F32)


def tn(a, b):
    return lax.dot_general(a, b, (((0,), (0,)), ((), ())), preferred_element_type=F32)


def norm(x, axis=-1):
    c = x - jnp.mean(x, axis=axis, keepdims=True)
    v = jnp.mean(c * c, axis=axis, keepdims=True)
    return c * lax.rsqrt(v + EPS)


def sig(x):
    return 1.0 / (1.0 + jnp.exp(-x))


def perm(sizes, order, first=0, count=None):
    n = math.prod(sizes)
    count = count or n
    strides = [math.prod(sizes[k + 1 :]) for k in range(len(sizes))]
    out = lax.broadcasted_iota(jnp.int32, (count, 1), 0) + first
    src = jnp.zeros((count, 1), jnp.int32)
    rest = out
    for axis in reversed(order):
        src = src + (rest & (sizes[axis] - 1)) * strides[axis]
        rest = lax.shift_right_logical(rest, int(math.log2(sizes[axis])))
    inp = lax.broadcasted_iota(jnp.int32, (count, n), 1)
    return jnp.where(src == inp, 1.0, 0.0).astype(BF)


def where_am_i():
    row, col = lax.axis_index("row"), lax.axis_index("col")
    return row, col, row // NZC, row % NZC


def in_quad():
    row, col, xy, zc = where_am_i()
    return 2 * col + zc // 4, zc % 4


def place(xy, m, e):
    return xy * NZC + m % 2 * 4 + e, m // 2


class Swap:
    def __init__(self, r, name):
        self.send, self.recv = r[name + "_s"], r[name + "_r"]
        self.row, self.col, self.xy, self.zc = where_am_i()
        self.m, self.e = in_quad()

    def put(self, src, dst, row, col):
        pltpu.make_async_remote_copy(
            src_ref=src,
            dst_ref=dst,
            send_sem=self.send,
            recv_sem=self.recv,
            device_id=(row, col),
            device_id_type=MESH,
        ).start()

    def keep(self, src, dst):
        pltpu.make_async_copy(src, dst, self.recv).start()

    def peers(self, kind):
        if kind == "xy":
            for d in range(1, NXY):
                g = lax.rem(self.xy + d, NXY)
                yield g, g * NZC + self.zc, self.col
        elif kind == "zc":
            for d in range(1, NZC):
                g = lax.rem(self.zc + d, NZC)
                yield g, self.xy * NZC + g, self.col
        elif kind == "quad":
            for d in range(1, 4):
                g = lax.rem(self.e + d, 4)
                yield g, *place(self.xy, self.m, g)
        else:
            for d in range(1, NCOL):
                g = lax.rem(self.col + d, NCOL)
                yield g, self.row, g

    def mine(self, kind):
        return {"xy": self.xy, "zc": self.zc, "col": self.col, "quad": self.e}[kind]

    def exchange(self, kind, src, dst):
        me = self.mine(kind)
        for g, row, col in self.peers(kind):
            self.put(src.at[g], dst.at[me], row, col)
        self.keep(src.at[me], dst.at[me])

    def gather(self, kind, buf):
        me = self.mine(kind)
        for g, row, col in self.peers(kind):
            self.put(buf.at[me], buf.at[me], row, col)

    def either(self, src, dst, away, row, col):
        @pl.when(away)
        def _():
            self.put(src, dst, row, col)

        @pl.when(jnp.logical_not(away))
        def _():
            self.keep(src, dst)

    def direct(self, src, slot, member):
        core = lax.rem(self.zc, 2)
        here = self.xy * 4 + self.m // 2
        for d in range(1, 64):
            g = lax.rem(here + d, 64)
            self.put(src.at[g], slot, *place(g // 4, g % 4 * 2 + core, member))
        row, col = place(self.xy, self.m // 2 * 2 + core, member)
        self.either(src.at[here], slot, self.elsewhere(member), row, col)

    def elsewhere(self, member):
        return jnp.logical_or(lax.rem(self.m, 2) != lax.rem(self.zc, 2), self.e != member)

    def sent64(self, src, member):
        self.sent(src.at[pl.ds(0, 63)])

        @pl.when(self.elsewhere(member))
        def _():
            self.sent(src.at[0])

    def back(self, src, dst):
        for d in range(1, 8):
            g = lax.rem(self.zc + d, 8)
            self.put(src.at[g], dst.at[self.m], self.xy * NZC + g, self.e)
        self.either(src.at[self.zc], dst.at[self.m], self.e != self.col, self.row, self.e)

    def sent8(self, src):
        self.sent(src.at[pl.ds(0, 7)])

        @pl.when(self.e != self.col)
        def _():
            self.sent(src.at[0])

    def got(self, ref):
        pltpu.make_async_copy(ref, ref, self.recv).wait()

    def sent(self, ref):
        pltpu.make_async_copy(ref, ref, self.send).wait()


def barrier_signal():
    row, col, xy, zc = where_am_i()
    m, e = in_quad()
    sem = pltpu.get_barrier_semaphore()

    def hail(r, c):
        pl.semaphore_signal(sem, inc=1, device_id=(r, c), device_id_type=MESH)

    for d in range(1, NXY):
        hail(lax.rem(xy + d, NXY) * NZC + zc, col)
    for d in range(1, 32):
        t = lax.rem(m * 4 + e + d, 32)
        hail(*place(xy, t // 4, t % 4))


def barrier_wait():
    pl.semaphore_wait(pltpu.get_barrier_semaphore(), NXY + 32 - 2)


def project(keys, own, weights):
    q = nn(own, weights[:, 0:256]).astype(BF)
    k = nn(keys, weights[:, 256:512]).astype(BF)
    v = nn(keys, weights[:, 512:768]).astype(BF)
    gate = nn(own, weights[:, 768:1024]).astype(BF).astype(F32)
    return q, k, jnp.concatenate([v, jnp.ones((keys.shape[0], 128), BF)], axis=1), gate


def attend(q, k, v, heads, bias):
    head = lax.broadcasted_iota(jnp.int32, q.shape, 1) // 32
    total = jnp.zeros(q.shape, F32)
    for h in heads:
        scores = nt(jnp.where(head == h, q, jnp.zeros_like(q)), k) * (1.0 / math.sqrt(32.0))
        if bias is not None:
            scores = scores + bias(h)
        top = jnp.max(scores, axis=-1, keepdims=True)
        p = jnp.exp(scores - top).astype(BF)
        mixed = nn(p, v)
        inv = 1.0 / mixed[:, 256:384]
        mixed = mixed[:, 0:256] * jnp.concatenate([inv, inv], axis=1)
        total = total + jnp.where(head == h, mixed, 0.0)
    return total


def by_kind(ref):
    w = ref[...]
    return jnp.concatenate(
        [w[:, 128 * h + 32 * k : 128 * h + 32 * k + 32] for k in range(4) for h in range(HEADS)], axis=1
    )


ROW_SCRATCH = dict(
    xr=((2, 128, 256), BF),
    xg=((2, 4, 128, 256), BF),
    bs=((2, 2, 8, 128), F32),
    bo=((2, 8, 128), F32),
    bq=((2, 16, 128), BF),
    brecv=((4, 4, 16, 128), BF),
    bx=((16, 128, 256), BF),
    wrow=((256, 1024), BF),
)
ROW_SEMS = ["m0", "m1", "g0", "g1", "bc", "b0", "b2", "b3"]


def row_part(r):
    row, col, xy, zc = where_am_i()
    m, e = in_quad()
    msa, xr, xg = r["msa"], r["xr"], r["xg"]
    zn = norm(r["pairs"][...].astype(F32)).astype(BF).reshape(512, 128)
    bias_t = nt(r["pair_bias"][...], zn)
    for k in range(4):
        r["bs"][k // 2, k % 2] = bias_t[:, 128 * k : 128 * k + 128]
    core = lax.rem(zc, 2)
    barrier_wait()
    sc = Swap(r, "bc")
    sc.put(r["bs"].at[1 - core], r["bo"], row + 1 - 2 * core, col)
    sc.got(r["bo"])
    ours, theirs = r["bs"][core], r["bo"][...]
    r["bq"][...] = jnp.concatenate(
        [jnp.where(core == 0, ours, theirs), jnp.where(core == 0, theirs, ours)], axis=1
    ).astype(BF)
    s0 = Swap(r, "b0")
    slot = r["brecv"].at[zc // 2, col]
    for d in range(1, 8):
        for k in range(2):
            s0.put(r["bq"].at[k], slot, *place(xy, lax.rem(m + d, 8), 2 * core + k))
    for k in range(2):
        s0.either(r["bq"].at[k], slot, e != 2 * core + k, *place(xy, m, 2 * core + k))
    direct = [Swap(r, "m0"), Swap(r, "m1")]
    away = jnp.logical_or(zc != m, col != e)
    for s in range(2):
        direct[s].either(msa.at[s], xr.at[s], away, *place(xy, zc, col))
    r["wrow"][...] = by_kind(r["row_w"])
    pz = perm((2, 4, 2, 2, 4), (3, 0, 4, 1, 2))
    shared = [Swap(r, "g0"), Swap(r, "g1")]

    def share(s):
        direct[s].got(xr.at[s])
        xg[s, e] = norm(xr[s].astype(F32)).astype(BF)
        shared[s].gather("quad", xg.at[s])

    s0.got(r["brecv"])
    b = r["brecv"]
    lo = jnp.concatenate([b[:, 0], b[:, 1]], axis=2).reshape(64, 256)
    hi = jnp.concatenate([b[:, 2], b[:, 3]], axis=2).reshape(64, 256)
    rows = jnp.concatenate([lo, hi], axis=0)
    r["bx"][xy] = nn(pz, rows).astype(BF)
    s2 = [Swap(r, "b2"), Swap(r, "b3")]
    for k in range(2):
        s2[k].gather("xy", r["bx"].at[:, pl.ds(64 * k, 64)])
    share(0)
    share(1)
    if "prep" in r:
        r["prep"]()
    ready = []
    for s in range(2):
        shared[s].got(xg.at[s, pl.ds(0, 3)])
        ready.append(project(xg[s].reshape(512, 256), xg[s, e], r["wrow"]))
    cache = {}
    to_zc = perm((16, 8), (1, 0))

    def bias(h):
        if h not in cache:
            pair = h // 2 * 2
            parts = []
            for jh in range(2):
                at = (h // 4 * 8 + jh * 4 + pair % 4) * 8
                parts.append(r["bx"][:, at : at + 16, :].astype(F32))
            for k in range(2):
                cache[pair + k] = jnp.concatenate(
                    [p[:, 8 * k : 8 * k + 8].reshape(128, 256) for p in parts], axis=1
                )
        return cache[h]

    totals = []
    for part in range(2):
        s2[part].got(r["bx"].at[pl.ds(0, 15), pl.ds(64 * part, 64)])
        for s in range(2):
            q, k, v, gate = ready[s]
            cache.clear()
            mixed = attend(q, k, v, range(4 * part, 4 * part + 4), bias)
            if part == 0:
                totals.append(mixed)
                continue
            gated = (sig(gate) * (totals[s] + mixed)).astype(BF)
            m1 = (xr[s].astype(F32) + nn(gated, r["row_out"][...])).astype(BF)
            r["cs1"][:, 16 * s : 16 * s + 16] = nn(to_zc, m1).astype(BF).reshape(8, 16, 256)
            rows = pl.ds(16 * s, 16)
            Swap(r, "c1" + "ab"[s]).back(r["cs1"].at[:, rows], r["cr1"].at[:, rows])
    def row_sent():
        for s in range(2):
            shared[s].sent(xg.at[s, pl.ds(0, 3)])

            @pl.when(away)
            def _():
                direct[s].sent(msa.at[s])

        s0.sent(r["brecv"].at[pl.ds(0, 3)])
        s0.sent(r["brecv"].at[0, pl.ds(0, 2)])
        for k in range(2):

            @pl.when(e != 2 * core + k)
            def _():
                s0.sent(r["bq"].at[k])

        sc.sent(r["bo"])
        for k in range(2):
            s2[k].sent(r["bx"].at[pl.ds(0, 15), pl.ds(64 * k, 64)])

    return row_sent


COL_SCRATCH = dict(
    cs1=((8, 32, 256), BF),
    cr1=((8, 32, 256), BF),
    cs2=((16, 16, 256), BF),
    cr2=((16, 16, 256), BF),
    ds1=((16, 16, 256), BF),
    dr1=((16, 16, 256), BF),
    ds2=((8, 32, 256), BF),
    dr2=((8, 32, 256), BF),
    lg=((4, 32, 256), BF),
    rz=((8, 32, 256), BF),
    rx=((16, 256, 256), BF),
    wcol=((256, 1024), BF),
    bd=((32, 128, 512), BF),
    at=((32, 256, 512), BF),
)
COL_SEMS = ["c1a", "c1b", "c2", "d1", "d2", "lg", "rz", "rx", "rc"]


def col_prep(r):
    r["wcol"][...] = by_kind(r["col_w"])
    by_u = nn(perm((32, 32), (1, 0)), r["outer_out"][...]).astype(BF).reshape(32, 32, 128)
    r["bd"][...] = jnp.zeros((32, 128, 512), BF)
    for i in range(4):
        r["bd"][:, 32 * i : 32 * i + 32, 128 * i : 128 * i + 128] = by_u


def col_part(r):
    row, col, xy, zc = where_am_i()
    core = lax.rem(zc, 2)
    to_xy = perm((8, 2, 16), (2, 0, 1))
    c1 = [Swap(r, "c1a"), Swap(r, "c1b")]
    for k in range(2):
        c1[k].got(r["cr1"].at[:, pl.ds(16 * k, 16)])
    r["cs2"][...] = nn(to_xy, r["cr1"][...].reshape(256, 256)).astype(BF).reshape(16, 16, 256)
    c2 = Swap(r, "c2")
    c2.exchange("xy", r["cs2"], r["cr2"])
    c2.got(r["cr2"])
    lines = r["cr2"][...].reshape(256, 256).astype(F32)
    x = norm(lines).astype(BF)
    q, k, v, gate = project(x, x, r["wcol"])
    gated = (sig(gate) * attend(q, k, v, range(HEADS), None)).astype(BF)
    m2 = lines + nn(gated, r["col_out"][...])
    x = norm(m2).astype(BF)
    ab = nt(r["maps"][...], x).astype(BF)
    r["lg"][col] = ab[0:32]
    r["rz"][zc] = ab[32:64]
    rz = Swap(r, "rz")
    rz.gather("zc", r["rz"])
    r["ds1"][...] = m2.astype(BF).reshape(16, 16, 256)
    to_u = perm((8, 32), (1, 0))
    lg = Swap(r, "lg")
    rz.got(r["rz"].at[pl.ds(0, 7)])
    lg.gather("col", r["lg"])
    right = nn(to_u, r["rz"][...].reshape(256, 256)).astype(BF)
    rx = r["rx"]
    for k in range(2):

        @pl.when(core == k)
        def _():
            rx[xy, 128 * k : 128 * k + 128] = right[128 * k : 128 * k + 128]

    half = pl.ds(pl.multiple_of(core * 128, 128), 128)
    other = pl.ds(pl.multiple_of(128 - core * 128, 128), 128)
    rxs = Swap(r, "rx")
    for g, prow, pcol in rxs.peers("xy"):
        rxs.put(rx.at[xy, half], rx.at[xy, half], prow, pcol)
    lg.got(r["lg"].at[pl.ds(0, 3)])
    left = r["lg"][...].reshape(128, 256).T
    for u in range(32):
        r["at"][u] = nn(left, r["bd"][u]).astype(BF)
    rxs.got(rx.at[pl.ds(0, 15), pl.ds(0, 128)])
    rc = Swap(r, "rc")
    rc.put(rx.at[:, half], rx.at[:, half], row + 1 - 2 * core, col)
    def add(base, acc):
        for up in range(8):
            at = pl.multiple_of(base * 8 + up * 16, 16)
            block = rx[:, pl.ds(at, 16), :].astype(F32)
            for k in range(2):
                acc = acc + nn(block[:, 8 * k : 8 * k + 8].reshape(128, 256).astype(BF), r["at"][base + 2 * up + k])
        return acc

    acc = add(core * 16, jnp.zeros((128, 512), F32))
    rc.got(rx.at[:, other])
    acc = add(16 - core * 16, acc)
    for i in range(4):
        r["z1"][i] = r["pairs"][i].astype(F32) + acc[:, 128 * i : 128 * i + 128] * (1.0 / 256.0)
    d1, d2 = Swap(r, "d1"), Swap(r, "d2")

    def plane():
        d1.exchange("xy", r["ds1"], r["dr1"])

    def line():
        d1.got(r["dr1"])
        rows = nn(perm((16, 8, 2), (1, 2, 0)), r["dr1"][...].reshape(256, 256))
        r["ds2"][...] = rows.astype(BF).reshape(8, 32, 256)
        d2.exchange("zc", r["ds2"], r["dr2"])

    def finish():
        d2.got(r["dr2"])
        rows = nn(perm((8, 2, 16), (1, 2, 0)), r["dr2"][...].reshape(256, 256))
        r["msa_out"][...] = rows.astype(BF).reshape(2, 128, 256)

    r["later"] = [plane, line, finish]

    def col_sent():
        for k in range(2):
            c1[k].sent8(r["cs1"].at[:, pl.ds(16 * k, 16)])
        c2.sent(r["cs2"].at[pl.ds(0, 15)])
        d1.sent(r["ds1"].at[pl.ds(0, 15)])
        d2.sent(r["ds2"].at[pl.ds(0, 7)])
        lg.sent(r["lg"].at[pl.ds(0, 3)])
        rz.sent(r["rz"].at[pl.ds(0, 7)])
        rxs.sent(rx.at[pl.ds(0, 15), pl.ds(0, 128)])
        rc.sent(rx.at[:, half])

    return col_sent


def tri_scratch(t, outgoing):
    return {
        t + "f": ((1024, 128), F32),
        t + "h": ((512, 128), F32),
        t + "s2": ((64, 16, 128), BF),
        t + "r2": ((16, 4, 16, 128), BF),
        t + "ps": ((4, 512, 128), BF),
        t + "pr": ((4, 512, 128), BF),
        t + "s3": ((8, 64, 128), BF),
        t + "r3": ((8, 64, 128), BF),
        t + "s4": ((16, 32, 128), BF),
        t + "r4": ((16, 32, 128), BF),
        t + "gate": ((512, 128), F32),
        t + "wg": ((256, 128), BF),
        t + "wv": ((256, 128), BF),
    }


def tri_sems(t):
    return [t + k for k in ("1", "2", "p0", "p1", "30", "31", "40", "41")]


def tri_prep(r, t):
    by_core = perm((16, 4, 2), (2, 0, 1))
    w = r[t + "_proj"]
    for k in range(2):
        rows = pl.ds(128 * k, 128)
        r[t + "wg"][rows] = nt(by_core, w[:, 256 * k : 256 * k + 128]).astype(BF)
        r[t + "wv"][rows] = nt(by_core, w[:, 256 * k + 128 : 256 * k + 256]).astype(BF)


def tri_part(r, t, src, dst, outgoing):
    row, col, xy, zc = where_am_i()
    m, e = in_quad()
    x = norm(r[src][...]).astype(BF).reshape(512, 128)
    both = sig(nt(r[t + "wg"][...], x)) * nt(r[t + "wv"][...], x)
    core = lax.rem(zc, 2)
    f, h, s2, r2 = (r[t + k] for k in ("f", "h", "s2", "r2"))
    for k in range(2):
        for q in range(4):
            f[pl.ds(4 * k + q, 128, stride=8), :] = both[128 * k : 128 * k + 128, 128 * q : 128 * q + 128]
    e1 = Swap(r, t + "1")
    theirs = f.at[pl.ds(pl.multiple_of(512 - core * 512, 512), 512)]
    e1.put(theirs, h, row + 1 - 2 * core, col)
    r[t + "gate"][...] = sig(nn(x, r[t + "_proj"][:, 512:640]))
    ours = f[pl.ds(pl.multiple_of(core * 512, 512), 512), :].reshape(64, 8, 128)
    e1.got(h)
    other = h[...].reshape(64, 8, 128)
    s2[...] = jnp.concatenate(
        [jnp.where(core == 0, ours, other), jnp.where(core == 0, other, ours)], axis=1
    ).astype(BF)
    e2 = Swap(r, t + "2")
    member, slot = (col, zc // 2) if outgoing else (zc // 2, col)
    e2.direct(s2, r2.at[xy, slot], member)
    if outgoing:
        r["later"][0]()
        to_left = perm((16, 4, 2, 2, 4), (3, 4, 1, 2, 0), 0, 512)
        to_right = perm((16, 4, 2, 2, 4), (3, 4, 0, 1, 2), 512, 512)
    else:
        r["later"][2]()
        to_both = perm((16, 4, 2, 2, 4), (3, 1, 0, 2, 4))
        natural = perm((16, 8), (1, 0))
    e2.got(r2)
    landed = r2[...].reshape(1024, 128)
    ps, pr = r[t + "ps"], r[t + "pr"]
    s3, r3, s4, r4 = (r[t + k] for k in ("s3", "r3", "s4", "r4"))
    if outgoing:
        left = nn(to_left, landed).astype(BF)
        right = nn(to_right, landed).astype(BF)
    else:
        rows = nn(to_both, landed).astype(BF)
        left = jnp.concatenate([nt(natural, rows[128 * c : 128 * c + 128]).astype(BF) for c in range(4)], axis=0)
        right = rows[512:1024]
    right = [right[128 * c : 128 * c + 128] for c in range(4)]
    ep = [Swap(r, t + "p0"), Swap(r, t + "p1")]
    e3 = [Swap(r, t + "30"), Swap(r, t + "31")]
    e4 = [Swap(r, t + "40"), Swap(r, t + "41")]
    for half in range(2):
        rows = pl.ds(256 * half, 256)
        part = left[256 * half : 256 * half + 256]
        for c in range(4):
            ps[c, rows] = (nt if outgoing else nn)(part, right[c]).astype(BF)
        ep[half].exchange("quad", ps.at[:, rows], pr.at[:, rows])
    by_plane = perm((8, 2, 16), (2, 1, 0))
    for half in range(2):
        rows = pl.ds(256 * half, 256)
        ep[half].got(pr.at[:, rows])
        mix = (pr[0, rows].astype(F32) + pr[1, rows].astype(F32)) + (pr[2, rows].astype(F32) + pr[3, rows].astype(F32))
        mix = mix.astype(BF).reshape(2, 8, 16, 128)
        for q in range(2):
            s3[:, 32 * half + 16 * q : 32 * half + 16 * q + 16] = mix[q]
        rows = pl.ds(32 * half, 32)
        e3[half].back(s3.at[:, rows], r3.at[:, rows])
    for half in range(2):
        rows = pl.ds(32 * half, 32)
        e3[half].got(r3.at[:, rows])
        rows4 = pl.ds(16 * half, 16)
        s4[:, rows4] = nn(by_plane, r3[:, rows].reshape(256, 128)).astype(BF).reshape(16, 16, 128)
        e4[half].exchange("xy", s4.at[:, rows4], r4.at[:, rows4])
    if outgoing:
        r["later"][1]()
    for half in range(2):
        rows4 = pl.ds(16 * half, 16)
        e4[half].got(r4.at[:, rows4])
        got = r4[:, rows4].astype(F32)
        for k in range(2):
            q = 2 * half + k
            step = tn(norm(got[:, 8 * k : 8 * k + 8].reshape(128, 128), 0).astype(BF), r[t + "_out"][...])
            r[dst][q] = r[src][q] + r[t + "gate"][128 * q : 128 * q + 128] * step
    def tri_sent():
        e1.sent(h)
        e2.sent64(s2, member)
        for half in range(2):
            ep[half].sent(ps.at[pl.ds(0, 3), pl.ds(0, 256)])
            e3[half].sent8(s3.at[:, pl.ds(32 * half, 32)])
            e4[half].sent(s4.at[pl.ds(0, 15), pl.ds(0, 16)])

    return tri_sent


SHAPES = dict(
    z1=((4, 128, 128), F32),
    z2=((4, 128, 128), F32),
    z3=((4, 128, 128), F32),
    msa_out=((2, 128, 256), BF),
)


PARTS = dict(
    row=dict(ins=["msa", "pairs", "row_w", "row_out", "pair_bias"], outs=[], scratch=ROW_SCRATCH, sems=ROW_SEMS),
    col=dict(
        ins=["pairs", "col_w", "col_out", "maps", "outer_out"],
        outs=["msa_out", "z1"],
        scratch=COL_SCRATCH,
        sems=COL_SEMS,
    ),
    out=dict(ins=["z1", "o_proj", "o_out"], outs=["z2"], scratch=tri_scratch("o", True), sems=tri_sems("o")),
    inc=dict(ins=["z2", "i_proj", "i_out"], outs=["z3"], scratch=tri_scratch("i", False), sems=tri_sems("i")),
)


def run_parts(parts, arrays, results, number):
    ins, made, scratch, sems = [], [], {}, []
    for p in parts:
        spec = PARTS[p]
        ins += [n for n in spec["ins"] if n not in ins and n not in made]
        made += spec["outs"]
        scratch.update(spec["scratch"])
        sems += spec["sems"]
    outs = [n for n in made if n in results]
    inner = {n: SHAPES[n] for n in made if n not in results}
    scratch = {**scratch, **inner}
    sem_names = [s + e for s in sems for e in ("_s", "_r")]

    def body(*refs):
        r = dict(zip(ins + outs + list(scratch) + sem_names, refs))
        barrier_signal()

        def prep():
            if "col" in parts:
                col_prep(r)
            if "out" in parts:
                tri_prep(r, "o")
            if "inc" in parts:
                tri_prep(r, "i")

        if parts[0] == "row":
            r["prep"] = prep
        else:
            prep()
            barrier_wait()
        waits = []
        for p in parts:
            if p == "row":
                waits.append(row_part(r))
            elif p == "col":
                waits.append(col_part(r))
            elif p == "out":
                waits.append(tri_part(r, "o", "z1", "z2", True))
            else:
                waits.append(tri_part(r, "i", "z2", "z3", False))
        for wait in waits:
            wait()

    vm = pl.BlockSpec(memory_space=pltpu.VMEM)
    got = pl.pallas_call(
        body,
        out_shape=[jax.ShapeDtypeStruct(*SHAPES[n]) for n in outs],
        in_specs=[vm] * len(ins),
        out_specs=[vm] * len(outs),
        scratch_shapes=[pltpu.VMEM(*scratch[n]) for n in scratch] + [pltpu.SemaphoreType.DMA] * len(sem_names),
        compiler_params=pltpu.CompilerParams(
            collective_id=number, has_side_effects=True, vmem_limit_bytes=56 * 1024 * 1024
        ),
        name="_".join(parts),
    )(*[arrays[n] for n in ins])
    arrays.update(zip(outs, got))


GROUPS = [["row", "col", "out", "inc"]]


def shards(*args, groups=None, results=("msa_out", "z3")):
    groups = groups or GROUPS
    names = ["msa", "pairs", "row_w", "row_out", "pair_bias", "col_w", "col_out", "maps", "outer_out"]
    names += ["o_proj", "o_out", "i_proj", "i_out"]
    arrays = dict(zip(names, args))
    msa_shape, pair_shape = arrays["msa"].shape, arrays["pairs"].shape
    arrays["pair_bias"], arrays["maps"] = arrays["pair_bias"].T, arrays["maps"].T
    arrays["msa"] = arrays["msa"].reshape(2, 128, 256)
    arrays["pairs"] = arrays["pairs"].reshape(4, 128, 128)
    for number, group in enumerate(groups):
        later = [n for g in groups[number + 1 :] for p in g for n in PARTS[p]["ins"]]
        run_parts(group, arrays, set(results) | set(later), number)
    outs = dict(
        msa_out=lambda a: a.reshape(msa_shape),
        z3=lambda a: a.reshape(pair_shape),
    )
    return tuple(outs.get(n, lambda a: a)(arrays[n]) for n in results)


def solution(mesh):
    return jax.shard_map(
        shards,
        mesh=mesh,
        in_specs=(P("row", None, "col", None, None),) * 2 + (P(),) * 11,
        out_specs=(P("row", None, "col", None, None),) * 2,
        check_vma=False,
    )
```

```python
import functools
import math

import jax
import jax.numpy as jnp
from jax import lax
from jax.experimental import pallas as pl
from jax.experimental.pallas import tpu as pltpu
from jax.sharding import PartitionSpec as P

MESH = pl.DeviceIdType.MESH
BF = jnp.bfloat16
F32 = jnp.float32
EPS = 1e-05
HEADS = 8
NXY = 16
NZC = 8
NCOL = 4


def nn(a, b):
    return lax.dot_general(a, b, (((1,), (0,)), ((), ())), preferred_element_type=F32)


def nt(a, b):
    return lax.dot_general(a, b, (((1,), (1,)), ((), ())), preferred_element_type=F32)


def tn(a, b):
    return lax.dot_general(a, b, (((0,), (0,)), ((), ())), preferred_element_type=F32)


def norm(x, axis=-1):
    c = x - jnp.mean(x, axis=axis, keepdims=True)
    v = jnp.mean(c * c, axis=axis, keepdims=True)
    return c * lax.rsqrt(v + EPS)


def sig(x):
    return 1.0 / (1.0 + jnp.exp(-x))


def perm(sizes, order, first=0, count=None):
    n = math.prod(sizes)
    count = count or n
    strides = [math.prod(sizes[k + 1 :]) for k in range(len(sizes))]
    out = lax.broadcasted_iota(jnp.int32, (count, 1), 0) + first
    src = jnp.zeros((count, 1), jnp.int32)
    rest = out
    for axis in reversed(order):
        src = src + (rest & (sizes[axis] - 1)) * strides[axis]
        rest = lax.shift_right_logical(rest, int(math.log2(sizes[axis])))
    inp = lax.broadcasted_iota(jnp.int32, (count, n), 1)
    return jnp.where(src == inp, 1.0, 0.0).astype(BF)


def where_am_i():
    row, col = lax.axis_index("row"), lax.axis_index("col")
    return row, col, row // NZC, row % NZC


def in_quad():
    row, col, xy, zc = where_am_i()
    return 2 * col + zc // 4, zc % 4


def place(xy, m, e):
    return xy * NZC + m % 2 * 4 + e, m // 2


class Swap:
    def __init__(self, r, name):
        self.send, self.recv = r[name + "_s"], r[name + "_r"]
        self.row, self.col, self.xy, self.zc = where_am_i()
        self.m, self.e = in_quad()

    def put(self, src, dst, row, col):
        pltpu.make_async_remote_copy(
            src_ref=src,
            dst_ref=dst,
            send_sem=self.send,
            recv_sem=self.recv,
            device_id=(row, col),
            device_id_type=MESH,
        ).start()

    def keep(self, src, dst):
        pltpu.make_async_copy(src, dst, self.recv).start()

    def peers(self, kind):
        if kind == "xy":
            for d in range(1, NXY):
                g = lax.rem(self.xy + d, NXY)
                yield g, g * NZC + self.zc, self.col
        elif kind == "zc":
            for d in range(1, NZC):
                g = lax.rem(self.zc + d, NZC)
                yield g, self.xy * NZC + g, self.col
        elif kind == "quad":
            for d in range(1, 4):
                g = lax.rem(self.e + d, 4)
                yield g, *place(self.xy, self.m, g)
        else:
            for d in range(1, NCOL):
                g = lax.rem(self.col + d, NCOL)
                yield g, self.row, g

    def mine(self, kind):
        return {"xy": self.xy, "zc": self.zc, "col": self.col, "quad": self.e}[kind]

    def exchange(self, kind, src, dst):
        me = self.mine(kind)
        for g, row, col in self.peers(kind):
            self.put(src.at[g], dst.at[me], row, col)
        self.keep(src.at[me], dst.at[me])

    def gather(self, kind, buf):
        me = self.mine(kind)
        for g, row, col in self.peers(kind):
            self.put(buf.at[me], buf.at[me], row, col)

    def either(self, src, dst, away, row, col):
        @pl.when(away)
        def _():
            self.put(src, dst, row, col)

        @pl.when(jnp.logical_not(away))
        def _():
            self.keep(src, dst)

    def direct(self, src, slot, member):
        core = lax.rem(self.zc, 2)
        here = self.xy * 4 + self.m // 2
        for d in range(1, 64):
            g = lax.rem(here + d, 64)
            self.put(src.at[g], slot, *place(g // 4, g % 4 * 2 + core, member))
        row, col = place(self.xy, self.m // 2 * 2 + core, member)
        self.either(src.at[here], slot, self.elsewhere(member), row, col)

    def elsewhere(self, member):
        return jnp.logical_or(lax.rem(self.m, 2) != lax.rem(self.zc, 2), self.e != member)

    def sent64(self, src, member):
        self.sent(src.at[pl.ds(0, 63)])

        @pl.when(self.elsewhere(member))
        def _():
            self.sent(src.at[0])

    def back(self, src, dst):
        for d in range(1, 8):
            g = lax.rem(self.zc + d, 8)
            self.put(src.at[g], dst.at[self.m], self.xy * NZC + g, self.e)
        self.either(src.at[self.zc], dst.at[self.m], self.e != self.col, self.row, self.e)

    def sent8(self, src):
        self.sent(src.at[pl.ds(0, 7)])

        @pl.when(self.e != self.col)
        def _():
            self.sent(src.at[0])

    def got(self, ref):
        pltpu.make_async_copy(ref, ref, self.recv).wait()

    def sent(self, ref):
        pltpu.make_async_copy(ref, ref, self.send).wait()


def barrier_signal():
    row, col, xy, zc = where_am_i()
    m, e = in_quad()
    sem = pltpu.get_barrier_semaphore()

    def hail(r, c):
        pl.semaphore_signal(sem, inc=1, device_id=(r, c), device_id_type=MESH)

    for d in range(1, NXY):
        hail(lax.rem(xy + d, NXY) * NZC + zc, col)
    for d in range(1, 32):
        t = lax.rem(m * 4 + e + d, 32)
        hail(*place(xy, t // 4, t % 4))


def barrier_wait():
    pl.semaphore_wait(pltpu.get_barrier_semaphore(), NXY + 32 - 2)


def project(keys, own, weights):
    q = nn(own, weights[:, 0:256]).astype(BF)
    k = nn(keys, weights[:, 256:512]).astype(BF)
    v = nn(keys, weights[:, 512:768]).astype(BF)
    gate = nn(own, weights[:, 768:1024]).astype(BF).astype(F32)
    return q, k, jnp.concatenate([v, jnp.ones((keys.shape[0], 128), BF)], axis=1), gate


def attend(q, k, v, heads, bias):
    head = lax.broadcasted_iota(jnp.int32, q.shape, 1) // 32
    total = jnp.zeros(q.shape, F32)
    for h in heads:
        scores = nt(jnp.where(head == h, q, jnp.zeros_like(q)), k) * (1.0 / math.sqrt(32.0))
        if bias is not None:
            scores = scores + bias(h)
        top = jnp.max(scores, axis=-1, keepdims=True)
        p = jnp.exp(scores - top).astype(BF)
        mixed = nn(p, v)
        inv = 1.0 / mixed[:, 256:384]
        mixed = mixed[:, 0:256] * jnp.concatenate([inv, inv], axis=1)
        total = total + jnp.where(head == h, mixed, 0.0)
    return total


def by_kind(ref):
    w = ref[...]
    return jnp.concatenate(
        [w[:, 128 * h + 32 * k : 128 * h + 32 * k + 32] for k in range(4) for h in range(HEADS)], axis=1
    )


ROW_SCRATCH = dict(
    xr=((2, 128, 256), BF),
    xg=((2, 4, 128, 256), BF),
    bs=((2, 2, 8, 128), F32),
    bo=((2, 8, 128), F32),
    bq=((2, 16, 128), BF),
    brecv=((4, 4, 16, 128), BF),
    bx=((16, 128, 256), BF),
    wrow=((256, 1024), BF),
)
ROW_SEMS = ["m0", "m1", "g0", "g1", "bc", "b0", "h0", "h1", "h2", "h3"]


def row_part(r):
    row, col, xy, zc = where_am_i()
    m, e = in_quad()
    msa, xr, xg = r["msa"], r["xr"], r["xg"]
    zn = norm(r["pairs"][...].astype(F32)).astype(BF).reshape(512, 128)
    bias_t = nt(r["pair_bias"][...], zn)
    for k in range(4):
        r["bs"][k // 2, k % 2] = bias_t[:, 128 * k : 128 * k + 128]
    core = lax.rem(zc, 2)
    barrier_wait()
    sc = Swap(r, "bc")
    sc.put(r["bs"].at[1 - core], r["bo"], row + 1 - 2 * core, col)
    sc.got(r["bo"])
    ours, theirs = r["bs"][core], r["bo"][...]
    r["bq"][...] = jnp.concatenate(
        [jnp.where(core == 0, ours, theirs), jnp.where(core == 0, theirs, ours)], axis=1
    ).astype(BF)
    s0 = Swap(r, "b0")
    slot = r["brecv"].at[zc // 2, col]
    for d in range(1, 8):
        for k in range(2):
            s0.put(r["bq"].at[k], slot, *place(xy, lax.rem(m + d, 8), 2 * core + k))
    for k in range(2):
        s0.either(r["bq"].at[k], slot, e != 2 * core + k, *place(xy, m, 2 * core + k))
    direct = [Swap(r, "m0"), Swap(r, "m1")]
    away = jnp.logical_or(zc != m, col != e)
    for s in range(2):
        direct[s].either(msa.at[s], xr.at[s], away, *place(xy, zc, col))
    r["wrow"][...] = by_kind(r["row_w"])
    pz = perm((2, 4, 2, 4, 2), (3, 0, 4, 1, 2))
    shared = [Swap(r, "g0"), Swap(r, "g1")]

    def share(s):
        direct[s].got(xr.at[s])
        xg[s, e] = norm(xr[s].astype(F32)).astype(BF)
        shared[s].gather("quad", xg.at[s])

    s0.got(r["brecv"])
    b = r["brecv"]
    lo = jnp.concatenate([b[:, 0], b[:, 1]], axis=2).reshape(64, 256)
    hi = jnp.concatenate([b[:, 2], b[:, 3]], axis=2).reshape(64, 256)
    rows = jnp.concatenate([lo, hi], axis=0)
    r["bx"][xy] = nn(pz, rows).astype(BF)
    s2 = [Swap(r, "h%d" % k) for k in range(4)]
    for k in range(4):
        s2[k].gather("xy", r["bx"].at[:, pl.ds(32 * k, 32)])
    share(0)
    share(1)
    if "prep" in r:
        r["prep"]()
    ready = []
    for s in range(2):
        shared[s].got(xg.at[s, pl.ds(0, 3)])
        ready.append(project(xg[s].reshape(512, 256), xg[s, e], r["wrow"]))
    cache = {}
    to_zc = perm((16, 8), (1, 0))

    def bias(h):
        if h not in cache:
            pair = h // 2 * 2
            parts = []
            for jh in range(2):
                at = (h // 2 * 4 + jh * 2) * 8
                parts.append(r["bx"][:, at : at + 16, :].astype(F32))
            for k in range(2):
                cache[pair + k] = jnp.concatenate(
                    [p[:, 8 * k : 8 * k + 8].reshape(128, 256) for p in parts], axis=1
                )
        return cache[h]

    totals = [0.0, 0.0]
    for part in range(4):
        s2[part].got(r["bx"].at[pl.ds(0, 15), pl.ds(32 * part, 32)])
        for s in range(2):
            q, k, v, gate = ready[s]
            cache.clear()
            mixed = attend(q, k, v, range(2 * part, 2 * part + 2), bias)
            totals[s] = totals[s] + mixed
            if part < 3:
                continue
            gated = (sig(gate) * totals[s]).astype(BF)
            m1 = (xr[s].astype(F32) + nn(gated, r["row_out"][...])).astype(BF)
            r["cs1"][:, 16 * s : 16 * s + 16] = nn(to_zc, m1).astype(BF).reshape(8, 16, 256)
            rows = pl.ds(16 * s, 16)
            Swap(r, "c1" + "ab"[s]).back(r["cs1"].at[:, rows], r["cr1"].at[:, rows])
    def row_sent():
        for s in range(2):
            shared[s].sent(xg.at[s, pl.ds(0, 3)])

            @pl.when(away)
            def _():
                direct[s].sent(msa.at[s])

        s0.sent(r["brecv"].at[pl.ds(0, 3)])
        s0.sent(r["brecv"].at[0, pl.ds(0, 2)])
        for k in range(2):

            @pl.when(e != 2 * core + k)
            def _():
                s0.sent(r["bq"].at[k])

        sc.sent(r["bo"])
        for k in range(4):
            s2[k].sent(r["bx"].at[pl.ds(0, 15), pl.ds(32 * k, 32)])

    return row_sent


COL_SCRATCH = dict(
    cs1=((8, 32, 256), BF),
    cr1=((8, 32, 256), BF),
    cs2=((16, 16, 256), BF),
    cr2=((16, 16, 256), BF),
    ds1=((16, 16, 256), BF),
    dr1=((16, 16, 256), BF),
    ds2=((8, 32, 256), BF),
    dr2=((8, 32, 256), BF),
    lg=((4, 32, 256), BF),
    rz=((8, 32, 256), BF),
    rx=((16, 256, 256), BF),
    wcol=((256, 1024), BF),
    bd=((32, 128, 512), BF),
    at=((32, 256, 512), BF),
)
COL_SEMS = ["c1a", "c1b", "c2", "d1", "d2", "lg", "rz", "rx", "rc"]


def col_prep(r):
    r["wcol"][...] = by_kind(r["col_w"])
    by_u = nn(perm((32, 32), (1, 0)), r["outer_out"][...]).astype(BF).reshape(32, 32, 128)
    r["bd"][...] = jnp.zeros((32, 128, 512), BF)
    for i in range(4):
        r["bd"][:, 32 * i : 32 * i + 32, 128 * i : 128 * i + 128] = by_u


def col_part(r):
    row, col, xy, zc = where_am_i()
    core = lax.rem(zc, 2)
    to_xy = perm((8, 2, 16), (2, 0, 1))
    c1 = [Swap(r, "c1a"), Swap(r, "c1b")]
    for k in range(2):
        c1[k].got(r["cr1"].at[:, pl.ds(16 * k, 16)])
    r["cs2"][...] = nn(to_xy, r["cr1"][...].reshape(256, 256)).astype(BF).reshape(16, 16, 256)
    c2 = Swap(r, "c2")
    c2.exchange("xy", r["cs2"], r["cr2"])
    c2.got(r["cr2"])
    lines = r["cr2"][...].reshape(256, 256).astype(F32)
    x = norm(lines).astype(BF)
    q, k, v, gate = project(x, x, r["wcol"])
    gated = (sig(gate) * attend(q, k, v, range(HEADS), None)).astype(BF)
    m2 = lines + nn(gated, r["col_out"][...])
    x = norm(m2).astype(BF)
    ab = nt(r["maps"][...], x).astype(BF)
    r["lg"][col] = ab[0:32]
    r["rz"][zc] = ab[32:64]
    rz = Swap(r, "rz")
    rz.gather("zc", r["rz"])
    r["ds1"][...] = m2.astype(BF).reshape(16, 16, 256)
    to_u = perm((8, 32), (1, 0))
    lg = Swap(r, "lg")
    rz.got(r["rz"].at[pl.ds(0, 7)])
    lg.gather("col", r["lg"])
    right = nn(to_u, r["rz"][...].reshape(256, 256)).astype(BF)
    rx = r["rx"]
    for k in range(2):

        @pl.when(core == k)
        def _():
            rx[xy, 128 * k : 128 * k + 128] = right[128 * k : 128 * k + 128]

    half = pl.ds(pl.multiple_of(core * 128, 128), 128)
    other = pl.ds(pl.multiple_of(128 - core * 128, 128), 128)
    rxs = Swap(r, "rx")
    for g, prow, pcol in rxs.peers("xy"):
        rxs.put(rx.at[xy, half], rx.at[xy, half], prow, pcol)
    lg.got(r["lg"].at[pl.ds(0, 3)])
    left = r["lg"][...].reshape(128, 256).T
    for u in range(32):
        r["at"][u] = nn(left, r["bd"][u]).astype(BF)
    rxs.got(rx.at[pl.ds(0, 15), pl.ds(0, 128)])
    rc = Swap(r, "rc")
    rc.put(rx.at[:, half], rx.at[:, half], row + 1 - 2 * core, col)
    def add(base, acc):
        for up in range(8):
            at = pl.multiple_of(base * 8 + up * 16, 16)
            block = rx[:, pl.ds(at, 16), :].astype(F32)
            for k in range(2):
                acc = acc + nn(block[:, 8 * k : 8 * k + 8].reshape(128, 256).astype(BF), r["at"][base + 2 * up + k])
        return acc

    acc = add(core * 16, jnp.zeros((128, 512), F32))
    rc.got(rx.at[:, other])
    acc = add(16 - core * 16, acc)
    for i in range(4):
        r["z1"][i] = r["pairs"][i].astype(F32) + acc[:, 128 * i : 128 * i + 128] * (1.0 / 256.0)
    d1, d2 = Swap(r, "d1"), Swap(r, "d2")

    def plane():
        d1.exchange("xy", r["ds1"], r["dr1"])

    def line():
        d1.got(r["dr1"])
        rows = nn(perm((16, 8, 2), (1, 2, 0)), r["dr1"][...].reshape(256, 256))
        r["ds2"][...] = rows.astype(BF).reshape(8, 32, 256)
        d2.exchange("zc", r["ds2"], r["dr2"])

    def finish():
        d2.got(r["dr2"])
        rows = nn(perm((8, 2, 16), (1, 2, 0)), r["dr2"][...].reshape(256, 256))
        r["msa_out"][...] = rows.astype(BF).reshape(2, 128, 256)

    r["later"] = [plane, line, finish]

    def col_sent():
        for k in range(2):
            c1[k].sent8(r["cs1"].at[:, pl.ds(16 * k, 16)])
        c2.sent(r["cs2"].at[pl.ds(0, 15)])
        d1.sent(r["ds1"].at[pl.ds(0, 15)])
        d2.sent(r["ds2"].at[pl.ds(0, 7)])
        lg.sent(r["lg"].at[pl.ds(0, 3)])
        rz.sent(r["rz"].at[pl.ds(0, 7)])
        rxs.sent(rx.at[pl.ds(0, 15), pl.ds(0, 128)])
        rc.sent(rx.at[:, half])

    return col_sent


def tri_scratch(t, outgoing):
    return {
        t + "f": ((1024, 128), F32),
        t + "h": ((512, 128), F32),
        t + "s2": ((64, 16, 128), BF),
        t + "r2": ((16, 4, 16, 128), BF),
        t + "ps": ((4, 512, 128), BF),
        t + "pr": ((4, 512, 128), BF),
        t + "s3": ((8, 64, 128), BF),
        t + "r3": ((8, 64, 128), BF),
        t + "s4": ((16, 32, 128), BF),
        t + "r4": ((16, 32, 128), BF),
        t + "gate": ((512, 128), F32),
        t + "wg": ((256, 128), BF),
        t + "wv": ((256, 128), BF),
    }


def tri_sems(t):
    return [t + k for k in ("1", "2", "p0", "p1", "p2", "p3", "30", "31", "32", "33", "40", "41")]


def tri_prep(r, t):
    by_core = perm((16, 4, 2), (2, 0, 1))
    w = r[t + "_proj"]
    for k in range(2):
        rows = pl.ds(128 * k, 128)
        r[t + "wg"][rows] = nt(by_core, w[:, 256 * k : 256 * k + 128]).astype(BF)
        r[t + "wv"][rows] = nt(by_core, w[:, 256 * k + 128 : 256 * k + 256]).astype(BF)


def tri_part(r, t, src, dst, outgoing):
    row, col, xy, zc = where_am_i()
    m, e = in_quad()
    x = norm(r[src][...]).astype(BF).reshape(512, 128)
    both = sig(nt(r[t + "wg"][...], x)) * nt(r[t + "wv"][...], x)
    core = lax.rem(zc, 2)
    f, h, s2, r2 = (r[t + k] for k in ("f", "h", "s2", "r2"))
    for k in range(2):
        for q in range(4):
            f[pl.ds(4 * k + q, 128, stride=8), :] = both[128 * k : 128 * k + 128, 128 * q : 128 * q + 128]
    e1 = Swap(r, t + "1")
    theirs = f.at[pl.ds(pl.multiple_of(512 - core * 512, 512), 512)]
    e1.put(theirs, h, row + 1 - 2 * core, col)
    r[t + "gate"][...] = sig(nn(x, r[t + "_proj"][:, 512:640]))
    ours = f[pl.ds(pl.multiple_of(core * 512, 512), 512), :].reshape(64, 8, 128)
    e1.got(h)
    other = h[...].reshape(64, 8, 128)
    s2[...] = jnp.concatenate(
        [jnp.where(core == 0, ours, other), jnp.where(core == 0, other, ours)], axis=1
    ).astype(BF)
    e2 = Swap(r, t + "2")
    member, slot = (col, zc // 2) if outgoing else (zc // 2, col)
    e2.direct(s2, r2.at[xy, slot], member)
    if outgoing:
        r["later"][0]()
        to_left = perm((16, 4, 2, 2, 4), (3, 4, 1, 2, 0), 0, 512)
        to_right = perm((16, 4, 2, 2, 4), (3, 4, 0, 1, 2), 512, 512)
    else:
        r["later"][2]()
        to_both = perm((16, 4, 2, 2, 4), (3, 1, 0, 2, 4))
        natural = perm((16, 8), (1, 0))
    e2.got(r2)
    landed = r2[...].reshape(1024, 128)
    ps, pr = r[t + "ps"], r[t + "pr"]
    s3, r3, s4, r4 = (r[t + k] for k in ("s3", "r3", "s4", "r4"))
    if outgoing:
        left = nn(to_left, landed).astype(BF)
        right = nn(to_right, landed).astype(BF)
    else:
        rows = nn(to_both, landed).astype(BF)
        left = jnp.concatenate([nt(natural, rows[128 * c : 128 * c + 128]).astype(BF) for c in range(4)], axis=0)
        right = rows[512:1024]
    right = [right[128 * c : 128 * c + 128] for c in range(4)]
    ep = [Swap(r, t + "p%d" % q) for q in range(4)]
    e3 = [Swap(r, t + "3%d" % q) for q in range(4)]
    e4 = [Swap(r, t + "40"), Swap(r, t + "41")]
    for q in range(4):
        rows = pl.ds(128 * q, 128)
        for c in range(4):
            ps[c, rows] = (nt if outgoing else nn)(left[128 * q : 128 * q + 128], right[c]).astype(BF)
        ep[q].exchange("quad", ps.at[:, rows], pr.at[:, rows])
    by_plane = perm((8, 2, 16), (2, 1, 0))
    for q in range(4):
        rows = pl.ds(128 * q, 128)
        ep[q].got(pr.at[:, rows])
        mix = (pr[0, rows].astype(F32) + pr[1, rows].astype(F32)) + (pr[2, rows].astype(F32) + pr[3, rows].astype(F32))
        s3[:, 16 * q : 16 * q + 16] = mix.astype(BF).reshape(8, 16, 128)
        rows = pl.ds(16 * q, 16)
        e3[q].back(s3.at[:, rows], r3.at[:, rows])
    for half in range(2):
        rows = pl.ds(32 * half, 32)
        for q in range(2 * half, 2 * half + 2):
            e3[q].got(r3.at[:, pl.ds(16 * q, 16)])
        rows4 = pl.ds(16 * half, 16)
        s4[:, rows4] = nn(by_plane, r3[:, rows].reshape(256, 128)).astype(BF).reshape(16, 16, 128)
        e4[half].exchange("xy", s4.at[:, rows4], r4.at[:, rows4])
    if outgoing:
        r["later"][1]()
    for half in range(2):
        rows4 = pl.ds(16 * half, 16)
        e4[half].got(r4.at[:, rows4])
        got = r4[:, rows4].astype(F32)
        for k in range(2):
            q = 2 * half + k
            step = tn(norm(got[:, 8 * k : 8 * k + 8].reshape(128, 128), 0).astype(BF), r[t + "_out"][...])
            r[dst][q] = r[src][q] + r[t + "gate"][128 * q : 128 * q + 128] * step
    def tri_sent():
        e1.sent(h)
        e2.sent64(s2, member)
        for half in range(2):
            for q in range(2 * half, 2 * half + 2):
                ep[q].sent(ps.at[pl.ds(0, 3), pl.ds(0, 128)])
                e3[q].sent8(s3.at[:, pl.ds(16 * q, 16)])
            e4[half].sent(s4.at[pl.ds(0, 15), pl.ds(0, 16)])

    return tri_sent


SHAPES = dict(
    z1=((4, 128, 128), F32),
    z2=((4, 128, 128), F32),
    z3=((4, 128, 128), F32),
    msa_out=((2, 128, 256), BF),
)


PARTS = dict(
    row=dict(ins=["msa", "pairs", "row_w", "row_out", "pair_bias"], outs=[], scratch=ROW_SCRATCH, sems=ROW_SEMS),
    col=dict(
        ins=["pairs", "col_w", "col_out", "maps", "outer_out"],
        outs=["msa_out", "z1"],
        scratch=COL_SCRATCH,
        sems=COL_SEMS,
    ),
    out=dict(ins=["z1", "o_proj", "o_out"], outs=["z2"], scratch=tri_scratch("o", True), sems=tri_sems("o")),
    inc=dict(ins=["z2", "i_proj", "i_out"], outs=["z3"], scratch=tri_scratch("i", False), sems=tri_sems("i")),
)


def run_parts(parts, arrays, results, number):
    ins, made, scratch, sems = [], [], {}, []
    for p in parts:
        spec = PARTS[p]
        ins += [n for n in spec["ins"] if n not in ins and n not in made]
        made += spec["outs"]
        scratch.update(spec["scratch"])
        sems += spec["sems"]
    outs = [n for n in made if n in results]
    inner = {n: SHAPES[n] for n in made if n not in results}
    scratch = {**scratch, **inner}
    sem_names = [s + e for s in sems for e in ("_s", "_r")]

    def body(*refs):
        r = dict(zip(ins + outs + list(scratch) + sem_names, refs))
        barrier_signal()

        def prep():
            if "col" in parts:
                col_prep(r)
            if "out" in parts:
                tri_prep(r, "o")
            if "inc" in parts:
                tri_prep(r, "i")

        if parts[0] == "row":
            r["prep"] = prep
        else:
            prep()
            barrier_wait()
        waits = []
        for p in parts:
            if p == "row":
                waits.append(row_part(r))
            elif p == "col":
                waits.append(col_part(r))
            elif p == "out":
                waits.append(tri_part(r, "o", "z1", "z2", True))
            else:
                waits.append(tri_part(r, "i", "z2", "z3", False))
        for wait in waits:
            wait()

    vm = pl.BlockSpec(memory_space=pltpu.VMEM)
    got = pl.pallas_call(
        body,
        out_shape=[jax.ShapeDtypeStruct(*SHAPES[n]) for n in outs],
        in_specs=[vm] * len(ins),
        out_specs=[vm] * len(outs),
        scratch_shapes=[pltpu.VMEM(*scratch[n]) for n in scratch] + [pltpu.SemaphoreType.DMA] * len(sem_names),
        compiler_params=pltpu.CompilerParams(
            collective_id=number, has_side_effects=True, vmem_limit_bytes=56 * 1024 * 1024
        ),
        name="_".join(parts),
    )(*[arrays[n] for n in ins])
    arrays.update(zip(outs, got))


GROUPS = [["row", "col", "out", "inc"]]


def shards(*args, groups=None, results=("msa_out", "z3")):
    groups = groups or GROUPS
    names = ["msa", "pairs", "row_w", "row_out", "pair_bias", "col_w", "col_out", "maps", "outer_out"]
    names += ["o_proj", "o_out", "i_proj", "i_out"]
    arrays = dict(zip(names, args))
    msa_shape, pair_shape = arrays["msa"].shape, arrays["pairs"].shape
    arrays["pair_bias"], arrays["maps"] = arrays["pair_bias"].T, arrays["maps"].T
    arrays["msa"] = arrays["msa"].reshape(2, 128, 256)
    arrays["pairs"] = arrays["pairs"].reshape(4, 128, 128)
    for number, group in enumerate(groups):
        later = [n for g in groups[number + 1 :] for p in g for n in PARTS[p]["ins"]]
        run_parts(group, arrays, set(results) | set(later), number)
    outs = dict(
        msa_out=lambda a: a.reshape(msa_shape),
        z3=lambda a: a.reshape(pair_shape),
    )
    return tuple(outs.get(n, lambda a: a)(arrays[n]) for n in results)


def solution(mesh):
    return jax.shard_map(
        shards,
        mesh=mesh,
        in_specs=(P("row", None, "col", None, None),) * 2 + (P(),) * 11,
        out_specs=(P("row", None, "col", None, None),) * 2,
        check_vma=False,
    )
```

```python
import functools
import math

import jax
import jax.numpy as jnp
from jax import lax
from jax.experimental import pallas as pl
from jax.experimental.pallas import tpu as pltpu
from jax.sharding import PartitionSpec as P

MESH = pl.DeviceIdType.MESH
BF = jnp.bfloat16
F32 = jnp.float32
EPS = 1e-05
HEADS = 8
NXY = 16
NZC = 8
NCOL = 4


def nn(a, b):
    return lax.dot_general(a, b, (((1,), (0,)), ((), ())), preferred_element_type=F32)


def nt(a, b):
    return lax.dot_general(a, b, (((1,), (1,)), ((), ())), preferred_element_type=F32)


def tn(a, b):
    return lax.dot_general(a, b, (((0,), (0,)), ((), ())), preferred_element_type=F32)


def norm(x, axis=-1):
    c = x - jnp.mean(x, axis=axis, keepdims=True)
    v = jnp.mean(c * c, axis=axis, keepdims=True)
    return c * lax.rsqrt(v + EPS)


def sig(x):
    return 1.0 / (1.0 + jnp.exp(-x))


def perm(sizes, order, first=0, count=None):
    n = math.prod(sizes)
    count = count or n
    strides = [math.prod(sizes[k + 1 :]) for k in range(len(sizes))]
    out = lax.broadcasted_iota(jnp.int32, (count, 1), 0) + first
    src = jnp.zeros((count, 1), jnp.int32)
    rest = out
    for axis in reversed(order):
        src = src + (rest & (sizes[axis] - 1)) * strides[axis]
        rest = lax.shift_right_logical(rest, int(math.log2(sizes[axis])))
    inp = lax.broadcasted_iota(jnp.int32, (count, n), 1)
    return jnp.where(src == inp, 1.0, 0.0).astype(BF)


def where_am_i():
    row, col = lax.axis_index("row"), lax.axis_index("col")
    return row, col, row // NZC, row % NZC


def in_quad():
    row, col, xy, zc = where_am_i()
    return 2 * col + zc // 4, zc % 4


def place(xy, m, e):
    return xy * NZC + m % 2 * 4 + e, m // 2


class Swap:
    def __init__(self, r, name):
        self.send, self.recv = r[name + "_s"], r[name + "_r"]
        self.row, self.col, self.xy, self.zc = where_am_i()
        self.m, self.e = in_quad()

    def put(self, src, dst, row, col):
        pltpu.make_async_remote_copy(
            src_ref=src,
            dst_ref=dst,
            send_sem=self.send,
            recv_sem=self.recv,
            device_id=(row, col),
            device_id_type=MESH,
        ).start()

    def keep(self, src, dst):
        pltpu.make_async_copy(src, dst, self.recv).start()

    def peers(self, kind):
        if kind == "xy":
            for d in range(1, NXY):
                g = lax.rem(self.xy + d, NXY)
                yield g, g * NZC + self.zc, self.col
        elif kind == "zc":
            for d in range(1, NZC):
                g = lax.rem(self.zc + d, NZC)
                yield g, self.xy * NZC + g, self.col
        elif kind == "quad":
            for d in range(1, 4):
                g = lax.rem(self.e + d, 4)
                yield g, *place(self.xy, self.m, g)
        else:
            for d in range(1, NCOL):
                g = lax.rem(self.col + d, NCOL)
                yield g, self.row, g

    def mine(self, kind):
        return {"xy": self.xy, "zc": self.zc, "col": self.col, "quad": self.e}[kind]

    def exchange(self, kind, src, dst):
        me = self.mine(kind)
        for g, row, col in self.peers(kind):
            self.put(src.at[g], dst.at[me], row, col)
        self.keep(src.at[me], dst.at[me])

    def gather(self, kind, buf):
        me = self.mine(kind)
        for g, row, col in self.peers(kind):
            self.put(buf.at[me], buf.at[me], row, col)

    def either(self, src, dst, away, row, col):
        @pl.when(away)
        def _():
            self.put(src, dst, row, col)

        @pl.when(jnp.logical_not(away))
        def _():
            self.keep(src, dst)

    def direct(self, src, slot, member):
        core = lax.rem(self.zc, 2)
        here = self.xy * 4 + self.m // 2
        for d in range(1, 64):
            g = lax.rem(here + d, 64)
            self.put(src.at[g], slot, *place(g // 4, g % 4 * 2 + core, member))
        row, col = place(self.xy, self.m // 2 * 2 + core, member)
        self.either(src.at[here], slot, self.elsewhere(member), row, col)

    def elsewhere(self, member):
        return jnp.logical_or(lax.rem(self.m, 2) != lax.rem(self.zc, 2), self.e != member)

    def sent64(self, src, member):
        self.sent(src.at[pl.ds(0, 63)])

        @pl.when(self.elsewhere(member))
        def _():
            self.sent(src.at[0])

    def back(self, src, dst):
        for d in range(1, 8):
            g = lax.rem(self.zc + d, 8)
            self.put(src.at[g], dst.at[self.m], self.xy * NZC + g, self.e)
        self.either(src.at[self.zc], dst.at[self.m], self.e != self.col, self.row, self.e)

    def sent8(self, src):
        self.sent(src.at[pl.ds(0, 7)])

        @pl.when(self.e != self.col)
        def _():
            self.sent(src.at[0])

    def got(self, ref):
        pltpu.make_async_copy(ref, ref, self.recv).wait()

    def sent(self, ref):
        pltpu.make_async_copy(ref, ref, self.send).wait()


def barrier_signal():
    row, col, xy, zc = where_am_i()
    m, e = in_quad()
    sem = pltpu.get_barrier_semaphore()

    def hail(r, c):
        pl.semaphore_signal(sem, inc=1, device_id=(r, c), device_id_type=MESH)

    for d in range(1, NXY):
        hail(lax.rem(xy + d, NXY) * NZC + zc, col)
    for d in range(1, 32):
        t = lax.rem(m * 4 + e + d, 32)
        hail(*place(xy, t // 4, t % 4))


def barrier_wait():
    pl.semaphore_wait(pltpu.get_barrier_semaphore(), NXY + 32 - 2)


def project(keys, own, weights):
    q = nn(own, weights[:, 0:256]).astype(BF)
    k = nn(keys, weights[:, 256:512]).astype(BF)
    v = nn(keys, weights[:, 512:768]).astype(BF)
    gate = nn(own, weights[:, 768:1024]).astype(BF).astype(F32)
    return q, k, jnp.concatenate([v, jnp.ones((keys.shape[0], 128), BF)], axis=1), gate


def attend(q, k, v, heads, bias):
    head = lax.broadcasted_iota(jnp.int32, q.shape, 1) // 32
    total = jnp.zeros(q.shape, F32)
    for h in heads:
        scores = nt(jnp.where(head == h, q, jnp.zeros_like(q)), k) * (1.0 / math.sqrt(32.0))
        if bias is not None:
            scores = scores + bias(h)
        top = jnp.max(scores, axis=-1, keepdims=True)
        p = jnp.exp(scores - top).astype(BF)
        mixed = nn(p, v)
        inv = 1.0 / mixed[:, 256:384]
        mixed = mixed[:, 0:256] * jnp.concatenate([inv, inv], axis=1)
        total = total + jnp.where(head == h, mixed, 0.0)
    return total


def by_kind(ref):
    w = ref[...]
    return jnp.concatenate(
        [w[:, 128 * h + 32 * k : 128 * h + 32 * k + 32] for k in range(4) for h in range(HEADS)], axis=1
    )


ROW_SCRATCH = dict(
    xr=((2, 128, 256), BF),
    xg=((2, 4, 128, 256), BF),
    bs=((2, 2, 8, 128), F32),
    bo=((2, 8, 128), F32),
    bq=((2, 16, 128), BF),
    brecv=((4, 4, 16, 128), BF),
    bx=((4, 4, 128, 256), BF),
    wrow=((256, 1024), BF),
)
ROW_SEMS = ["m0", "m1", "g0", "g1", "bc", "b0", "b1", "b2", "b3"]


def row_part(r):
    row, col, xy, zc = where_am_i()
    m, e = in_quad()
    msa, xr, xg = r["msa"], r["xr"], r["xg"]
    zn = norm(r["pairs"][...].astype(F32)).astype(BF).reshape(512, 128)
    bias_t = nt(r["pair_bias"][...], zn)
    for k in range(4):
        r["bs"][k // 2, k % 2] = bias_t[:, 128 * k : 128 * k + 128]
    core = lax.rem(zc, 2)
    barrier_wait()
    sc = Swap(r, "bc")
    sc.put(r["bs"].at[1 - core], r["bo"], row + 1 - 2 * core, col)
    sc.got(r["bo"])
    ours, theirs = r["bs"][core], r["bo"][...]
    r["bq"][...] = jnp.concatenate(
        [jnp.where(core == 0, ours, theirs), jnp.where(core == 0, theirs, ours)], axis=1
    ).astype(BF)
    s0 = Swap(r, "b0")
    slot = r["brecv"].at[zc // 2, col]
    for d in range(1, 8):
        for k in range(2):
            s0.put(r["bq"].at[k], slot, *place(xy, lax.rem(m + d, 8), 2 * core + k))
    for k in range(2):
        s0.either(r["bq"].at[k], slot, e != 2 * core + k, *place(xy, m, 2 * core + k))
    direct = [Swap(r, "m0"), Swap(r, "m1")]
    away = jnp.logical_or(zc != m, col != e)
    for s in range(2):
        direct[s].either(msa.at[s], xr.at[s], away, *place(xy, zc, col))
    r["wrow"][...] = by_kind(r["row_w"])
    pz = perm((2, 4, 2, 2, 4), (3, 0, 4, 1, 2))
    shared = [Swap(r, "g0"), Swap(r, "g1")]

    def share(s):
        direct[s].got(xr.at[s])
        xg[s, e] = norm(xr[s].astype(F32)).astype(BF)
        shared[s].gather("quad", xg.at[s])

    s0.got(r["brecv"])
    b = r["brecv"]
    lo = jnp.concatenate([b[:, 0], b[:, 1]], axis=2).reshape(64, 256)
    hi = jnp.concatenate([b[:, 2], b[:, 3]], axis=2).reshape(64, 256)
    rows = jnp.concatenate([lo, hi], axis=0)
    bx, y, x = r["bx"], xy // 4, xy % 4
    bx[y, x] = nn(pz, rows).astype(BF)
    s2 = [Swap(r, "b2"), Swap(r, "b3")]
    near = Swap(r, "b1")
    for d in range(1, 4):
        to = lax.rem(y + d * core, 4) * 4 + lax.rem(x + d - d * core, 4)
        near.put(bx.at[y, x], bx.at[y, x], to * NZC + zc, col)
    share(0)
    share(1)
    near.got(bx.at[0, pl.ds(0, 3)])

    @pl.when(core == 0)
    def _():
        for k in range(2):
            line = bx.at[y, :, pl.ds(64 * k, 64)]
            for d in range(1, 4):
                s2[k].put(line, line, (lax.rem(y + d, 4) * 4 + x) * NZC + zc, col)

    @pl.when(core == 1)
    def _():
        for k in range(2):
            line = bx.at[:, x, pl.ds(64 * k, 64)]
            for d in range(1, 4):
                s2[k].put(line, line, (y * 4 + lax.rem(x + d, 4)) * NZC + zc, col)

    if "prep" in r:
        r["prep"]()
    ready = []
    for s in range(2):
        shared[s].got(xg.at[s, pl.ds(0, 3)])
        ready.append(project(xg[s].reshape(512, 256), xg[s, e], r["wrow"]))
    cache = {}
    to_zc = perm((16, 8), (1, 0))

    def bias(h):
        if h not in cache:
            pair = h // 2 * 2
            parts = []
            for jh in range(2):
                at = (h // 4 * 8 + jh * 4 + pair % 4) * 8
                parts.append(bx[:, :, at : at + 16, :].reshape(16, 16, 256).astype(F32))
            for k in range(2):
                cache[pair + k] = jnp.concatenate(
                    [p[:, 8 * k : 8 * k + 8].reshape(128, 256) for p in parts], axis=1
                )
        return cache[h]

    totals = []
    for part in range(2):
        s2[part].got(bx.at[pl.ds(0, 3), :, pl.ds(64 * part, 64)])
        for s in range(2):
            q, k, v, gate = ready[s]
            cache.clear()
            mixed = attend(q, k, v, range(4 * part, 4 * part + 4), bias)
            if part == 0:
                totals.append(mixed)
                continue
            gated = (sig(gate) * (totals[s] + mixed)).astype(BF)
            m1 = (xr[s].astype(F32) + nn(gated, r["row_out"][...])).astype(BF)
            r["cs1"][:, 16 * s : 16 * s + 16] = nn(to_zc, m1).astype(BF).reshape(8, 16, 256)
            rows = pl.ds(16 * s, 16)
            Swap(r, "c1" + "ab"[s]).back(r["cs1"].at[:, rows], r["cr1"].at[:, rows])
    def row_sent():
        for s in range(2):
            shared[s].sent(xg.at[s, pl.ds(0, 3)])

            @pl.when(away)
            def _():
                direct[s].sent(msa.at[s])

        s0.sent(r["brecv"].at[pl.ds(0, 3)])
        s0.sent(r["brecv"].at[0, pl.ds(0, 2)])
        for k in range(2):

            @pl.when(e != 2 * core + k)
            def _():
                s0.sent(r["bq"].at[k])

        sc.sent(r["bo"])
        for k in range(2):
            s2[k].sent(bx.at[pl.ds(0, 3), :, pl.ds(64 * k, 64)])
        near.sent(bx.at[0, pl.ds(0, 3)])

    return row_sent


COL_SCRATCH = dict(
    cs1=((8, 32, 256), BF),
    cr1=((8, 32, 256), BF),
    cs2=((16, 16, 256), BF),
    cr2=((16, 16, 256), BF),
    ds1=((16, 16, 256), BF),
    dr1=((16, 16, 256), BF),
    ds2=((8, 32, 256), BF),
    dr2=((8, 32, 256), BF),
    lg=((4, 32, 256), BF),
    rz=((8, 32, 256), BF),
    rx=((4, 4, 256, 256), BF),
    wcol=((256, 1024), BF),
    bd=((32, 128, 512), BF),
    at=((32, 256, 512), BF),
)
COL_SEMS = ["c1a", "c1b", "c2", "d1", "d2", "lg", "rz", "rx", "ry", "rc"]


def col_prep(r):
    r["wcol"][...] = by_kind(r["col_w"])
    by_u = nn(perm((32, 32), (1, 0)), r["outer_out"][...]).astype(BF).reshape(32, 32, 128)
    r["bd"][...] = jnp.zeros((32, 128, 512), BF)
    for i in range(4):
        r["bd"][:, 32 * i : 32 * i + 32, 128 * i : 128 * i + 128] = by_u


def col_part(r):
    row, col, xy, zc = where_am_i()
    core = lax.rem(zc, 2)
    to_xy = perm((8, 2, 16), (2, 0, 1))
    c1 = [Swap(r, "c1a"), Swap(r, "c1b")]
    for k in range(2):
        c1[k].got(r["cr1"].at[:, pl.ds(16 * k, 16)])
    r["cs2"][...] = nn(to_xy, r["cr1"][...].reshape(256, 256)).astype(BF).reshape(16, 16, 256)
    c2 = Swap(r, "c2")
    c2.exchange("xy", r["cs2"], r["cr2"])
    c2.got(r["cr2"])
    lines = r["cr2"][...].reshape(256, 256).astype(F32)
    x = norm(lines).astype(BF)
    q, k, v, gate = project(x, x, r["wcol"])
    gated = (sig(gate) * attend(q, k, v, range(HEADS), None)).astype(BF)
    m2 = lines + nn(gated, r["col_out"][...])
    x = norm(m2).astype(BF)
    ab = nt(r["maps"][...], x).astype(BF)
    r["lg"][col] = ab[0:32]
    r["rz"][zc] = ab[32:64]
    rz = Swap(r, "rz")
    rz.gather("zc", r["rz"])
    r["ds1"][...] = m2.astype(BF).reshape(16, 16, 256)
    to_u = perm((8, 32), (1, 0))
    lg = Swap(r, "lg")
    rz.got(r["rz"].at[pl.ds(0, 7)])
    lg.gather("col", r["lg"])
    right = nn(to_u, r["rz"][...].reshape(256, 256)).astype(BF)
    rx = r["rx"]
    y, x = xy // 4, xy % 4
    for k in range(2):

        @pl.when(core == k)
        def _():
            rx[y, x, 128 * k : 128 * k + 128] = right[128 * k : 128 * k + 128]

    half = pl.ds(pl.multiple_of(core * 128, 128), 128)
    other = pl.ds(pl.multiple_of(128 - core * 128, 128), 128)
    rxs = Swap(r, "rx")
    for d in range(1, 4):
        to = lax.rem(y + d * core, 4) * 4 + lax.rem(x + d - d * core, 4)
        rxs.put(rx.at[y, x, half], rx.at[y, x, half], to * NZC + zc, col)
    rxs.got(rx.at[0, pl.ds(0, 3), pl.ds(0, 128)])
    rys = Swap(r, "ry")

    @pl.when(core == 0)
    def _():
        line = rx.at[y, :, pl.ds(0, 128)]
        for d in range(1, 4):
            rys.put(line, line, (lax.rem(y + d, 4) * 4 + x) * NZC + zc, col)

    @pl.when(core == 1)
    def _():
        line = rx.at[:, x, pl.ds(128, 128)]
        for d in range(1, 4):
            rys.put(line, line, (y * 4 + lax.rem(x + d, 4)) * NZC + zc, col)

    lg.got(r["lg"].at[pl.ds(0, 3)])
    left = r["lg"][...].reshape(128, 256).T
    for u in range(32):
        r["at"][u] = nn(left, r["bd"][u]).astype(BF)
    rys.got(rx.at[pl.ds(0, 3), :, pl.ds(0, 128)])
    rc = Swap(r, "rc")
    rc.put(rx.at[:, :, half], rx.at[:, :, half], row + 1 - 2 * core, col)
    def add(base, acc):
        for up in range(8):
            at = pl.multiple_of(base * 8 + up * 16, 16)
            block = rx[:, :, pl.ds(at, 16), :].reshape(16, 16, 256).astype(F32)
            for k in range(2):
                acc = acc + nn(block[:, 8 * k : 8 * k + 8].reshape(128, 256).astype(BF), r["at"][base + 2 * up + k])
        return acc

    acc = add(core * 16, jnp.zeros((128, 512), F32))
    rc.got(rx.at[:, :, other])
    acc = add(16 - core * 16, acc)
    for i in range(4):
        r["z1"][i] = r["pairs"][i].astype(F32) + acc[:, 128 * i : 128 * i + 128] * (1.0 / 256.0)
    d1, d2 = Swap(r, "d1"), Swap(r, "d2")

    def plane():
        d1.exchange("xy", r["ds1"], r["dr1"])

    def line():
        d1.got(r["dr1"])
        rows = nn(perm((16, 8, 2), (1, 2, 0)), r["dr1"][...].reshape(256, 256))
        r["ds2"][...] = rows.astype(BF).reshape(8, 32, 256)
        d2.exchange("zc", r["ds2"], r["dr2"])

    def finish():
        d2.got(r["dr2"])
        rows = nn(perm((8, 2, 16), (1, 2, 0)), r["dr2"][...].reshape(256, 256))
        r["msa_out"][...] = rows.astype(BF).reshape(2, 128, 256)

    r["later"] = [plane, line, finish]

    def col_sent():
        for k in range(2):
            c1[k].sent8(r["cs1"].at[:, pl.ds(16 * k, 16)])
        c2.sent(r["cs2"].at[pl.ds(0, 15)])
        d1.sent(r["ds1"].at[pl.ds(0, 15)])
        d2.sent(r["ds2"].at[pl.ds(0, 7)])
        lg.sent(r["lg"].at[pl.ds(0, 3)])
        rz.sent(r["rz"].at[pl.ds(0, 7)])
        rxs.sent(rx.at[0, pl.ds(0, 3), pl.ds(0, 128)])
        rys.sent(rx.at[pl.ds(0, 3), :, pl.ds(0, 128)])
        rc.sent(rx.at[:, :, half])

    return col_sent


def tri_scratch(t, outgoing):
    return {
        t + "f": ((1024, 128), F32),
        t + "h": ((512, 128), F32),
        t + "s2": ((64, 16, 128), BF),
        t + "r2": ((16, 4, 16, 128), BF),
        t + "ps": ((4, 512, 128), BF),
        t + "pr": ((4, 512, 128), BF),
        t + "s3": ((8, 64, 128), BF),
        t + "r3": ((8, 64, 128), BF),
        t + "s4": ((16, 32, 128), BF),
        t + "r4": ((16, 32, 128), BF),
        t + "gate": ((512, 128), F32),
        t + "wg": ((256, 128), BF),
        t + "wv": ((256, 128), BF),
    }


def tri_sems(t):
    return [t + k for k in ("1", "2", "p0", "p1", "30", "31", "40", "41")]


def tri_prep(r, t):
    by_core = perm((16, 4, 2), (2, 0, 1))
    w = r[t + "_proj"]
    for k in range(2):
        rows = pl.ds(128 * k, 128)
        r[t + "wg"][rows] = nt(by_core, w[:, 256 * k : 256 * k + 128]).astype(BF)
        r[t + "wv"][rows] = nt(by_core, w[:, 256 * k + 128 : 256 * k + 256]).astype(BF)


def tri_part(r, t, src, dst, outgoing):
    row, col, xy, zc = where_am_i()
    m, e = in_quad()
    x = norm(r[src][...]).astype(BF).reshape(512, 128)
    both = sig(nt(r[t + "wg"][...], x)) * nt(r[t + "wv"][...], x)
    core = lax.rem(zc, 2)
    f, h, s2, r2 = (r[t + k] for k in ("f", "h", "s2", "r2"))
    for k in range(2):
        for q in range(4):
            f[pl.ds(4 * k + q, 128, stride=8), :] = both[128 * k : 128 * k + 128, 128 * q : 128 * q + 128]
    e1 = Swap(r, t + "1")
    theirs = f.at[pl.ds(pl.multiple_of(512 - core * 512, 512), 512)]
    e1.put(theirs, h, row + 1 - 2 * core, col)
    r[t + "gate"][...] = sig(nn(x, r[t + "_proj"][:, 512:640]))
    ours = f[pl.ds(pl.multiple_of(core * 512, 512), 512), :].reshape(64, 8, 128)
    e1.got(h)
    other = h[...].reshape(64, 8, 128)
    s2[...] = jnp.concatenate(
        [jnp.where(core == 0, ours, other), jnp.where(core == 0, other, ours)], axis=1
    ).astype(BF)
    e2 = Swap(r, t + "2")
    member, slot = (col, zc // 2) if outgoing else (zc // 2, col)
    e2.direct(s2, r2.at[xy, slot], member)
    if outgoing:
        r["later"][0]()
        to_left = perm((16, 4, 2, 2, 4), (3, 4, 1, 2, 0), 0, 512)
        to_right = perm((16, 4, 2, 2, 4), (3, 4, 0, 1, 2), 512, 512)
    else:
        r["later"][2]()
        to_both = perm((16, 4, 2, 2, 4), (3, 1, 0, 2, 4))
        natural = perm((16, 8), (1, 0))
    e2.got(r2)
    landed = r2[...].reshape(1024, 128)
    ps, pr = r[t + "ps"], r[t + "pr"]
    s3, r3, s4, r4 = (r[t + k] for k in ("s3", "r3", "s4", "r4"))
    if outgoing:
        left = nn(to_left, landed).astype(BF)
        right = nn(to_right, landed).astype(BF)
    else:
        rows = nn(to_both, landed).astype(BF)
        left = jnp.concatenate([nt(natural, rows[128 * c : 128 * c + 128]).astype(BF) for c in range(4)], axis=0)
        right = rows[512:1024]
    right = [right[128 * c : 128 * c + 128] for c in range(4)]
    ep = [Swap(r, t + "p0"), Swap(r, t + "p1")]
    e3 = [Swap(r, t + "30"), Swap(r, t + "31")]
    e4 = [Swap(r, t + "40"), Swap(r, t + "41")]
    for half in range(2):
        rows = pl.ds(256 * half, 256)
        part = left[256 * half : 256 * half + 256]
        for c in range(4):
            ps[c, rows] = (nt if outgoing else nn)(part, right[c]).astype(BF)
        ep[half].exchange("quad", ps.at[:, rows], pr.at[:, rows])
    by_plane = perm((8, 2, 16), (2, 1, 0))
    for half in range(2):
        rows = pl.ds(256 * half, 256)
        ep[half].got(pr.at[:, rows])
        mix = (pr[0, rows].astype(F32) + pr[1, rows].astype(F32)) + (pr[2, rows].astype(F32) + pr[3, rows].astype(F32))
        mix = mix.astype(BF).reshape(2, 8, 16, 128)
        for q in range(2):
            s3[:, 32 * half + 16 * q : 32 * half + 16 * q + 16] = mix[q]
        rows = pl.ds(32 * half, 32)
        e3[half].back(s3.at[:, rows], r3.at[:, rows])
    for half in range(2):
        rows = pl.ds(32 * half, 32)
        e3[half].got(r3.at[:, rows])
        rows4 = pl.ds(16 * half, 16)
        s4[:, rows4] = nn(by_plane, r3[:, rows].reshape(256, 128)).astype(BF).reshape(16, 16, 128)
        e4[half].exchange("xy", s4.at[:, rows4], r4.at[:, rows4])
    if outgoing:
        r["later"][1]()
    for half in range(2):
        rows4 = pl.ds(16 * half, 16)
        e4[half].got(r4.at[:, rows4])
        got = r4[:, rows4].astype(F32)
        for k in range(2):
            q = 2 * half + k
            step = tn(norm(got[:, 8 * k : 8 * k + 8].reshape(128, 128), 0).astype(BF), r[t + "_out"][...])
            r[dst][q] = r[src][q] + r[t + "gate"][128 * q : 128 * q + 128] * step
    def tri_sent():
        e1.sent(h)
        e2.sent64(s2, member)
        for half in range(2):
            ep[half].sent(ps.at[pl.ds(0, 3), pl.ds(0, 256)])
            e3[half].sent8(s3.at[:, pl.ds(32 * half, 32)])
            e4[half].sent(s4.at[pl.ds(0, 15), pl.ds(0, 16)])

    return tri_sent


SHAPES = dict(
    z1=((4, 128, 128), F32),
    z2=((4, 128, 128), F32),
    z3=((4, 128, 128), F32),
    msa_out=((2, 128, 256), BF),
)


PARTS = dict(
    row=dict(ins=["msa", "pairs", "row_w", "row_out", "pair_bias"], outs=[], scratch=ROW_SCRATCH, sems=ROW_SEMS),
    col=dict(
        ins=["pairs", "col_w", "col_out", "maps", "outer_out"],
        outs=["msa_out", "z1"],
        scratch=COL_SCRATCH,
        sems=COL_SEMS,
    ),
    out=dict(ins=["z1", "o_proj", "o_out"], outs=["z2"], scratch=tri_scratch("o", True), sems=tri_sems("o")),
    inc=dict(ins=["z2", "i_proj", "i_out"], outs=["z3"], scratch=tri_scratch("i", False), sems=tri_sems("i")),
)


def run_parts(parts, arrays, results, number):
    ins, made, scratch, sems = [], [], {}, []
    for p in parts:
        spec = PARTS[p]
        ins += [n for n in spec["ins"] if n not in ins and n not in made]
        made += spec["outs"]
        scratch.update(spec["scratch"])
        sems += spec["sems"]
    outs = [n for n in made if n in results]
    inner = {n: SHAPES[n] for n in made if n not in results}
    scratch = {**scratch, **inner}
    sem_names = [s + e for s in sems for e in ("_s", "_r")]

    def body(*refs):
        r = dict(zip(ins + outs + list(scratch) + sem_names, refs))
        barrier_signal()

        def prep():
            if "col" in parts:
                col_prep(r)
            if "out" in parts:
                tri_prep(r, "o")
            if "inc" in parts:
                tri_prep(r, "i")

        if parts[0] == "row":
            r["prep"] = prep
        else:
            prep()
            barrier_wait()
        waits = []
        for p in parts:
            if p == "row":
                waits.append(row_part(r))
            elif p == "col":
                waits.append(col_part(r))
            elif p == "out":
                waits.append(tri_part(r, "o", "z1", "z2", True))
            else:
                waits.append(tri_part(r, "i", "z2", "z3", False))
        for wait in waits:
            wait()

    vm = pl.BlockSpec(memory_space=pltpu.VMEM)
    got = pl.pallas_call(
        body,
        out_shape=[jax.ShapeDtypeStruct(*SHAPES[n]) for n in outs],
        in_specs=[vm] * len(ins),
        out_specs=[vm] * len(outs),
        scratch_shapes=[pltpu.VMEM(*scratch[n]) for n in scratch] + [pltpu.SemaphoreType.DMA] * len(sem_names),
        compiler_params=pltpu.CompilerParams(
            collective_id=number, has_side_effects=True, vmem_limit_bytes=56 * 1024 * 1024
        ),
        name="_".join(parts),
    )(*[arrays[n] for n in ins])
    arrays.update(zip(outs, got))


GROUPS = [["row", "col", "out", "inc"]]


def shards(*args, groups=None, results=("msa_out", "z3")):
    groups = groups or GROUPS
    names = ["msa", "pairs", "row_w", "row_out", "pair_bias", "col_w", "col_out", "maps", "outer_out"]
    names += ["o_proj", "o_out", "i_proj", "i_out"]
    arrays = dict(zip(names, args))
    msa_shape, pair_shape = arrays["msa"].shape, arrays["pairs"].shape
    arrays["pair_bias"], arrays["maps"] = arrays["pair_bias"].T, arrays["maps"].T
    arrays["msa"] = arrays["msa"].reshape(2, 128, 256)
    arrays["pairs"] = arrays["pairs"].reshape(4, 128, 128)
    for number, group in enumerate(groups):
        later = [n for g in groups[number + 1 :] for p in g for n in PARTS[p]["ins"]]
        run_parts(group, arrays, set(results) | set(later), number)
    outs = dict(
        msa_out=lambda a: a.reshape(msa_shape),
        z3=lambda a: a.reshape(pair_shape),
    )
    return tuple(outs.get(n, lambda a: a)(arrays[n]) for n in results)


def solution(mesh):
    return jax.shard_map(
        shards,
        mesh=mesh,
        in_specs=(P("row", None, "col", None, None),) * 2 + (P(),) * 11,
        out_specs=(P("row", None, "col", None, None),) * 2,
        check_vma=False,
    )
```

```python
import functools
import math

import jax
import jax.numpy as jnp
from jax import lax
from jax.experimental import pallas as pl
from jax.experimental.pallas import tpu as pltpu
from jax.sharding import PartitionSpec as P

MESH = pl.DeviceIdType.MESH
BF = jnp.bfloat16
F32 = jnp.float32
EPS = 1e-05
HEADS = 8
NXY = 16
NZC = 8
NCOL = 4


def nn(a, b):
    return lax.dot_general(a, b, (((1,), (0,)), ((), ())), preferred_element_type=F32)


def nt(a, b):
    return lax.dot_general(a, b, (((1,), (1,)), ((), ())), preferred_element_type=F32)


def tn(a, b):
    return lax.dot_general(a, b, (((0,), (0,)), ((), ())), preferred_element_type=F32)


def norm(x, axis=-1):
    c = x - jnp.mean(x, axis=axis, keepdims=True)
    v = jnp.mean(c * c, axis=axis, keepdims=True)
    return c * lax.rsqrt(v + EPS)


def sig(x):
    return 1.0 / (1.0 + jnp.exp(-x))


def perm(sizes, order, first=0, count=None):
    n = math.prod(sizes)
    count = count or n
    strides = [math.prod(sizes[k + 1 :]) for k in range(len(sizes))]
    out = lax.broadcasted_iota(jnp.int32, (count, 1), 0) + first
    src = jnp.zeros((count, 1), jnp.int32)
    rest = out
    for axis in reversed(order):
        src = src + (rest & (sizes[axis] - 1)) * strides[axis]
        rest = lax.shift_right_logical(rest, int(math.log2(sizes[axis])))
    inp = lax.broadcasted_iota(jnp.int32, (count, n), 1)
    return jnp.where(src == inp, 1.0, 0.0).astype(BF)


def where_am_i():
    row, col = lax.axis_index("row"), lax.axis_index("col")
    return row, col, row // NZC, row % NZC


def in_quad():
    row, col, xy, zc = where_am_i()
    return 2 * col + zc // 4, zc % 4


def place(xy, m, e):
    return xy * NZC + m % 2 * 4 + e, m // 2


class Swap:
    def __init__(self, r, name):
        self.send, self.recv = r[name + "_s"], r[name + "_r"]
        self.row, self.col, self.xy, self.zc = where_am_i()
        self.m, self.e = in_quad()

    def put(self, src, dst, row, col):
        pltpu.make_async_remote_copy(
            src_ref=src,
            dst_ref=dst,
            send_sem=self.send,
            recv_sem=self.recv,
            device_id=(row, col),
            device_id_type=MESH,
        ).start()

    def keep(self, src, dst):
        pltpu.make_async_copy(src, dst, self.recv).start()

    def peers(self, kind):
        if kind == "xy":
            for d in range(1, NXY):
                g = lax.rem(self.xy + d, NXY)
                yield g, g * NZC + self.zc, self.col
        elif kind == "zc":
            for d in range(1, NZC):
                g = lax.rem(self.zc + d, NZC)
                yield g, self.xy * NZC + g, self.col
        elif kind == "quad":
            for d in range(1, 4):
                g = lax.rem(self.e + d, 4)
                yield g, *place(self.xy, self.m, g)
        else:
            for d in range(1, NCOL):
                g = lax.rem(self.col + d, NCOL)
                yield g, self.row, g

    def mine(self, kind):
        return {"xy": self.xy, "zc": self.zc, "col": self.col, "quad": self.e}[kind]

    def exchange(self, kind, src, dst):
        me = self.mine(kind)
        for g, row, col in self.peers(kind):
            self.put(src.at[g], dst.at[me], row, col)
        self.keep(src.at[me], dst.at[me])

    def gather(self, kind, buf):
        me = self.mine(kind)
        for g, row, col in self.peers(kind):
            self.put(buf.at[me], buf.at[me], row, col)

    def either(self, src, dst, away, row, col):
        @pl.when(away)
        def _():
            self.put(src, dst, row, col)

        @pl.when(jnp.logical_not(away))
        def _():
            self.keep(src, dst)

    def direct(self, src, slot, member):
        core = lax.rem(self.zc, 2)
        here = self.xy * 4 + self.m // 2
        for d in range(1, 64):
            g = lax.rem(here + d, 64)
            self.put(src.at[g], slot, *place(g // 4, g % 4 * 2 + core, member))
        row, col = place(self.xy, self.m // 2 * 2 + core, member)
        self.either(src.at[here], slot, self.elsewhere(member), row, col)

    def elsewhere(self, member):
        return jnp.logical_or(lax.rem(self.m, 2) != lax.rem(self.zc, 2), self.e != member)

    def sent64(self, src, member):
        self.sent(src.at[pl.ds(0, 63)])

        @pl.when(self.elsewhere(member))
        def _():
            self.sent(src.at[0])

    def back(self, src, dst):
        for d in range(1, 8):
            g = lax.rem(self.zc + d, 8)
            self.put(src.at[g], dst.at[self.m], self.xy * NZC + g, self.e)
        self.either(src.at[self.zc], dst.at[self.m], self.e != self.col, self.row, self.e)

    def sent8(self, src):
        self.sent(src.at[pl.ds(0, 7)])

        @pl.when(self.e != self.col)
        def _():
            self.sent(src.at[0])

    def got(self, ref):
        pltpu.make_async_copy(ref, ref, self.recv).wait()

    def sent(self, ref):
        pltpu.make_async_copy(ref, ref, self.send).wait()


def barrier_signal():
    row, col, xy, zc = where_am_i()
    m, e = in_quad()
    sem = pltpu.get_barrier_semaphore()

    def hail(r, c):
        pl.semaphore_signal(sem, inc=1, device_id=(r, c), device_id_type=MESH)

    for d in range(1, NXY):
        hail(lax.rem(xy + d, NXY) * NZC + zc, col)
    for d in range(1, 32):
        t = lax.rem(m * 4 + e + d, 32)
        hail(*place(xy, t // 4, t % 4))


def barrier_wait():
    pl.semaphore_wait(pltpu.get_barrier_semaphore(), NXY + 32 - 2)


def project(keys, own, weights):
    q = nn(own, weights[:, 0:256]).astype(BF)
    k = nn(keys, weights[:, 256:512]).astype(BF)
    v = nn(keys, weights[:, 512:768]).astype(BF)
    gate = nn(own, weights[:, 768:1024]).astype(BF).astype(F32)
    return q, k, jnp.concatenate([v, jnp.ones((keys.shape[0], 128), BF)], axis=1), gate


def attend(q, k, v, heads, bias):
    head = lax.broadcasted_iota(jnp.int32, q.shape, 1) // 32
    total = jnp.zeros(q.shape, F32)
    for h in heads:
        scores = nt(jnp.where(head == h, q, jnp.zeros_like(q)), k) * (1.0 / math.sqrt(32.0))
        if bias is not None:
            scores = scores + bias(h)
        top = jnp.max(scores, axis=-1, keepdims=True)
        p = jnp.exp(scores - top).astype(BF)
        mixed = nn(p, v)
        inv = 1.0 / mixed[:, 256:384]
        mixed = mixed[:, 0:256] * jnp.concatenate([inv, inv], axis=1)
        total = total + jnp.where(head == h, mixed, 0.0)
    return total


def by_kind(ref):
    w = ref[...]
    return jnp.concatenate(
        [w[:, 128 * h + 32 * k : 128 * h + 32 * k + 32] for k in range(4) for h in range(HEADS)], axis=1
    )


ROW_SCRATCH = dict(
    xr=((2, 128, 256), BF),
    xg=((2, 4, 128, 256), BF),
    bs=((2, 2, 8, 128), F32),
    bo=((2, 8, 128), F32),
    bq=((2, 16, 128), BF),
    brecv=((4, 4, 16, 128), BF),
    bx=((4, 4, 128, 256), BF),
    wrow=((256, 1024), BF),
)
ROW_SEMS = ["m0", "m1", "g0", "g1", "bc", "b0", "b1", "b2", "b3"]


def row_part(r):
    row, col, xy, zc = where_am_i()
    m, e = in_quad()
    msa, xr, xg = r["msa"], r["xr"], r["xg"]
    zn = norm(r["pairs"][...].astype(F32)).astype(BF).reshape(512, 128)
    bias_t = nt(r["pair_bias"][...], zn)
    for k in range(4):
        r["bs"][k // 2, k % 2] = bias_t[:, 128 * k : 128 * k + 128]
    core = lax.rem(zc, 2)
    barrier_wait()
    sc = Swap(r, "bc")
    sc.put(r["bs"].at[1 - core], r["bo"], row + 1 - 2 * core, col)
    sc.got(r["bo"])
    ours, theirs = r["bs"][core], r["bo"][...]
    r["bq"][...] = jnp.concatenate(
        [jnp.where(core == 0, ours, theirs), jnp.where(core == 0, theirs, ours)], axis=1
    ).astype(BF)
    s0 = Swap(r, "b0")
    slot = r["brecv"].at[zc // 2, col]
    for d in range(1, 8):
        for k in range(2):
            s0.put(r["bq"].at[k], slot, *place(xy, lax.rem(m + d, 8), 2 * core + k))
    for k in range(2):
        s0.either(r["bq"].at[k], slot, e != 2 * core + k, *place(xy, m, 2 * core + k))
    direct = [Swap(r, "m0"), Swap(r, "m1")]
    away = jnp.logical_or(zc != m, col != e)
    for s in range(2):
        direct[s].either(msa.at[s], xr.at[s], away, *place(xy, zc, col))
    r["wrow"][...] = by_kind(r["row_w"])
    pz = perm((2, 4, 2, 2, 4), (3, 0, 4, 1, 2))
    shared = [Swap(r, "g0"), Swap(r, "g1")]

    def share(s):
        direct[s].got(xr.at[s])
        xg[s, e] = norm(xr[s].astype(F32)).astype(BF)
        shared[s].gather("quad", xg.at[s])

    s0.got(r["brecv"])
    b = r["brecv"]
    lo = jnp.concatenate([b[:, 0], b[:, 1]], axis=2).reshape(64, 256)
    hi = jnp.concatenate([b[:, 2], b[:, 3]], axis=2).reshape(64, 256)
    rows = jnp.concatenate([lo, hi], axis=0)
    bx, y, x = r["bx"], xy // 4, xy % 4
    bx[y, x] = nn(pz, rows).astype(BF)
    s2 = [Swap(r, "b2"), Swap(r, "b3")]
    near = Swap(r, "b1")
    for d in range(1, 4):
        to = lax.rem(y + d * core, 4) * 4 + lax.rem(x + d - d * core, 4)
        near.put(bx.at[y, x], bx.at[y, x], to * NZC + zc, col)
    share(0)
    share(1)
    near.got(bx.at[0, pl.ds(0, 3)])

    @pl.when(core == 0)
    def _():
        for k in range(2):
            line = bx.at[y, :, pl.ds(64 * k, 64)]
            for d in range(1, 4):
                s2[k].put(line, line, (lax.rem(y + d, 4) * 4 + x) * NZC + zc, col)

    @pl.when(core == 1)
    def _():
        for k in range(2):
            line = bx.at[:, x, pl.ds(64 * k, 64)]
            for d in range(1, 4):
                s2[k].put(line, line, (y * 4 + lax.rem(x + d, 4)) * NZC + zc, col)

    if "prep" in r:
        r["prep"]()
    ready = []
    for s in range(2):
        shared[s].got(xg.at[s, pl.ds(0, 3)])
        ready.append(project(xg[s].reshape(512, 256), xg[s, e], r["wrow"]))
    cache = {}
    to_zc = perm((16, 8), (1, 0))

    def bias(h):
        if h not in cache:
            pair = h // 2 * 2
            parts = []
            for jh in range(2):
                at = (h // 4 * 8 + jh * 4 + pair % 4) * 8
                parts.append(bx[:, :, at : at + 16, :].reshape(16, 16, 256).astype(F32))
            for k in range(2):
                cache[pair + k] = jnp.concatenate(
                    [p[:, 8 * k : 8 * k + 8].reshape(128, 256) for p in parts], axis=1
                )
        return cache[h]

    totals = []
    for part in range(2):
        s2[part].got(bx.at[pl.ds(0, 3), :, pl.ds(64 * part, 64)])
        for s in range(2):
            q, k, v, gate = ready[s]
            cache.clear()
            mixed = attend(q, k, v, range(4 * part, 4 * part + 4), bias)
            if part == 0:
                totals.append(mixed)
                continue
            gated = (sig(gate) * (totals[s] + mixed)).astype(BF)
            m1 = (xr[s].astype(F32) + nn(gated, r["row_out"][...])).astype(BF)
            r["cs1"][:, 16 * s : 16 * s + 16] = nn(to_zc, m1).astype(BF).reshape(8, 16, 256)
            rows = pl.ds(16 * s, 16)
            Swap(r, "c1" + "ab"[s]).back(r["cs1"].at[:, rows], r["cr1"].at[:, rows])
    def row_sent():
        for s in range(2):
            shared[s].sent(xg.at[s, pl.ds(0, 3)])

            @pl.when(away)
            def _():
                direct[s].sent(msa.at[s])

        s0.sent(r["brecv"].at[pl.ds(0, 3)])
        s0.sent(r["brecv"].at[0, pl.ds(0, 2)])
        for k in range(2):

            @pl.when(e != 2 * core + k)
            def _():
                s0.sent(r["bq"].at[k])

        sc.sent(r["bo"])
        for k in range(2):
            s2[k].sent(bx.at[pl.ds(0, 3), :, pl.ds(64 * k, 64)])
        near.sent(bx.at[0, pl.ds(0, 3)])

    return row_sent


COL_SCRATCH = dict(
    cs1=((8, 32, 256), BF),
    cr1=((8, 32, 256), BF),
    cs2=((16, 16, 256), BF),
    cr2=((16, 16, 256), BF),
    ds1=((16, 16, 256), BF),
    dr1=((16, 16, 256), BF),
    ds2=((8, 32, 256), BF),
    dr2=((8, 32, 256), BF),
    lg=((4, 32, 256), BF),
    rz=((8, 32, 256), BF),
    rx=((4, 4, 256, 256), BF),
    wcol=((256, 1024), BF),
    bd=((32, 128, 512), BF),
    at=((32, 256, 512), BF),
)
COL_SEMS = ["c1a", "c1b", "c2", "d1", "d2", "lg", "rz", "rx", "ry", "rc"]


def col_prep(r):
    r["wcol"][...] = by_kind(r["col_w"])
    by_u = nn(perm((32, 32), (1, 0)), r["outer_out"][...]).astype(BF).reshape(32, 32, 128)
    r["bd"][...] = jnp.zeros((32, 128, 512), BF)
    for i in range(4):
        r["bd"][:, 32 * i : 32 * i + 32, 128 * i : 128 * i + 128] = by_u


def col_part(r):
    row, col, xy, zc = where_am_i()
    core = lax.rem(zc, 2)
    to_xy = perm((8, 2, 16), (2, 0, 1))
    c1 = [Swap(r, "c1a"), Swap(r, "c1b")]
    for k in range(2):
        c1[k].got(r["cr1"].at[:, pl.ds(16 * k, 16)])
    r["cs2"][...] = nn(to_xy, r["cr1"][...].reshape(256, 256)).astype(BF).reshape(16, 16, 256)
    c2 = Swap(r, "c2")
    c2.exchange("xy", r["cs2"], r["cr2"])
    c2.got(r["cr2"])
    lines = r["cr2"][...].reshape(256, 256).astype(F32)
    x = norm(lines).astype(BF)
    q, k, v, gate = project(x, x, r["wcol"])
    gated = (sig(gate) * attend(q, k, v, range(HEADS), None)).astype(BF)
    m2 = lines + nn(gated, r["col_out"][...])
    x = norm(m2).astype(BF)
    ab = nt(r["maps"][...], x).astype(BF)
    r["lg"][col] = ab[0:32]
    r["rz"][zc] = ab[32:64]
    rz = Swap(r, "rz")
    rz.gather("zc", r["rz"])
    r["ds1"][...] = m2.astype(BF).reshape(16, 16, 256)
    to_u = perm((8, 32), (1, 0))
    lg = Swap(r, "lg")
    rz.got(r["rz"].at[pl.ds(0, 7)])
    lg.gather("col", r["lg"])
    right = nn(to_u, r["rz"][...].reshape(256, 256)).astype(BF)
    rx = r["rx"]
    y, x = xy // 4, xy % 4
    for k in range(2):

        @pl.when(core == k)
        def _():
            rx[y, x, 128 * k : 128 * k + 128] = right[128 * k : 128 * k + 128]

    half = pl.ds(pl.multiple_of(core * 128, 128), 128)
    other = pl.ds(pl.multiple_of(128 - core * 128, 128), 128)
    rxs = Swap(r, "rx")
    for d in range(1, 4):
        to = lax.rem(y + d * core, 4) * 4 + lax.rem(x + d - d * core, 4)
        rxs.put(rx.at[y, x, half], rx.at[y, x, half], to * NZC + zc, col)
    rxs.got(rx.at[0, pl.ds(0, 3), pl.ds(0, 128)])
    rys = Swap(r, "ry")

    @pl.when(core == 0)
    def _():
        line = rx.at[y, :, pl.ds(0, 128)]
        for d in range(1, 4):
            rys.put(line, line, (lax.rem(y + d, 4) * 4 + x) * NZC + zc, col)

    @pl.when(core == 1)
    def _():
        line = rx.at[:, x, pl.ds(128, 128)]
        for d in range(1, 4):
            rys.put(line, line, (y * 4 + lax.rem(x + d, 4)) * NZC + zc, col)

    lg.got(r["lg"].at[pl.ds(0, 3)])
    left = r["lg"][...].reshape(128, 256).T
    for u in range(32):
        r["at"][u] = nn(left, r["bd"][u]).astype(BF)
    rys.got(rx.at[pl.ds(0, 3), :, pl.ds(0, 128)])
    rc = Swap(r, "rc")
    rc.put(rx.at[:, :, half], rx.at[:, :, half], row + 1 - 2 * core, col)
    def add(base, acc):
        for up in range(8):
            at = pl.multiple_of(base * 8 + up * 16, 16)
            block = rx[:, :, pl.ds(at, 16), :].reshape(16, 16, 256).astype(F32)
            for k in range(2):
                acc = acc + nn(block[:, 8 * k : 8 * k + 8].reshape(128, 256).astype(BF), r["at"][base + 2 * up + k])
        return acc

    acc = add(core * 16, jnp.zeros((128, 512), F32))
    rc.got(rx.at[:, :, other])
    acc = add(16 - core * 16, acc)
    for i in range(4):
        r["z1"][i] = r["pairs"][i].astype(F32) + acc[:, 128 * i : 128 * i + 128] * (1.0 / 256.0)
    d1, d2 = Swap(r, "d1"), Swap(r, "d2")

    def plane():
        d1.exchange("xy", r["ds1"], r["dr1"])

    def line():
        d1.got(r["dr1"])
        rows = nn(perm((16, 8, 2), (1, 2, 0)), r["dr1"][...].reshape(256, 256))
        r["ds2"][...] = rows.astype(BF).reshape(8, 32, 256)
        d2.exchange("zc", r["ds2"], r["dr2"])

    def finish():
        d2.got(r["dr2"])
        rows = nn(perm((8, 2, 16), (1, 2, 0)), r["dr2"][...].reshape(256, 256))
        r["msa_out"][...] = rows.astype(BF).reshape(2, 128, 256)

    r["later"] = [plane, line, finish]

    def col_sent():
        for k in range(2):
            c1[k].sent8(r["cs1"].at[:, pl.ds(16 * k, 16)])
        c2.sent(r["cs2"].at[pl.ds(0, 15)])
        d1.sent(r["ds1"].at[pl.ds(0, 15)])
        d2.sent(r["ds2"].at[pl.ds(0, 7)])
        lg.sent(r["lg"].at[pl.ds(0, 3)])
        rz.sent(r["rz"].at[pl.ds(0, 7)])
        rxs.sent(rx.at[0, pl.ds(0, 3), pl.ds(0, 128)])
        rys.sent(rx.at[pl.ds(0, 3), :, pl.ds(0, 128)])
        rc.sent(rx.at[:, :, half])

    return col_sent


def tri_scratch(t, outgoing):
    return {
        t + "f": ((1032, 128), F32),
        t + "h": ((512, 128), F32),
        t + "s2": ((64, 16, 128), BF),
        t + "r2": ((16, 4, 16, 128), BF),
        t + "ps": ((4, 512, 128), BF),
        t + "pr": ((4, 512, 128), BF),
        t + "s3": ((8, 64, 128), BF),
        t + "r3": ((8, 64, 128), BF),
        t + "s4": ((16, 32, 128), BF),
        t + "r4": ((16, 32, 128), BF),
        t + "gate": ((512, 128), F32),
        t + "wg": ((256, 128), BF),
        t + "wv": ((256, 128), BF),
    }


def tri_sems(t):
    return [t + k for k in ("1", "2", "p0", "p1", "30", "31", "40", "41")]


def tri_prep(r, t):
    by_core = perm((16, 4, 2), (2, 0, 1))
    w = r[t + "_proj"]
    for k in range(2):
        rows = pl.ds(128 * k, 128)
        r[t + "wg"][rows] = nt(by_core, w[:, 256 * k : 256 * k + 128]).astype(BF)
        r[t + "wv"][rows] = nt(by_core, w[:, 256 * k + 128 : 256 * k + 256]).astype(BF)


def tri_part(r, t, src, dst, outgoing):
    row, col, xy, zc = where_am_i()
    m, e = in_quad()
    x = norm(r[src][...]).astype(BF).reshape(512, 128)
    both = sig(nt(r[t + "wg"][...], x)) * nt(r[t + "wv"][...], x)
    core = lax.rem(zc, 2)
    f, h, s2, r2 = (r[t + k] for k in ("f", "h", "s2", "r2"))
    for k in range(2):
        for q in range(4):
            f[pl.ds(4 * k + q, 128, stride=8), :] = both[128 * k : 128 * k + 128, 128 * q : 128 * q + 128]
    e1 = Swap(r, t + "1")
    theirs = f.at[pl.ds(pl.multiple_of(512 - core * 512, 512), 512)]
    e1.put(theirs, h, row + 1 - 2 * core, col)
    r[t + "gate"][...] = sig(nn(x, r[t + "_proj"][:, 512:640]))
    ours = f[pl.ds(pl.multiple_of(core * 512, 512), 512), :].reshape(64, 8, 128)
    e1.got(h)
    other = h[...].reshape(64, 8, 128)
    s2[...] = jnp.concatenate(
        [jnp.where(core == 0, ours, other), jnp.where(core == 0, other, ours)], axis=1
    ).astype(BF)
    e2 = Swap(r, t + "2")
    member, slot = (col, zc // 2) if outgoing else (zc // 2, col)
    e2.direct(s2, r2.at[xy, slot], member)
    if outgoing:
        r["later"][0]()
        to_left = perm((16, 4, 2, 2, 4), (3, 4, 1, 2, 0), 0, 512)
        to_right = perm((16, 4, 2, 2, 4), (3, 4, 0, 1, 2), 512, 512)
    else:
        r["later"][2]()
        to_both = perm((16, 4, 2, 2, 4), (3, 1, 0, 2, 4))
        natural = perm((16, 8), (1, 0))
    e2.got(r2)
    landed = r2[...].reshape(1024, 128)
    ps, pr = r[t + "ps"], r[t + "pr"]
    s3, r3, s4, r4 = (r[t + k] for k in ("s3", "r3", "s4", "r4"))
    if outgoing:
        left = nn(to_left, landed).astype(BF)
        right = nn(to_right, landed).astype(BF)
    else:
        rows = nn(to_both, landed).astype(BF)
        left = jnp.concatenate([nt(natural, rows[128 * c : 128 * c + 128]).astype(BF) for c in range(4)], axis=0)
        right = rows[512:1024]
    right = [right[128 * c : 128 * c + 128] for c in range(4)]
    ep = [Swap(r, t + "p0"), Swap(r, t + "p1")]
    e3 = [Swap(r, t + "30"), Swap(r, t + "31")]
    e4 = [Swap(r, t + "40"), Swap(r, t + "41")]
    for half in range(2):
        rows = pl.ds(256 * half, 256)
        part = left[256 * half : 256 * half + 256]
        for c in range(4):
            ps[c, rows] = (nt if outgoing else nn)(part, right[c]).astype(BF)
        ep[half].exchange("quad", ps.at[:, rows], pr.at[:, rows])
    by_plane = perm((8, 2, 16), (2, 1, 0))
    for half in range(2):
        rows = pl.ds(256 * half, 256)
        ep[half].got(pr.at[:, rows])
        mix = (pr[0, rows].astype(F32) + pr[1, rows].astype(F32)) + (pr[2, rows].astype(F32) + pr[3, rows].astype(F32))
        mix = mix.astype(BF).reshape(2, 8, 16, 128)
        for q in range(2):
            s3[:, 32 * half + 16 * q : 32 * half + 16 * q + 16] = mix[q]
        rows = pl.ds(32 * half, 32)
        e3[half].back(s3.at[:, rows], r3.at[:, rows])
    for half in range(2):
        rows = pl.ds(32 * half, 32)
        e3[half].got(r3.at[:, rows])
        rows4 = pl.ds(16 * half, 16)
        s4[:, rows4] = nn(by_plane, r3[:, rows].reshape(256, 128)).astype(BF).reshape(16, 16, 128)
        e4[half].exchange("xy", s4.at[:, rows4], r4.at[:, rows4])
    if outgoing:
        r["later"][1]()
    for half in range(2):
        rows4 = pl.ds(16 * half, 16)
        e4[half].got(r4.at[:, rows4])
        got = r4[:, rows4].astype(F32)
        for k in range(2):
            q = 2 * half + k
            step = tn(norm(got[:, 8 * k : 8 * k + 8].reshape(128, 128), 0).astype(BF), r[t + "_out"][...])
            r[dst][q] = r[src][q] + r[t + "gate"][128 * q : 128 * q + 128] * step
    def tri_sent():
        e1.sent(h)
        e2.sent64(s2, member)
        for half in range(2):
            ep[half].sent(ps.at[pl.ds(0, 3), pl.ds(0, 256)])
            e3[half].sent8(s3.at[:, pl.ds(32 * half, 32)])
            e4[half].sent(s4.at[pl.ds(0, 15), pl.ds(0, 16)])

    return tri_sent


SHAPES = dict(
    z1=((4, 128, 128), F32),
    z2=((4, 128, 128), F32),
    z3=((4, 128, 128), F32),
    msa_out=((2, 128, 256), BF),
)


PARTS = dict(
    row=dict(ins=["msa", "pairs", "row_w", "row_out", "pair_bias"], outs=[], scratch=ROW_SCRATCH, sems=ROW_SEMS),
    col=dict(
        ins=["pairs", "col_w", "col_out", "maps", "outer_out"],
        outs=["msa_out", "z1"],
        scratch=COL_SCRATCH,
        sems=COL_SEMS,
    ),
    out=dict(ins=["z1", "o_proj", "o_out"], outs=["z2"], scratch=tri_scratch("o", True), sems=tri_sems("o")),
    inc=dict(ins=["z2", "i_proj", "i_out"], outs=["z3"], scratch=tri_scratch("i", False), sems=tri_sems("i")),
)


def run_parts(parts, arrays, results, number):
    ins, made, scratch, sems = [], [], {}, []
    for p in parts:
        spec = PARTS[p]
        ins += [n for n in spec["ins"] if n not in ins and n not in made]
        made += spec["outs"]
        scratch.update(spec["scratch"])
        sems += spec["sems"]
    outs = [n for n in made if n in results]
    inner = {n: SHAPES[n] for n in made if n not in results}
    scratch = {**scratch, **inner}
    sem_names = [s + e for s in sems for e in ("_s", "_r")]

    def body(*refs):
        r = dict(zip(ins + outs + list(scratch) + sem_names, refs))
        barrier_signal()

        def prep():
            if "col" in parts:
                col_prep(r)
            if "out" in parts:
                tri_prep(r, "o")
            if "inc" in parts:
                tri_prep(r, "i")

        if parts[0] == "row":
            r["prep"] = prep
        else:
            prep()
            barrier_wait()
        waits = []
        for p in parts:
            if p == "row":
                waits.append(row_part(r))
            elif p == "col":
                waits.append(col_part(r))
            elif p == "out":
                waits.append(tri_part(r, "o", "z1", "z2", True))
            else:
                waits.append(tri_part(r, "i", "z2", "z3", False))
        for wait in waits:
            wait()

    vm = pl.BlockSpec(memory_space=pltpu.VMEM)
    got = pl.pallas_call(
        body,
        out_shape=[jax.ShapeDtypeStruct(*SHAPES[n]) for n in outs],
        in_specs=[vm] * len(ins),
        out_specs=[vm] * len(outs),
        scratch_shapes=[pltpu.VMEM(*scratch[n]) for n in scratch] + [pltpu.SemaphoreType.DMA] * len(sem_names),
        compiler_params=pltpu.CompilerParams(
            collective_id=number, has_side_effects=True, vmem_limit_bytes=56 * 1024 * 1024
        ),
        name="_".join(parts),
    )(*[arrays[n] for n in ins])
    arrays.update(zip(outs, got))


GROUPS = [["row", "col", "out", "inc"]]


def shards(*args, groups=None, results=("msa_out", "z3")):
    groups = groups or GROUPS
    names = ["msa", "pairs", "row_w", "row_out", "pair_bias", "col_w", "col_out", "maps", "outer_out"]
    names += ["o_proj", "o_out", "i_proj", "i_out"]
    arrays = dict(zip(names, args))
    msa_shape, pair_shape = arrays["msa"].shape, arrays["pairs"].shape
    arrays["pair_bias"], arrays["maps"] = arrays["pair_bias"].T, arrays["maps"].T
    arrays["msa"] = arrays["msa"].reshape(2, 128, 256)
    arrays["pairs"] = arrays["pairs"].reshape(4, 128, 128)
    for number, group in enumerate(groups):
        later = [n for g in groups[number + 1 :] for p in g for n in PARTS[p]["ins"]]
        run_parts(group, arrays, set(results) | set(later), number)
    outs = dict(
        msa_out=lambda a: a.reshape(msa_shape),
        z3=lambda a: a.reshape(pair_shape),
    )
    return tuple(outs.get(n, lambda a: a)(arrays[n]) for n in results)


def solution(mesh):
    return jax.shard_map(
        shards,
        mesh=mesh,
        in_specs=(P("row", None, "col", None, None),) * 2 + (P(),) * 11,
        out_specs=(P("row", None, "col", None, None),) * 2,
        check_vma=False,
    )
```
